32 devices in a mesh: dp: 8 (over y, x, core), tensor: 4 (over z).
Axes of the slice: x: 2, y: 2, z: 4, core: 2. Of those that a mesh axis runs over, the one named last changes fastest.
Arguments:
- hidden_in: bfloat16 [8192, 2048], P(('dp', 'tensor')), may hold values from -6 to 6
- segments: int32 [8192], P('dp'), may hold values from 0 to 3, as said below
- norm_gain: bfloat16 [2048], P('dp'), may hold values from 0.25 to 1.75
- mamba_in: bfloat16 [2048, 2, 3072], P('dp', None, 'tensor'), may hold values from -0.125 to 0.125
- step_weight: bfloat16 [2048, 48], P('dp', 'tensor'), may hold values from -0.125 to 0.125
- state_weight: bfloat16 [2048, 2, 256], P('dp'), may hold values from -0.03125 to 0.03125
- decay_log: float32 [48], P('tensor'), may hold values from -5.8 to -1.2
- step_bias: float32 [48], P('tensor'), may hold values from -4 to -2
- skip_gain: float32 [48], P('tensor'), may hold values from 0.5 to 2
- gated_gain: bfloat16 [3072], P('tensor'), may hold values from 0.25 to 1.75
- query_weight: bfloat16 [2048, 1024], P('dp', 'tensor'), may hold values from -0.125 to 0.125
- keyval_weight: bfloat16 [2048, 2, 256], P('dp'), may hold values from -0.125 to 0.125
- mamba_out: bfloat16 [3072, 2048], P('tensor', 'dp'), may hold values from -0.109375 to 0.109375
- attn_out: bfloat16 [1024, 2048], P('tensor', 'dp'), may hold values from -0.75 to 0.75
- ffn_gain: bfloat16 [2048], P('dp'), may hold values from 0.25 to 1.75
- gate_up: bfloat16 [2048, 2, 4096], P('dp', None, 'tensor'), may hold values from -0.125 to 0.125
- down_weight: bfloat16 [4096, 2048], P('tensor', 'dp'), may hold values from -0.09375 to 0.09375
- cotangent: bfloat16 [8192, 2048], P(('dp', 'tensor')), may hold values from -6 to 6
Outputs:
- hidden_out: bfloat16 [8192, 2048], P(('dp', 'tensor'))
- hidden_grad: float32 [8192, 2048], P(('dp', 'tensor'))
- norm_gain_grad: float32 [2048], P('dp')
- mamba_in_grad: float32 [2048, 2, 3072], P('dp', None, 'tensor')
- step_weight_grad: float32 [2048, 48], P('dp', 'tensor')
- state_weight_grad: float32 [2048, 2, 256], P('dp')
- decay_log_grad: float32 [48], P('tensor')
- step_bias_grad: float32 [48], P('tensor')
- skip_gain_grad: float32 [48], P('tensor')
- gated_gain_grad: float32 [3072], P('tensor')
- query_weight_grad: float32 [2048, 1024], P('dp', 'tensor')
- keyval_weight_grad: float32 [2048, 2, 256], P('dp')
- mamba_out_grad: float32 [3072, 2048], P('tensor', 'dp')
- attn_out_grad: float32 [1024, 2048], P('tensor', 'dp')
- ffn_gain_grad: float32 [2048], P('dp')
- gate_up_grad: float32 [2048, 2, 4096], P('dp', None, 'tensor')
- down_weight_grad: float32 [4096, 2048], P('tensor', 'dp')
The draws below stay inside these ranges and needn't reach their ends.
Inputs may be any that keep to these rules, and one draw needn't show every extreme that they name: `segments`: within each sequence of 1024 tokens the numbers start at 0 and rise by one at each document start; every document holds one eighth of 1024 tokens or more; some sequence is a single document and some holds four.
All inputs are finite; a program needn't handle non-finite values.
Results may differ from the reference program's by a relative error of at most 0.018.
Values may be sent and summed in bfloat16 or wider, within the bound.
A program may use at most 256 MiB of HBM per device.

```python
import math
import jax
import jax.numpy as jnp
from jax import lax

D = 2048
MAMBA_HEADS = 48
HEAD_DIM = 64
STATE = 256
ATT_HEADS = 8
KV_HEADS = 2
ATT_DIM = 128
FF = 4096
SEQ_LEN = 1024
STRETCH = 128
ATT_BLOCK = 512
SEQS = 8
TOKENS = 8192


def draw_segments(key, part):
    key = jax.random.fold_in(key, 11)
    key_one, key_two, key_three = jax.random.split(key, 3)
    quarter = SEQ_LEN // 4
    jitter = jax.random.randint(key_one, (SEQS, 3), -(quarter // 4), quarter // 4 + 1)
    cuts = quarter * jnp.arange(1, 4, dtype=jnp.int32)[None, :] + jitter
    live = jax.random.randint(key_two, (SEQS, 3), 0, 2)
    picked = jax.random.permutation(key_three, SEQS)[:2]
    row_ids = jnp.arange(SEQS, dtype=jnp.int32)[:, None]
    live = jnp.where(row_ids == picked[0], 0, live)
    live = jnp.where(row_ids == picked[1], 1, live)
    positions = jnp.arange(SEQ_LEN, dtype=jnp.int32)
    passed = (positions[None, :, None] >= cuts[:, None, :]) & (live[:, None, :] == 1)
    numbers = jnp.sum(passed.astype(jnp.int32), -1)
    return numbers.reshape(TOKENS).astype(jnp.int32)


def block_levels(rng, dims, shards, smallest, high):
    level, own = 1.0, jax.random.fold_in(rng, 6)
    for dim, blocks in shards:
        draws = jnp.exp(jax.random.uniform(jax.random.fold_in(own, dim), (blocks,), jnp.float32, smallest / len(shards), high / len(shards)))
        level = level * jnp.repeat(draws, dims[dim] // blocks).reshape([-1 if axis == dim else 1 for axis in range(len(dims))])
    return level


def scatter_about(key, dims, deviation, most, cuts=(), held_as=jnp.bfloat16):
    entries = jax.random.normal(key, dims, jnp.float32) * deviation
    if len(cuts) > 0:
        entries = block_levels(key, dims, cuts, -0.22, 0.18) * entries
    return jnp.clip(entries, min=-most, max=most).astype(held_as)


def setup_inputs(seed: int = 0) -> dict:
    seeds = jax.random.split(jax.random.key(seed), 19)
    hidden_in = scatter_about(seeds[0], (TOKENS, D), 1.0, 6.0, ((0, 32),))
    segments = draw_segments(jax.random.fold_in(seeds[18], 71), 0)
    norm_gain = jnp.clip(1.0 + 0.15 * jax.random.normal(seeds[2], (D,), jnp.float32), 0.25, 1.75).astype(jnp.bfloat16)
    mamba_in = scatter_about(seeds[3], (D, 2, MAMBA_HEADS * HEAD_DIM), D ** -0.5, 0.125, ((0, 8), (2, 4)))
    step_weight = scatter_about(seeds[4], (D, MAMBA_HEADS), D ** -0.5, 0.125, ((0, 8), (1, 4)))
    state_weight = scatter_about(seeds[5], (D, 2, STATE), (16 * D) ** -0.5, 0.03125, ((0, 8),))
    decay_log = jnp.clip(-5.8 + 4.6000001430511475 * jax.random.uniform(seeds[6], (MAMBA_HEADS,), jnp.float32) ** block_levels(seeds[6], (MAMBA_HEADS,), ((0, 4),), -0.2, 0.2), -5.8, -1.2)
    step_bias = jnp.clip(-4.0 + 2.0 * jax.random.uniform(seeds[7], (MAMBA_HEADS,), jnp.float32) ** block_levels(seeds[7], (MAMBA_HEADS,), ((0, 4),), -0.2, 0.2), -4.0, -2.0)
    skip_gain = jnp.clip(0.5 + 1.5 * jax.random.uniform(seeds[8], (MAMBA_HEADS,), jnp.float32) ** block_levels(seeds[8], (MAMBA_HEADS,), ((0, 4),), -0.2, 0.2), 0.5, 2.0)
    gated_gain = jnp.clip(1.0 + 0.15 * jax.random.normal(seeds[9], (MAMBA_HEADS * HEAD_DIM,), jnp.float32), 0.25, 1.75).astype(jnp.bfloat16)
    query_weight = scatter_about(seeds[10], (D, ATT_HEADS * ATT_DIM), D ** -0.5, 0.125, ((0, 8), (1, 4)))
    keyval_weight = scatter_about(seeds[11], (D, 2, KV_HEADS * ATT_DIM), D ** -0.5, 0.125, ((0, 8),))
    mamba_out = scatter_about(seeds[12], (MAMBA_HEADS * HEAD_DIM, D), (MAMBA_HEADS * HEAD_DIM) ** -0.5, 0.109375, ((0, 4), (1, 8)))
    attn_out = scatter_about(seeds[13], (ATT_HEADS * ATT_DIM, D), (ATT_HEADS * ATT_DIM // 16) ** -0.5, 0.75, ((0, 4), (1, 8)))
    ffn_gain = jnp.clip(1.0 + 0.15 * jax.random.normal(seeds[14], (D,), jnp.float32), 0.25, 1.75).astype(jnp.bfloat16)
    gate_up = scatter_about(seeds[15], (D, 2, FF), D ** -0.5, 0.125, ((0, 8), (2, 4)))
    down_weight = scatter_about(seeds[16], (FF, D), FF ** -0.5, 0.09375, ((0, 4), (1, 8)))
    cotangent = scatter_about(seeds[17], (TOKENS, D), 1.0, 6.0, ((0, 32),))
    return {"hidden_in": hidden_in, "segments": segments, "norm_gain": norm_gain, "mamba_in": mamba_in, "step_weight": step_weight, "state_weight": state_weight, "decay_log": decay_log, "step_bias": step_bias, "skip_gain": skip_gain, "gated_gain": gated_gain, "query_weight": query_weight, "keyval_weight": keyval_weight, "mamba_out": mamba_out, "attn_out": attn_out, "ffn_gain": ffn_gain, "gate_up": gate_up, "down_weight": down_weight, "cotangent": cotangent}


@jax.custom_vjp
def low(v):
    return lax.optimization_barrier(v.astype(jnp.bfloat16)).astype(jnp.float32)

@jax.custom_vjp
def low_back(v):
    return v

def low_keep(v):
    return (low(v), None)

def low_pass(kept, grad):
    return (grad,)

def back_keep(v):
    return (v, None)

def back_low(kept, grad):
    return (low(grad),)
low.defvjp(low_keep, low_pass)
low_back.defvjp(back_keep, back_low)
EPSILON = 1e-05
PRECISE = lax.Precision.HIGHEST
ROPE_BASE = 10000.0

def rms_norm(values, gain_vals):
    return values * lax.rsqrt(lax.optimization_barrier(jnp.mean(values * values, -1, keepdims=True)) + EPSILON) * gain_vals

def rotate(values):
    half_width = values.shape[-1] // 2
    positions = jnp.arange(values.shape[0], dtype=jnp.float32)
    frequency = ROPE_BASE ** (-jnp.arange(half_width, dtype=jnp.float32) / half_width)
    angles = positions[:, None] * frequency[None, :]
    cosine = jnp.cos(angles)[:, None, :]
    sine_vals = jnp.sin(angles)[:, None, :]
    front_half = values[..., :half_width]
    back_half = values[..., half_width:]
    return jnp.concatenate([front_half * cosine - back_half * sine_vals, back_half * cosine + front_half * sine_vals], -1)

def attend(queries, keys_full, values_full, segment_ids):
    length = queries.shape[0]
    query_heads = queries.shape[1]
    head_size = queries.shape[2]
    repeat_count = query_heads // keys_full.shape[1]
    keys_full = rotate(jnp.repeat(keys_full, repeat_count, axis=1))
    values_full = jnp.repeat(values_full, repeat_count, axis=1)
    queries = rotate(queries)
    positions = jnp.arange(length, dtype=jnp.int32)

    def score_block(block_index):
        first_row = block_index * ATT_BLOCK
        query_block = lax.dynamic_slice_in_dim(queries, first_row, ATT_BLOCK, 0)
        segment_block = lax.dynamic_slice_in_dim(segment_ids, first_row, ATT_BLOCK, 0)
        place_block = first_row + jnp.arange(ATT_BLOCK, dtype=jnp.int32)
        scores = jnp.einsum('qhe,khe->hqk', query_block, keys_full, precision=PRECISE) / math.sqrt(head_size)
        allowed = (place_block[:, None] >= positions[None, :]) & (segment_block[:, None] == segment_ids[None, :])
        scores = jnp.where(allowed[None], scores, -1e+30)
        highest = lax.optimization_barrier(jnp.max(scores, -1, keepdims=True))
        weights = jnp.exp(scores - highest)
        weights = weights / lax.optimization_barrier(jnp.sum(weights, -1, keepdims=True))
        return jnp.einsum('hqk,khe->qhe', weights, values_full, precision=PRECISE)
    blocks = length // ATT_BLOCK
    attended = lax.map(jax.checkpoint(score_block), jnp.arange(blocks, dtype=jnp.int32))
    return attended.reshape(length, query_heads * head_size)

def stretch_step(carried, pieces):
    drive_part, keep_part, input_part, output_part, segment_part, before_id = pieces
    span = segment_part.shape[0]
    running = jnp.cumsum(keep_part, 0)
    places = jnp.arange(span, dtype=jnp.int32)
    causal = (places[:, None] >= places[None, :]) & (segment_part[:, None] == segment_part[None, :])
    spread_log = running[:, None, :] - running[None, :, :]
    decays = jnp.exp(jnp.where(causal[:, :, None], spread_log, -jnp.inf))
    scores = jnp.dot(output_part, input_part.T, precision=PRECISE)
    within = jnp.einsum('tsh,shp->thp', decays * scores[:, :, None], drive_part, precision=PRECISE)
    carry_live = (segment_part == before_id).astype(running.dtype)
    across = jnp.einsum('tn,hpn->thp', output_part, carried, precision=PRECISE)
    across = across * (jnp.exp(running) * carry_live[:, None])[:, :, None]
    final_log = running[-1]
    tail_live = (segment_part == segment_part[-1]).astype(running.dtype)
    weights = jnp.exp(final_log[None, :] - running) * tail_live[:, None]
    keep_old = jnp.exp(final_log) * (segment_part[-1] == before_id).astype(running.dtype)
    updated = carried * keep_old[:, None, None] + jnp.einsum('sh,shp,sn->hpn', weights, drive_part, input_part, precision=PRECISE)
    return (updated, within + across)

def mixer_scan(drive_vals, raw_vals, input_map, output_map, decay_rates, biases, skip_vals, segment_ids):
    length, head_count, head_width = drive_vals.shape
    stretch_count = length // STRETCH
    step_size = jax.nn.softplus(raw_vals + biases[None, :])
    log_keep = -jnp.exp(decay_rates)[None, :] * step_size
    driven = drive_vals * step_size[:, :, None]
    before = jnp.concatenate([jnp.full((1,), -1, jnp.int32), segment_ids[STRETCH - 1:length - 1:STRETCH].astype(jnp.int32)])
    pieces = (driven.reshape(stretch_count, STRETCH, head_count, head_width), log_keep.reshape(stretch_count, STRETCH, head_count), input_map.reshape(stretch_count, STRETCH, -1), output_map.reshape(stretch_count, STRETCH, -1), segment_ids.reshape(stretch_count, STRETCH).astype(jnp.int32), before)
    initial = jnp.zeros((head_count, head_width, input_map.shape[1]), jnp.float32)
    last_state, stretch_outs = lax.scan(jax.checkpoint(stretch_step), initial, pieces)
    return stretch_outs.reshape(length, head_count, head_width) + skip_vals[None, :, None] * drive_vals

def layer(params, hidden, segment_ids):
    norm_gain, mamba_in, step_weight, state_weight, decay_log, step_bias, skip_gain, gated_gain, query_weight, keyval_weight, mamba_out, attn_out, ffn_gain, gate_up, down_weight = params
    groups, length, features = hidden.shape
    normed = low(rms_norm(hidden, norm_gain))
    inner_vals = low_back(jnp.einsum('gsd,dkc->gskc', normed, mamba_in, precision=PRECISE))
    raw_step = low_back(jnp.einsum('gsd,dh->gsh', normed, step_weight, precision=PRECISE))
    states = jnp.einsum('gsd,dkn->gskn', normed, state_weight, precision=PRECISE)
    queries = low_back(jnp.einsum('gsd,de->gse', normed, query_weight, precision=PRECISE))
    keyvals = jnp.einsum('gsd,dke->gske', normed, keyval_weight, precision=PRECISE)
    drive_vals = inner_vals[:, :, 1].reshape(groups, length, MAMBA_HEADS, HEAD_DIM)
    result = jax.vmap(mixer_scan, in_axes=(0, 0, 0, 0, None, None, None, 0))(drive_vals, raw_step, states[:, :, 0], states[:, :, 1], decay_log, step_bias, skip_gain, segment_ids)
    gated_vals = result.reshape(groups, length, MAMBA_HEADS * HEAD_DIM) * jax.nn.silu(inner_vals[:, :, 0])
    mamba_normed = low(rms_norm(gated_vals, gated_gain))
    attended = low(jax.vmap(attend)(queries.reshape(groups, length, ATT_HEADS, ATT_DIM), keyvals[:, :, 0].reshape(groups, length, KV_HEADS, ATT_DIM), keyvals[:, :, 1].reshape(groups, length, KV_HEADS, ATT_DIM), segment_ids))
    mixed_vals = low_back(jnp.einsum('gsc,cd->gsd', mamba_normed, mamba_out, precision=PRECISE) + jnp.einsum('gsc,cd->gsd', attended, attn_out, precision=PRECISE))
    middle = hidden + mixed_vals
    ffn_in = low(rms_norm(middle, ffn_gain))
    gate_vals = low_back(jnp.einsum('gsd,dkf->gskf', ffn_in, gate_up, precision=PRECISE))
    activated = low(jax.nn.silu(gate_vals[:, :, 0]) * gate_vals[:, :, 1])
    ffn_out = low_back(jnp.einsum('gsf,fd->gsd', activated, down_weight, precision=PRECISE))
    return middle + ffn_out

def reference(hidden_in, segments, norm_gain, mamba_in, step_weight, state_weight, decay_log, step_bias, skip_gain, gated_gain, query_weight, keyval_weight, mamba_out, attn_out, ffn_gain, gate_up, down_weight, cotangent):
    params = tuple((weight_arg.astype(jnp.float32) for weight_arg in (norm_gain, mamba_in, step_weight, state_weight, decay_log, step_bias, skip_gain, gated_gain, query_weight, keyval_weight, mamba_out, attn_out, ffn_gain, gate_up, down_weight)))
    group_size = math.gcd(SEQS, 4)
    blocks = SEQS // group_size
    hidden = hidden_in.astype(jnp.float32).reshape(blocks, group_size, SEQ_LEN, D)
    grads_in = cotangent.astype(jnp.float32).reshape(blocks, group_size, SEQ_LEN, D)
    segment_blocks = segments.astype(jnp.int32).reshape(blocks, group_size, SEQ_LEN)

    def one_block(totals, pieces):
        hidden_block, segment_block, grad_block = pieces
        result, pullback = jax.vjp(lambda weights, values: layer(weights, values, segment_block), params, hidden_block)
        weight_grads, input_grad = pullback(grad_block)
        return (jax.tree.map(jnp.add, totals, weight_grads), (result, input_grad))
    totals, (outputs, input_grads) = lax.scan(one_block, jax.tree.map(jnp.zeros_like, params), (hidden, segment_blocks, grads_in))
    return (outputs.reshape(TOKENS, D).astype(jnp.bfloat16), input_grads.reshape(TOKENS, D), totals[0], totals[1], totals[2], totals[3], totals[4], totals[5], totals[6], totals[7], totals[8], totals[9], totals[10], totals[11], totals[12], totals[13], totals[14])
```

```python
import functools
import math
import jax
import jax.numpy as jnp
from jax import lax
from jax.experimental import pallas as pl
from jax.experimental.pallas import tpu as pltpu
from jax.sharding import PartitionSpec as P

MAMBA_HEADS = 48
HEAD_DIM = 64
ATT_HEADS = 8
KV_HEADS = 2
ATT_DIM = 128
STRETCH = 128
ATT_BLOCK = 256
EPSILON = 1e-05
PRECISE = lax.Precision.HIGHEST
ROPE_BASE = 10000.0
LANES = 128
MASKED = -1e30
HALF = jnp.bfloat16
FULL = jnp.float32


def mm(a, b):
    return jnp.dot(a, b, preferred_element_type=FULL)


def mm_nt(a, b):
    return lax.dot_general(a, b, (((1,), (1,)), ((), ())), preferred_element_type=FULL)


def mm_tn(a, b):
    return lax.dot_general(a, b, (((0,), (0,)), ((), ())), preferred_element_type=FULL)


def softplus(v):
    return jnp.maximum(v, 0.0) + jnp.log1p(jnp.exp(-jnp.abs(v)))


def sigmoid(v):
    return 1.0 / (1.0 + jnp.exp(-v))


def iota(shape, dim):
    return lax.broadcasted_iota(jnp.int32, shape, dim)


def halves(left, right, size):
    return jnp.where(iota((size, LANES), 1) < HEAD_DIM, left, right)


def stacked_pair(pair):
    low = iota(pair.shape, 1) < HEAD_DIM
    zero = jnp.zeros_like(pair)
    return jnp.concatenate([jnp.where(low, pair, zero), jnp.where(low, zero, pair)], 0)


class Columns:
    def __init__(self, query, width, state):
        self.query = (0, query)
        self.key = (query, query + ATT_DIM)
        self.value = (query + ATT_DIM, query + 2 * ATT_DIM)
        start = query + 2 * ATT_DIM
        self.attention = start
        self.gate = (start, start + width)
        self.drive = (start + width, start + 2 * width)
        start += 2 * width
        self.inmap = (start, start + state)
        self.outmap = (start + state, start + 2 * state)
        start += 2 * state
        self.step = (start, start + LANES)
        self.total = start + LANES


def stretch_common(col, packed, segc_ref, segr_ref, head_ref, before):
    span = STRETCH
    raw = packed[:, col.step[0] : col.step[1]] + head_ref[1:2, :]
    step = softplus(raw)
    keep = -jnp.exp(head_ref[0:1, :]) * step
    row, column = iota((span, span), 0), iota((span, span), 1)
    running = jnp.dot(
        (row >= column).astype(FULL), keep, precision=PRECISE, preferred_element_type=FULL
    )
    segc, segr = segc_ref[...], segr_ref[0]
    causal = (row >= column) & (segc == segr)
    blocked = jnp.where(causal, 0.0, MASKED)
    live = (segc == before).astype(FULL)
    last = segc[span - 1 : span, :]
    tail = (segc == last).astype(FULL)
    old = (last == before).astype(FULL)
    return raw, step, keep, running, running.T, blocked, live, tail, old


def pair_decay(pair, running, running_t, blocked, live, tail, old):
    span = STRETCH
    a, b = 2 * pair, 2 * pair + 1
    col_a = jnp.broadcast_to(running[:, a : a + 1], (span, LANES))
    col_b = jnp.broadcast_to(running[:, b : b + 1], (span, LANES))
    decay_a = jnp.exp(col_a - running_t[a : a + 1, :] + blocked)
    decay_b = jnp.exp(col_b - running_t[b : b + 1, :] + blocked)
    both = halves(col_a, col_b, span)
    last = both[span - 1 : span, :]
    into = jnp.exp(both) * live
    weight = jnp.exp(last - both) * tail
    keep_old = jnp.exp(last) * old
    return decay_a, decay_b, into, weight, keep_old


def scan_forward_kernel(col, heads, p_ref, segc_ref, segr_ref, head_ref, y_ref, states_ref, gated_ref, square_ref, state, before):
    index = pl.program_id(0)
    span = STRETCH

    @pl.when(index == 0)
    def _():
        state[...] = jnp.zeros_like(state)
        before[...] = jnp.full_like(before, -1)

    raw, step, keep, running, running_t, blocked, live, tail, old = stretch_common(
        col, p_ref, segc_ref, segr_ref, head_ref, before[...]
    )
    inmap = p_ref[:, col.inmap[0] : col.inmap[1]].astype(HALF)
    outmap = p_ref[:, col.outmap[0] : col.outmap[1]].astype(HALF)
    inmap_t = inmap.T
    scores = mm_nt(outmap, inmap)
    square = jnp.zeros((span, 1), FULL)
    for pair in range(heads // 2):
        at = pair * LANES
        lanes = slice(at, at + LANES)
        decay_a, decay_b, into, weight, keep_old = pair_decay(
            pair, running, running_t, blocked, live, tail, old
        )
        drive = p_ref[:, col.drive[0] + at : col.drive[0] + at + LANES]
        gate = p_ref[:, col.gate[0] + at : col.gate[0] + at + LANES]
        driven = drive * halves(step[:, 2 * pair : 2 * pair + 1], step[:, 2 * pair + 1 : 2 * pair + 2], span)
        driven_low = driven.astype(HALF)
        mix = jnp.concatenate([(decay_a * scores).astype(HALF), (decay_b * scores).astype(HALF)], 1)
        held = state[:, lanes]
        held_low = held.astype(HALF)
        states_ref[0, :, lanes] = held_low
        result = mm(mix, stacked_pair(driven_low)) + mm(outmap, held_low) * into
        state[:, lanes] = held * keep_old + mm(inmap_t, (driven_low.astype(FULL) * weight).astype(HALF))
        y_ref[:, lanes] = result
        skip = halves(head_ref[2:3, 2 * pair : 2 * pair + 1], head_ref[2:3, 2 * pair + 1 : 2 * pair + 2], 1)
        gated = (result + skip * drive) * (gate * sigmoid(gate))
        gated_ref[:, lanes] = gated
        square = square + jnp.sum(gated * gated, 1, keepdims=True)
    square_ref[...] = jnp.broadcast_to(square, square_ref.shape)
    before[...] = segc_ref[span - 1 : span, :]


def scan_forward(col, heads, state_size, packed, segments, head_params):
    length = packed.shape[0]
    width = heads * HEAD_DIM
    count = length // STRETCH
    return pl.pallas_call(
        functools.partial(scan_forward_kernel, col, heads),
        grid=(count,),
        in_specs=[
            pl.BlockSpec((STRETCH, col.total), lambda i: (i, 0)),
            pl.BlockSpec((STRETCH, 1), lambda i: (i, 0)),
            pl.BlockSpec((1, 1, STRETCH), lambda i: (i, 0, 0)),
            pl.BlockSpec((8, LANES), lambda i: (0, 0)),
        ],
        out_specs=[
            pl.BlockSpec((STRETCH, width), lambda i: (i, 0)),
            pl.BlockSpec((1, state_size, width), lambda i: (i, 0, 0)),
            pl.BlockSpec((STRETCH, width), lambda i: (i, 0)),
            pl.BlockSpec((STRETCH, LANES), lambda i: (i, 0)),
        ],
        out_shape=[
            jax.ShapeDtypeStruct((length, width), FULL),
            jax.ShapeDtypeStruct((count, state_size, width), HALF),
            jax.ShapeDtypeStruct((length, width), FULL),
            jax.ShapeDtypeStruct((length, LANES), FULL),
        ],
        scratch_shapes=[pltpu.VMEM((state_size, width), FULL), pltpu.VMEM((1, 1), jnp.int32)],
        cost_estimate=pl.CostEstimate(flops=6_000_000_000, bytes_accessed=30_000_000, transcendentals=0),
        compiler_params=pltpu.CompilerParams(vmem_limit_bytes=48 * 2**20),
    )(packed, segments[:, None], segments.reshape(count, 1, STRETCH), head_params)


def scan_backward_kernel(
    col, heads, total_width, p_ref, y_ref, states_ref, gm_ref, inv_ref, prod_ref, gain_ref,
    segc_ref, segr_ref, segb_ref, head_ref, g_ref, gain_grad_ref, skip_grad_ref, head_grad_ref, future,
):
    step_index = pl.program_id(0)
    count = pl.num_programs(0)
    span = STRETCH

    @pl.when(step_index == 0)
    def _():
        future[...] = jnp.zeros_like(future)
        gain_grad_ref[...] = jnp.zeros_like(gain_grad_ref)
        skip_grad_ref[...] = jnp.zeros_like(skip_grad_ref)
        head_grad_ref[...] = jnp.zeros_like(head_grad_ref)

    before = jnp.where(step_index == count - 1, -1, segb_ref[span - 1 : span, :])
    raw, step, keep, running, running_t, blocked, live, tail, old = stretch_common(
        col, p_ref, segc_ref, segr_ref, head_ref, before
    )
    inmap = p_ref[:, col.inmap[0] : col.inmap[1]].astype(HALF)
    outmap = p_ref[:, col.outmap[0] : col.outmap[1]].astype(HALF)
    outmap_t = outmap.T
    scores = mm_nt(outmap, inmap)
    lane = iota((span, LANES), 1)
    head_lane = iota((1, LANES), 1)
    paired = jnp.zeros((span, span), FULL)
    grad_in = jnp.zeros(inmap.shape, FULL)
    grad_out = jnp.zeros(outmap.shape, FULL)
    grad_running = jnp.zeros((span, LANES), FULL)
    grad_step = jnp.zeros((span, LANES), FULL)
    grad_last = jnp.zeros((1, LANES), FULL)
    inverse, product = inv_ref[:, 0:1], prod_ref[:, 0:1] * (1.0 / total_width)
    for pair in range(heads // 2):
        at = pair * LANES
        lanes = slice(at, at + LANES)
        a, b = 2 * pair, 2 * pair + 1
        decay_a, decay_b, into, weight, keep_old = pair_decay(
            pair, running, running_t, blocked, live, tail, old
        )
        drive = p_ref[:, col.drive[0] + at : col.drive[0] + at + LANES]
        gate = p_ref[:, col.gate[0] + at : col.gate[0] + at + LANES]
        result = y_ref[:, lanes]
        skip = halves(head_ref[2:3, a : a + 1], head_ref[2:3, b : b + 1], 1)
        sig = sigmoid(gate)
        silu = gate * sig
        ssm = result + skip * drive
        plain = ssm * silu * inverse
        grad_above = gm_ref[:, lanes].astype(FULL)
        gain_grad_ref[:, lanes] += jnp.sum(grad_above * plain, 0, keepdims=True)
        grad_gated = inverse * (grad_above * gain_ref[:, lanes] - plain * product)
        g_ref[:, col.gate[0] + at : col.gate[0] + at + LANES] = (
            grad_gated * ssm * (sig * (1.0 + gate * (1.0 - sig)))
        ).astype(HALF)
        grad_y = grad_gated * silu
        grad_y_low = grad_y.astype(HALF)
        grad_y = grad_y_low.astype(FULL)
        step_pair = halves(step[:, a : a + 1], step[:, b : b + 1], span)
        driven_low = (drive * step_pair).astype(HALF)
        driven = driven_low.astype(FULL)
        grad_rows = stacked_pair(grad_y_low)
        inner = mm_nt(grad_rows, driven_low)
        paired = paired + decay_a * inner[:span] + decay_b * inner[span:]
        mix = jnp.concatenate([(decay_a * scores).astype(HALF), (decay_b * scores).astype(HALF)], 0)
        later = future[:, lanes]
        later_low = later.astype(HALF)
        held_low = states_ref[0, :, lanes]
        reach = mm(inmap, later_low) * weight
        grad_driven = mm_tn(mix, grad_rows) + reach
        weighted = (driven * weight).astype(HALF)
        spread = (grad_y * into).astype(HALF)
        grad_in = grad_in + mm_nt(weighted, later_low)
        grad_out = grad_out + mm_nt(spread, held_low)
        future[:, lanes] = later * keep_old + mm(outmap_t, spread)
        g_ref[:, col.drive[0] + at : col.drive[0] + at + LANES] = (
            step_pair * grad_driven + skip * grad_y
        ).astype(HALF)
        skip_grad_ref[:, lanes] += jnp.sum(grad_y * drive, 0, keepdims=True)
        turn = grad_y * result - driven * grad_driven
        left = lane < HEAD_DIM
        from_drive = drive * grad_driven
        ends = jnp.sum(driven * reach, 0, keepdims=True) + keep_old * jnp.sum(
            later * held_low.astype(FULL), 0, keepdims=True
        )
        for head, mask in ((a, left), (b, ~left)):
            grad_running = grad_running + jnp.where(
                lane == head, jnp.sum(jnp.where(mask, turn, 0.0), 1, keepdims=True), 0.0
            )
            grad_step = grad_step + jnp.where(
                lane == head, jnp.sum(jnp.where(mask, from_drive, 0.0), 1, keepdims=True), 0.0
            )
            grad_last = grad_last + jnp.where(
                head_lane == head, jnp.sum(jnp.where(mask[0:1], ends, 0.0), 1, keepdims=True), 0.0
            )
    paired = paired.astype(HALF)
    grad_out = grad_out + mm(paired, inmap)
    grad_in = grad_in + mm_tn(paired, outmap)
    g_ref[:, col.inmap[0] : col.inmap[1]] = grad_in.astype(HALF)
    g_ref[:, col.outmap[0] : col.outmap[1]] = grad_out.astype(HALF)
    row, column = iota((span, span), 0), iota((span, span), 1)
    grad_keep = (
        jnp.dot((row <= column).astype(FULL), grad_running, precision=PRECISE, preferred_element_type=FULL)
        + grad_last
    )
    grad_raw = (grad_step - grad_keep * jnp.exp(head_ref[0:1, :])) * sigmoid(raw)
    grad_raw = jnp.where(lane < heads, grad_raw, 0.0)
    g_ref[:, col.step[0] : col.step[1]] = grad_raw.astype(HALF)
    g_ref[:, 0 : col.attention] = jnp.zeros((span, col.attention), HALF)
    head_grad_ref[0:1, :] += jnp.sum(keep * grad_keep, 0, keepdims=True)
    head_grad_ref[1:2, :] += jnp.sum(grad_raw, 0, keepdims=True)


def scan_backward(col, heads, state_size, packed, y, states, grad_mamba, inverse, product, gain, segments, head_params):
    length = packed.shape[0]
    width = heads * HEAD_DIM
    count = length // STRETCH
    back = lambda i: (count - 1 - i, 0)
    return pl.pallas_call(
        functools.partial(scan_backward_kernel, col, heads, MAMBA_HEADS * HEAD_DIM),
        grid=(count,),
        in_specs=[
            pl.BlockSpec((STRETCH, col.total), back),
            pl.BlockSpec((STRETCH, width), back),
            pl.BlockSpec((1, state_size, width), lambda i: (count - 1 - i, 0, 0)),
            pl.BlockSpec((STRETCH, width), back),
            pl.BlockSpec((STRETCH, 1), back),
            pl.BlockSpec((STRETCH, 1), back),
            pl.BlockSpec((1, width), lambda i: (0, 0)),
            pl.BlockSpec((STRETCH, 1), back),
            pl.BlockSpec((1, 1, STRETCH), lambda i: (count - 1 - i, 0, 0)),
            pl.BlockSpec((STRETCH, 1), lambda i: (jnp.maximum(count - 2 - i, 0), 0)),
            pl.BlockSpec((8, LANES), lambda i: (0, 0)),
        ],
        out_specs=[
            pl.BlockSpec((STRETCH, col.total), back),
            pl.BlockSpec((1, width), lambda i: (0, 0)),
            pl.BlockSpec((1, width), lambda i: (0, 0)),
            pl.BlockSpec((8, LANES), lambda i: (0, 0)),
        ],
        out_shape=[
            jax.ShapeDtypeStruct((length, col.total), HALF),
            jax.ShapeDtypeStruct((1, width), FULL),
            jax.ShapeDtypeStruct((1, width), FULL),
            jax.ShapeDtypeStruct((8, LANES), FULL),
        ],
        scratch_shapes=[pltpu.VMEM((state_size, width), FULL)],
        cost_estimate=pl.CostEstimate(flops=20_000_000_000, bytes_accessed=40_000_000, transcendentals=0),
        compiler_params=pltpu.CompilerParams(vmem_limit_bytes=48 * 2**20),
    )(
        packed, y, states, grad_mamba, inverse, product, gain, segments[:, None],
        segments.reshape(count, 1, STRETCH), segments[:, None], head_params,
    )


def turned(values, cosine, sine):
    return values * cosine + pltpu.roll(values, ATT_DIM // 2, 1) * sine


def attend_forward_kernel(col, heads, p_ref, cos_ref, sin_ref, segc_ref, segr_ref, out_ref, lse_ref):
    length = p_ref.shape[0]
    scale = 1.0 / math.sqrt(ATT_DIM)
    keys = turned(p_ref[:, col.key[0] : col.key[1]], cos_ref[...], sin_ref[...]).astype(HALF)
    values = p_ref[:, col.value[0] : col.value[1]].astype(HALF)
    for block in range(length // ATT_BLOCK):
        rows = slice(block * ATT_BLOCK, (block + 1) * ATT_BLOCK)
        end = (block + 1) * ATT_BLOCK
        place = iota((ATT_BLOCK, end), 0) + block * ATT_BLOCK
        allowed = (place >= iota((ATT_BLOCK, end), 1)) & (segc_ref[rows, :] == segr_ref[:, :end])
        blocked = jnp.where(allowed, 0.0, MASKED)
        for head in range(heads):
            lanes = slice(head * ATT_DIM, (head + 1) * ATT_DIM)
            query = (turned(p_ref[rows, lanes], cos_ref[rows, :], sin_ref[rows, :]) * scale).astype(HALF)
            scores = mm_nt(query, keys[:end]) + blocked
            highest = jnp.max(scores, 1, keepdims=True)
            weights = jnp.exp(scores - highest)
            total = jnp.sum(weights, 1, keepdims=True)
            out_ref[rows, lanes] = (mm(weights.astype(HALF), values[:end]) / total).astype(HALF)
            lse_ref[rows, lanes] = jnp.broadcast_to(highest + jnp.log(total), (ATT_BLOCK, ATT_DIM))


def attend_forward(col, heads, packed, tables, segments):
    length = packed.shape[0]
    whole = lambda i: (0, 0)
    return pl.pallas_call(
        functools.partial(attend_forward_kernel, col, heads),
        grid=(1,),
        in_specs=[
            pl.BlockSpec((length, col.attention), whole),
            pl.BlockSpec((length, ATT_DIM), whole),
            pl.BlockSpec((length, ATT_DIM), whole),
            pl.BlockSpec((length, 1), whole),
            pl.BlockSpec((1, length), whole),
        ],
        out_specs=[
            pl.BlockSpec((length, heads * ATT_DIM), whole),
            pl.BlockSpec((length, heads * ATT_DIM), whole),
        ],
        out_shape=[
            jax.ShapeDtypeStruct((length, heads * ATT_DIM), HALF),
            jax.ShapeDtypeStruct((length, heads * ATT_DIM), FULL),
        ],
        cost_estimate=pl.CostEstimate(flops=2_000_000_000, bytes_accessed=5_000_000, transcendentals=2_000_000),
        compiler_params=pltpu.CompilerParams(vmem_limit_bytes=48 * 2**20),
    )(packed, tables[0], tables[1], segments[:, None], segments[None, :])


def attend_backward_kernel(
    col, heads, p_ref, out_ref, lse_ref, go_ref, cos_ref, sin_ref, segc_ref, segr_ref, g_in_ref, g_ref,
    key_grad, value_grad,
):
    length = p_ref.shape[0]
    scale = 1.0 / math.sqrt(ATT_DIM)
    keys = turned(p_ref[:, col.key[0] : col.key[1]], cos_ref[...], sin_ref[...]).astype(HALF)
    values = p_ref[:, col.value[0] : col.value[1]].astype(HALF)
    key_grad[...] = jnp.zeros_like(key_grad)
    value_grad[...] = jnp.zeros_like(value_grad)
    for block in range(length // ATT_BLOCK):
        rows = slice(block * ATT_BLOCK, (block + 1) * ATT_BLOCK)
        end = (block + 1) * ATT_BLOCK
        place = iota((ATT_BLOCK, end), 0) + block * ATT_BLOCK
        allowed = (place >= iota((ATT_BLOCK, end), 1)) & (segc_ref[rows, :] == segr_ref[:, :end])
        blocked = jnp.where(allowed, 0.0, MASKED)
        cosine, sine = cos_ref[rows, :], sin_ref[rows, :]
        for head in range(heads):
            lanes = slice(head * ATT_DIM, (head + 1) * ATT_DIM)
            query = (turned(p_ref[rows, lanes], cosine, sine) * scale).astype(HALF)
            weights = jnp.exp(mm_nt(query, keys[:end]) + blocked - lse_ref[rows, lanes][:, 0:1])
            grad_low = go_ref[rows, lanes].astype(HALF)
            delta = jnp.sum(grad_low.astype(FULL) * out_ref[rows, lanes].astype(FULL), 1, keepdims=True)
            grad_scores = (weights * (mm_nt(grad_low, values[:end]) - delta)).astype(HALF)
            value_grad[:end, :] += mm_tn(weights.astype(HALF), grad_low)
            key_grad[:end, :] += mm_tn(grad_scores, query)
            grad_query = mm(grad_scores, keys[:end]) * scale
            g_ref[rows, lanes] = turned(grad_query, cosine, -sine).astype(HALF)
    g_ref[:, col.key[0] : col.key[1]] = turned(key_grad[...], cos_ref[...], -sin_ref[...]).astype(HALF)
    g_ref[:, col.value[0] : col.value[1]] = value_grad[...].astype(HALF)


def attend_backward(col, heads, packed, attended, lse, grad_attended, tables, segments, grads):
    length = packed.shape[0]
    width = heads * ATT_DIM
    whole = lambda i: (0, 0)
    return pl.pallas_call(
        functools.partial(attend_backward_kernel, col, heads),
        grid=(1,),
        in_specs=[
            pl.BlockSpec((length, col.attention), whole),
            pl.BlockSpec((length, width), whole),
            pl.BlockSpec((length, width), whole),
            pl.BlockSpec((length, width), whole),
            pl.BlockSpec((length, ATT_DIM), whole),
            pl.BlockSpec((length, ATT_DIM), whole),
            pl.BlockSpec((length, 1), whole),
            pl.BlockSpec((1, length), whole),
            pl.BlockSpec(memory_space=pl.ANY),
        ],
        out_specs=pl.BlockSpec((length, col.attention), whole),
        out_shape=jax.ShapeDtypeStruct(grads.shape, grads.dtype),
        scratch_shapes=[pltpu.VMEM((length, ATT_DIM), FULL), pltpu.VMEM((length, ATT_DIM), FULL)],
        input_output_aliases={8: 0},
        cost_estimate=pl.CostEstimate(flops=5_000_000_000, bytes_accessed=10_000_000, transcendentals=2_000_000),
        compiler_params=pltpu.CompilerParams(vmem_limit_bytes=48 * 2**20),
    )(
        packed, attended, lse, grad_attended, tables[0], tables[1], segments[:, None], segments[None, :], grads
    )


def rope_tables(length):
    half = ATT_DIM // 2
    positions = jnp.arange(length, dtype=FULL)
    frequency = ROPE_BASE ** (-jnp.arange(half, dtype=FULL) / half)
    angles = positions[:, None] * frequency[None, :]
    cosine, sine = jnp.cos(angles), jnp.sin(angles)
    return jnp.concatenate([cosine, cosine], 1), jnp.concatenate([-sine, sine], 1)


def gather_rows(pieces):
    return lax.all_gather(pieces, "tensor", axis=0, tiled=True)


def sum_rows(pieces):
    return lax.psum_scatter(pieces, "tensor", scatter_dimension=0, tiled=True).astype(FULL)


def norm_forward(values, gain_vals):
    inverse = lax.rsqrt(jnp.mean(values * values, -1, keepdims=True) + EPSILON)
    plain = values * inverse
    return plain, inverse, plain * gain_vals


def norm_backward(grad_above, plain, inverse, gain_vals):
    grad_plain = grad_above * gain_vals
    grad_below = inverse * (grad_plain - plain * jnp.mean(grad_plain * plain, -1, keepdims=True))
    return grad_below, jnp.sum(grad_above * plain, 0)


def silu_parts(gate_input):
    sigmoid_vals = jax.nn.sigmoid(gate_input)
    return gate_input * sigmoid_vals, sigmoid_vals * (1.0 + gate_input * (1.0 - sigmoid_vals))


def dot_tn(a, b):
    return jnp.einsum("sa,sb->ab", a, b, preferred_element_type=FULL)


def dot_nt(a, b):
    return jnp.einsum("sb,ab->sa", a, b, preferred_element_type=FULL)


def body(
    hidden_in,
    segments,
    norm_gain,
    mamba_in,
    step_weight,
    state_weight,
    decay_log,
    step_bias,
    skip_gain,
    gated_gain,
    query_weight,
    keyval_weight,
    mamba_out,
    attn_out,
    ffn_gain,
    gate_up,
    down_weight,
    cotangent,
):
    tensor_index = lax.axis_index("tensor")
    heads = decay_log.shape[0]
    width = mamba_in.shape[2]
    state_size = state_weight.shape[2]
    query_width = query_weight.shape[1]
    qheads = query_width // ATT_DIM
    units = gate_up.shape[2]
    rows_local = hidden_in.shape[0]
    block = norm_gain.shape[0]
    group_size = ATT_HEADS // KV_HEADS
    kv_head = tensor_index * qheads // group_size
    col = Columns(query_width, width, state_size)

    own_keyval = lax.dynamic_slice_in_dim(keyval_weight, kv_head * ATT_DIM, ATT_DIM, 2)
    spare = LANES - heads - 2
    packed_in = jnp.concatenate(
        [
            query_weight,
            own_keyval[:, 0],
            own_keyval[:, 1],
            mamba_in[:, 0],
            mamba_in[:, 1],
            state_weight[:, 0],
            state_weight[:, 1],
            step_weight,
            jnp.zeros((block, spare), HALF),
            norm_gain[:, None],
            ffn_gain[:, None],
        ],
        1,
    )
    weight_in = lax.all_gather(packed_in, "dp", axis=0, tiled=True)
    hidden_rows = gather_rows(hidden_in)
    weight_out = lax.all_gather(jnp.concatenate([mamba_out, attn_out], 0), "dp", axis=1, tiled=True)
    weight_up = lax.all_gather(gate_up.reshape(block, 2 * units), "dp", axis=0, tiled=True)
    weight_down = lax.all_gather(down_weight, "dp", axis=1, tiled=True)
    grad_rows = gather_rows(cotangent)

    gain_one = weight_in[:, col.total - 2].astype(FULL)
    gain_two = weight_in[:, col.total - 1].astype(FULL)
    sequence = norm_forward(hidden_rows.astype(FULL), gain_one)[2].astype(HALF)
    length = sequence.shape[0]
    packed = jnp.dot(sequence, weight_in, preferred_element_type=FULL)
    head_params = jnp.pad(
        jnp.stack([decay_log, step_bias, skip_gain]), ((0, 5), (0, LANES - heads))
    )
    tables = rope_tables(length)

    scan_y, states, gated_vals, squares = scan_forward(
        col, heads, state_size, packed, segments, head_params
    )
    square_sum = lax.psum(squares[:, 0], "tensor")
    gated_inverse = lax.rsqrt(square_sum / (MAMBA_HEADS * HEAD_DIM) + EPSILON)[:, None]
    attended, lse = attend_forward(col, qheads, packed, tables, segments)
    gated_scale = gated_gain.astype(FULL)
    gated_plain = gated_vals * gated_inverse
    branches = jnp.concatenate([(gated_plain * gated_scale).astype(HALF), attended], 1)
    middle = hidden_in.astype(FULL) + sum_rows(jnp.dot(branches, weight_out))
    plain_two, inverse_two, scaled_two = norm_forward(middle, gain_two)
    ffn_rows = gather_rows(scaled_two.astype(HALF))
    gate_vals = jnp.dot(ffn_rows, weight_up, preferred_element_type=FULL)
    gate_part, up_part = gate_vals[:, :units], gate_vals[:, units:]
    silu_gate, silu_slope = silu_parts(gate_part)
    activated = (silu_gate * up_part).astype(HALF)
    grad_act = dot_nt(grad_rows, weight_down)
    grad_gate = jnp.concatenate(
        [grad_act * up_part * silu_slope, grad_act * silu_gate], 1
    ).astype(HALF)
    grad_ffn_in = sum_rows(dot_nt(grad_gate, weight_up).astype(HALF))
    grad_middle_norm, ffn_gain_part = norm_backward(grad_ffn_in, plain_two, inverse_two, gain_two)
    grad_middle = cotangent.astype(FULL) + grad_middle_norm
    grad_mixed = gather_rows(grad_middle.astype(HALF))

    ffn_out = sum_rows(jnp.dot(activated, weight_down))
    hidden_out = (middle + ffn_out).astype(HALF)
    up_grad = dot_tn(ffn_rows, grad_gate).astype(HALF)
    down_grad = dot_tn(activated, grad_rows).astype(HALF)
    gate_share = lax.psum_scatter(up_grad, "dp", scatter_dimension=0, tiled=True)
    down_share = lax.psum_scatter(down_grad, "dp", scatter_dimension=1, tiled=True)

    grad_branches = dot_nt(grad_mixed, weight_out)
    out_grad = dot_tn(branches, grad_mixed).astype(HALF)
    out_share = lax.psum_scatter(out_grad, "dp", scatter_dimension=1, tiled=True)
    grad_mamba = grad_branches[:, :width]
    product_sum = lax.psum(jnp.sum(grad_mamba * gated_scale * gated_plain, -1), "tensor")[:, None]
    grads, gain_part, skip_part, head_part = scan_backward(
        col,
        heads,
        state_size,
        packed,
        scan_y,
        states,
        grad_mamba,
        gated_inverse,
        product_sum,
        gated_scale[None, :],
        segments,
        head_params,
    )
    grads = attend_backward(
        col, qheads, packed, attended, lse, grad_branches[:, width:], tables, segments, grads
    )
    grad_first = sum_rows(dot_nt(grads, weight_in).astype(HALF))
    in_grad = dot_tn(sequence, grads)
    in_share = lax.psum_scatter(in_grad.astype(HALF), "dp", scatter_dimension=0, tiled=True)
    plain_one, inverse_one, _ = norm_forward(hidden_in.astype(FULL), gain_one)
    grad_hidden_norm, norm_gain_part = norm_backward(grad_first, plain_one, inverse_one, gain_one)
    hidden_grad = grad_middle + grad_hidden_norm

    keyval_part = jnp.stack(
        [in_share[:, slice(*col.key)], in_share[:, slice(*col.value)]], 1
    )
    keyval_grad = lax.dynamic_update_slice_in_dim(
        jnp.zeros(keyval_weight.shape, HALF), keyval_part, kv_head * ATT_DIM, 2
    ).reshape(block, -1)
    shared = lax.psum(
        jnp.concatenate([in_share[:, col.inmap[0] : col.outmap[1]], keyval_grad], 1), "tensor"
    ).astype(FULL)
    state_weight_grad = shared[:, : 2 * state_size].reshape(state_weight.shape)
    keyval_weight_grad = shared[:, 2 * state_size :].reshape(keyval_weight.shape)

    gains = lax.psum(jnp.stack([norm_gain_part, ffn_gain_part]), ("dp", "tensor"))
    dp_index = lax.axis_index("dp")
    gains = lax.dynamic_slice_in_dim(gains, dp_index * block, block, 1)
    head_sums = lax.psum(
        jnp.concatenate(
            [
                head_part[0, :heads],
                head_part[1, :heads],
                skip_part.reshape(heads, HEAD_DIM).sum(1),
                gain_part[0],
            ]
        ),
        "dp",
    )
    inner_grad = jnp.stack([in_share[:, slice(*col.gate)], in_share[:, slice(*col.drive)]], 1)
    return (
        hidden_out,
        hidden_grad,
        gains[0],
        inner_grad.astype(FULL),
        in_share[:, col.step[0] : col.step[0] + heads].astype(FULL),
        state_weight_grad,
        head_sums[:heads],
        head_sums[heads : 2 * heads],
        head_sums[2 * heads : 3 * heads],
        head_sums[3 * heads :],
        in_share[:, slice(*col.query)].astype(FULL),
        keyval_weight_grad,
        out_share[:width].astype(FULL),
        out_share[width:].astype(FULL),
        gains[1],
        gate_share.reshape(gate_up.shape).astype(FULL),
        down_share.astype(FULL),
    )


def solution(mesh):
    rows = P(("dp", "tensor"), None)
    weights_in = P("dp", None, "tensor")
    return jax.shard_map(
        body,
        mesh=mesh,
        in_specs=(
            rows,
            P("dp"),
            P("dp"),
            weights_in,
            P("dp", "tensor"),
            P("dp", None, None),
            P("tensor"),
            P("tensor"),
            P("tensor"),
            P("tensor"),
            P("dp", "tensor"),
            P("dp", None, None),
            P("tensor", "dp"),
            P("tensor", "dp"),
            P("dp"),
            weights_in,
            P("tensor", "dp"),
            rows,
        ),
        out_specs=(
            rows,
            rows,
            P("dp"),
            weights_in,
            P("dp", "tensor"),
            P("dp", None, None),
            P("tensor"),
            P("tensor"),
            P("tensor"),
            P("tensor"),
            P("dp", "tensor"),
            P("dp", None, None),
            P("tensor", "dp"),
            P("tensor", "dp"),
            P("dp"),
            weights_in,
            P("tensor", "dp"),
        ),
        check_vma=False,
    )
```

```python
import functools
import math
import jax
import jax.numpy as jnp
from jax import lax
from jax.experimental import pallas as pl
from jax.experimental.pallas import tpu as pltpu
from jax.sharding import PartitionSpec as P

MAMBA_HEADS = 48
HEAD_DIM = 64
ATT_HEADS = 8
KV_HEADS = 2
ATT_DIM = 128
STRETCH = 128
ATT_BLOCK = 256
EPSILON = 1e-05
PRECISE = lax.Precision.HIGHEST
ROPE_BASE = 10000.0
LANES = 128
MASKED = -1e30
HALF = jnp.bfloat16
FULL = jnp.float32


def mm(a, b):
    return jnp.dot(a, b, preferred_element_type=FULL)


def mm_nt(a, b):
    return lax.dot_general(a, b, (((1,), (1,)), ((), ())), preferred_element_type=FULL)


def mm_tn(a, b):
    return lax.dot_general(a, b, (((0,), (0,)), ((), ())), preferred_element_type=FULL)


def softplus(v):
    return jnp.maximum(v, 0.0) + jnp.log1p(jnp.exp(-jnp.abs(v)))


def sigmoid(v):
    return 1.0 / (1.0 + jnp.exp(-v))


def iota(shape, dim):
    return lax.broadcasted_iota(jnp.int32, shape, dim)


def halves(left, right, size):
    return jnp.where(iota((size, LANES), 1) < HEAD_DIM, left, right)


def stacked_pair(pair):
    low = iota(pair.shape, 1) < HEAD_DIM
    zero = jnp.zeros_like(pair)
    return jnp.concatenate([jnp.where(low, pair, zero), jnp.where(low, zero, pair)], 0)


class Columns:
    def __init__(self, query, width, state):
        self.query = (0, query)
        self.key = (query, query + ATT_DIM)
        self.value = (query + ATT_DIM, query + 2 * ATT_DIM)
        start = query + 2 * ATT_DIM
        self.attention = start
        self.gate = (start, start + width)
        self.drive = (start + width, start + 2 * width)
        start += 2 * width
        self.inmap = (start, start + state)
        self.outmap = (start + state, start + 2 * state)
        start += 2 * state
        self.step = (start, start + LANES)
        self.total = start + LANES


def stretch_common(col, packed, segc_ref, segr_ref, head_ref, before):
    span = STRETCH
    raw = packed[:, col.step[0] : col.step[1]] + head_ref[1:2, :]
    step = softplus(raw)
    keep = -jnp.exp(head_ref[0:1, :]) * step
    row, column = iota((span, span), 0), iota((span, span), 1)
    running = jnp.dot(
        (row >= column).astype(FULL), keep, precision=PRECISE, preferred_element_type=FULL
    )
    segc, segr = segc_ref[...], segr_ref[0]
    causal = (row >= column) & (segc == segr)
    blocked = jnp.where(causal, 0.0, MASKED)
    live = (segc == before).astype(FULL)
    last = segc[span - 1 : span, :]
    tail = (segc == last).astype(FULL)
    old = (last == before).astype(FULL)
    return raw, step, keep, running, running.T, blocked, live, tail, old


def pair_decay(pair, running, running_t, blocked, live, tail, old):
    span = STRETCH
    a, b = 2 * pair, 2 * pair + 1
    col_a = jnp.broadcast_to(running[:, a : a + 1], (span, LANES))
    col_b = jnp.broadcast_to(running[:, b : b + 1], (span, LANES))
    decay_a = jnp.exp(col_a - running_t[a : a + 1, :] + blocked)
    decay_b = jnp.exp(col_b - running_t[b : b + 1, :] + blocked)
    both = halves(col_a, col_b, span)
    last = both[span - 1 : span, :]
    into = jnp.exp(both) * live
    weight = jnp.exp(last - both) * tail
    keep_old = jnp.exp(last) * old
    return decay_a, decay_b, into, weight, keep_old


def scan_forward_kernel(col, heads, p_ref, segc_ref, segr_ref, head_ref, y_ref, states_ref, gated_ref, square_ref, state, before):
    index = pl.program_id(0)
    span = STRETCH

    @pl.when(index == 0)
    def _():
        state[...] = jnp.zeros_like(state)
        before[...] = jnp.full_like(before, -1)

    raw, step, keep, running, running_t, blocked, live, tail, old = stretch_common(
        col, p_ref, segc_ref, segr_ref, head_ref, before[...]
    )
    inmap = p_ref[:, col.inmap[0] : col.inmap[1]].astype(HALF)
    outmap = p_ref[:, col.outmap[0] : col.outmap[1]].astype(HALF)
    inmap_t = inmap.T
    scores = mm_nt(outmap, inmap)
    square = jnp.zeros((span, 1), FULL)
    for pair in range(heads // 2):
        at = pair * LANES
        lanes = slice(at, at + LANES)
        decay_a, decay_b, into, weight, keep_old = pair_decay(
            pair, running, running_t, blocked, live, tail, old
        )
        drive = p_ref[:, col.drive[0] + at : col.drive[0] + at + LANES]
        gate = p_ref[:, col.gate[0] + at : col.gate[0] + at + LANES]
        driven = drive * halves(step[:, 2 * pair : 2 * pair + 1], step[:, 2 * pair + 1 : 2 * pair + 2], span)
        driven_low = driven.astype(HALF)
        mix = jnp.concatenate([(decay_a * scores).astype(HALF), (decay_b * scores).astype(HALF)], 1)
        held = state[:, lanes]
        held_low = held.astype(HALF)
        states_ref[0, :, lanes] = held_low
        result = mm(mix, stacked_pair(driven_low)) + mm(outmap, held_low) * into
        state[:, lanes] = held * keep_old + mm(inmap_t, (driven_low.astype(FULL) * weight).astype(HALF))
        y_ref[:, lanes] = result
        skip = halves(head_ref[2:3, 2 * pair : 2 * pair + 1], head_ref[2:3, 2 * pair + 1 : 2 * pair + 2], 1)
        gated = (result + skip * drive) * (gate * sigmoid(gate))
        gated_ref[:, lanes] = gated
        square = square + jnp.sum(gated * gated, 1, keepdims=True)
    square_ref[...] = jnp.broadcast_to(square, square_ref.shape)
    before[...] = segc_ref[span - 1 : span, :]


def scan_forward(col, heads, state_size, packed, segments, head_params):
    length = packed.shape[0]
    width = heads * HEAD_DIM
    count = length // STRETCH
    return pl.pallas_call(
        functools.partial(scan_forward_kernel, col, heads),
        grid=(count,),
        in_specs=[
            pl.BlockSpec((STRETCH, col.total), lambda i: (i, 0)),
            pl.BlockSpec((STRETCH, 1), lambda i: (i, 0)),
            pl.BlockSpec((1, 1, STRETCH), lambda i: (i, 0, 0)),
            pl.BlockSpec((8, LANES), lambda i: (0, 0)),
        ],
        out_specs=[
            pl.BlockSpec((STRETCH, width), lambda i: (i, 0)),
            pl.BlockSpec((1, state_size, width), lambda i: (i, 0, 0)),
            pl.BlockSpec((STRETCH, width), lambda i: (i, 0)),
            pl.BlockSpec((STRETCH, LANES), lambda i: (i, 0)),
        ],
        out_shape=[
            jax.ShapeDtypeStruct((length, width), FULL),
            jax.ShapeDtypeStruct((count, state_size, width), HALF),
            jax.ShapeDtypeStruct((length, width), FULL),
            jax.ShapeDtypeStruct((length, LANES), FULL),
        ],
        scratch_shapes=[pltpu.VMEM((state_size, width), FULL), pltpu.VMEM((1, 1), jnp.int32)],
        cost_estimate=pl.CostEstimate(flops=6_000_000_000, bytes_accessed=30_000_000, transcendentals=0),
        compiler_params=pltpu.CompilerParams(vmem_limit_bytes=48 * 2**20),
    )(packed, segments[:, None], segments.reshape(count, 1, STRETCH), head_params)


def scan_backward_kernel(
    col, heads, total_width, p_ref, y_ref, states_ref, gm_ref, inv_ref, prod_ref, gain_ref,
    segc_ref, segr_ref, segb_ref, head_ref, g_ref, gain_grad_ref, skip_grad_ref, head_grad_ref, future,
):
    step_index = pl.program_id(0)
    count = pl.num_programs(0)
    span = STRETCH

    @pl.when(step_index == 0)
    def _():
        future[...] = jnp.zeros_like(future)
        gain_grad_ref[...] = jnp.zeros_like(gain_grad_ref)
        skip_grad_ref[...] = jnp.zeros_like(skip_grad_ref)
        head_grad_ref[...] = jnp.zeros_like(head_grad_ref)

    before = jnp.where(step_index == count - 1, -1, segb_ref[span - 1 : span, :])
    raw, step, keep, running, running_t, blocked, live, tail, old = stretch_common(
        col, p_ref, segc_ref, segr_ref, head_ref, before
    )
    inmap = p_ref[:, col.inmap[0] : col.inmap[1]].astype(HALF)
    outmap = p_ref[:, col.outmap[0] : col.outmap[1]].astype(HALF)
    outmap_t = outmap.T
    scores = mm_nt(outmap, inmap)
    lane = iota((span, LANES), 1)
    head_lane = iota((1, LANES), 1)
    paired = jnp.zeros((span, span), FULL)
    grad_in = jnp.zeros(inmap.shape, FULL)
    grad_out = jnp.zeros(outmap.shape, FULL)
    grad_running = jnp.zeros((span, LANES), FULL)
    grad_step = jnp.zeros((span, LANES), FULL)
    grad_last = jnp.zeros((1, LANES), FULL)
    inverse, product = inv_ref[:, 0:1], prod_ref[:, 0:1] * (1.0 / total_width)
    for pair in range(heads // 2):
        at = pair * LANES
        lanes = slice(at, at + LANES)
        a, b = 2 * pair, 2 * pair + 1
        decay_a, decay_b, into, weight, keep_old = pair_decay(
            pair, running, running_t, blocked, live, tail, old
        )
        drive = p_ref[:, col.drive[0] + at : col.drive[0] + at + LANES]
        gate = p_ref[:, col.gate[0] + at : col.gate[0] + at + LANES]
        result = y_ref[:, lanes]
        skip = halves(head_ref[2:3, a : a + 1], head_ref[2:3, b : b + 1], 1)
        sig = sigmoid(gate)
        silu = gate * sig
        ssm = result + skip * drive
        plain = ssm * silu * inverse
        grad_above = gm_ref[:, lanes].astype(FULL)
        gain_grad_ref[:, lanes] += jnp.sum(grad_above * plain, 0, keepdims=True)
        grad_gated = inverse * (grad_above * gain_ref[:, lanes] - plain * product)
        g_ref[:, col.gate[0] + at : col.gate[0] + at + LANES] = (
            grad_gated * ssm * (sig * (1.0 + gate * (1.0 - sig)))
        ).astype(HALF)
        grad_y = grad_gated * silu
        grad_y_low = grad_y.astype(HALF)
        grad_y = grad_y_low.astype(FULL)
        step_pair = halves(step[:, a : a + 1], step[:, b : b + 1], span)
        driven_low = (drive * step_pair).astype(HALF)
        driven = driven_low.astype(FULL)
        grad_rows = stacked_pair(grad_y_low)
        inner = mm_nt(grad_rows, driven_low)
        paired = paired + decay_a * inner[:span] + decay_b * inner[span:]
        mix = jnp.concatenate([(decay_a * scores).astype(HALF), (decay_b * scores).astype(HALF)], 0)
        later = future[:, lanes]
        later_low = later.astype(HALF)
        held_low = states_ref[0, :, lanes]
        reach = mm(inmap, later_low) * weight
        grad_driven = mm_tn(mix, grad_rows) + reach
        weighted = (driven * weight).astype(HALF)
        spread = (grad_y * into).astype(HALF)
        grad_in = grad_in + mm_nt(weighted, later_low)
        grad_out = grad_out + mm_nt(spread, held_low)
        future[:, lanes] = later * keep_old + mm(outmap_t, spread)
        g_ref[:, col.drive[0] + at : col.drive[0] + at + LANES] = (
            step_pair * grad_driven + skip * grad_y
        ).astype(HALF)
        skip_grad_ref[:, lanes] += jnp.sum(grad_y * drive, 0, keepdims=True)
        turn = grad_y * result - driven * grad_driven
        left = lane < HEAD_DIM
        from_drive = drive * grad_driven
        ends = jnp.sum(driven * reach, 0, keepdims=True) + keep_old * jnp.sum(
            later * held_low.astype(FULL), 0, keepdims=True
        )
        for head, mask in ((a, left), (b, ~left)):
            grad_running = grad_running + jnp.where(
                lane == head, jnp.sum(jnp.where(mask, turn, 0.0), 1, keepdims=True), 0.0
            )
            grad_step = grad_step + jnp.where(
                lane == head, jnp.sum(jnp.where(mask, from_drive, 0.0), 1, keepdims=True), 0.0
            )
            grad_last = grad_last + jnp.where(
                head_lane == head, jnp.sum(jnp.where(mask[0:1], ends, 0.0), 1, keepdims=True), 0.0
            )
    paired = paired.astype(HALF)
    grad_out = grad_out + mm(paired, inmap)
    grad_in = grad_in + mm_tn(paired, outmap)
    g_ref[:, col.inmap[0] : col.inmap[1]] = grad_in.astype(HALF)
    g_ref[:, col.outmap[0] : col.outmap[1]] = grad_out.astype(HALF)
    row, column = iota((span, span), 0), iota((span, span), 1)
    grad_keep = (
        jnp.dot((row <= column).astype(FULL), grad_running, precision=PRECISE, preferred_element_type=FULL)
        + grad_last
    )
    grad_raw = (grad_step - grad_keep * jnp.exp(head_ref[0:1, :])) * sigmoid(raw)
    grad_raw = jnp.where(lane < heads, grad_raw, 0.0)
    g_ref[:, col.step[0] : col.step[1]] = grad_raw.astype(HALF)
    g_ref[:, 0 : col.attention] = jnp.zeros((span, col.attention), HALF)
    head_grad_ref[0:1, :] += jnp.sum(keep * grad_keep, 0, keepdims=True)
    head_grad_ref[1:2, :] += jnp.sum(grad_raw, 0, keepdims=True)


def scan_backward(col, heads, state_size, packed, y, states, grad_mamba, inverse, product, gain, segments, head_params):
    length = packed.shape[0]
    width = heads * HEAD_DIM
    count = length // STRETCH
    back = lambda i: (count - 1 - i, 0)
    return pl.pallas_call(
        functools.partial(scan_backward_kernel, col, heads, MAMBA_HEADS * HEAD_DIM),
        grid=(count,),
        in_specs=[
            pl.BlockSpec((STRETCH, col.total), back),
            pl.BlockSpec((STRETCH, width), back),
            pl.BlockSpec((1, state_size, width), lambda i: (count - 1 - i, 0, 0)),
            pl.BlockSpec((STRETCH, width), back),
            pl.BlockSpec((STRETCH, 1), back),
            pl.BlockSpec((STRETCH, 1), back),
            pl.BlockSpec((1, width), lambda i: (0, 0)),
            pl.BlockSpec((STRETCH, 1), back),
            pl.BlockSpec((1, 1, STRETCH), lambda i: (count - 1 - i, 0, 0)),
            pl.BlockSpec((STRETCH, 1), lambda i: (jnp.maximum(count - 2 - i, 0), 0)),
            pl.BlockSpec((8, LANES), lambda i: (0, 0)),
        ],
        out_specs=[
            pl.BlockSpec((STRETCH, col.total), back),
            pl.BlockSpec((1, width), lambda i: (0, 0)),
            pl.BlockSpec((1, width), lambda i: (0, 0)),
            pl.BlockSpec((8, LANES), lambda i: (0, 0)),
        ],
        out_shape=[
            jax.ShapeDtypeStruct((length, col.total), HALF),
            jax.ShapeDtypeStruct((1, width), FULL),
            jax.ShapeDtypeStruct((1, width), FULL),
            jax.ShapeDtypeStruct((8, LANES), FULL),
        ],
        scratch_shapes=[pltpu.VMEM((state_size, width), FULL)],
        cost_estimate=pl.CostEstimate(flops=20_000_000_000, bytes_accessed=40_000_000, transcendentals=0),
        compiler_params=pltpu.CompilerParams(vmem_limit_bytes=48 * 2**20),
    )(
        packed, y, states, grad_mamba, inverse, product, gain, segments[:, None],
        segments.reshape(count, 1, STRETCH), segments[:, None], head_params,
    )


def turned(values, cosine, sine):
    return values * cosine + pltpu.roll(values, ATT_DIM // 2, 1) * sine


def attend_forward_kernel(col, heads, p_ref, cos_ref, sin_ref, segc_ref, segr_ref, out_ref, lse_ref):
    length = p_ref.shape[0]
    scale = 1.0 / math.sqrt(ATT_DIM)
    keys = turned(p_ref[:, col.key[0] : col.key[1]], cos_ref[...], sin_ref[...]).astype(HALF)
    values = p_ref[:, col.value[0] : col.value[1]].astype(HALF)
    for block in range(length // ATT_BLOCK):
        rows = slice(block * ATT_BLOCK, (block + 1) * ATT_BLOCK)
        end = (block + 1) * ATT_BLOCK
        place = iota((ATT_BLOCK, end), 0) + block * ATT_BLOCK
        allowed = (place >= iota((ATT_BLOCK, end), 1)) & (segc_ref[rows, :] == segr_ref[:, :end])
        blocked = jnp.where(allowed, 0.0, MASKED)
        for head in range(heads):
            lanes = slice(head * ATT_DIM, (head + 1) * ATT_DIM)
            query = (turned(p_ref[rows, lanes], cos_ref[rows, :], sin_ref[rows, :]) * scale).astype(HALF)
            scores = mm_nt(query, keys[:end]) + blocked
            highest = jnp.max(scores, 1, keepdims=True)
            weights = jnp.exp(scores - highest)
            total = jnp.sum(weights, 1, keepdims=True)
            out_ref[rows, lanes] = (mm(weights.astype(HALF), values[:end]) / total).astype(HALF)
            lse_ref[rows, lanes] = jnp.broadcast_to(highest + jnp.log(total), (ATT_BLOCK, ATT_DIM))


def attend_forward(col, heads, packed, tables, segments):
    length = packed.shape[0]
    whole = lambda i: (0, 0)
    return pl.pallas_call(
        functools.partial(attend_forward_kernel, col, heads),
        grid=(1,),
        in_specs=[
            pl.BlockSpec((length, col.attention), whole),
            pl.BlockSpec((length, ATT_DIM), whole),
            pl.BlockSpec((length, ATT_DIM), whole),
            pl.BlockSpec((length, 1), whole),
            pl.BlockSpec((1, length), whole),
        ],
        out_specs=[
            pl.BlockSpec((length, heads * ATT_DIM), whole),
            pl.BlockSpec((length, heads * ATT_DIM), whole),
        ],
        out_shape=[
            jax.ShapeDtypeStruct((length, heads * ATT_DIM), HALF),
            jax.ShapeDtypeStruct((length, heads * ATT_DIM), FULL),
        ],
        cost_estimate=pl.CostEstimate(flops=2_000_000_000, bytes_accessed=5_000_000, transcendentals=2_000_000),
        compiler_params=pltpu.CompilerParams(vmem_limit_bytes=48 * 2**20),
    )(packed, tables[0], tables[1], segments[:, None], segments[None, :])


def attend_backward_kernel(
    col, heads, p_ref, out_ref, lse_ref, go_ref, cos_ref, sin_ref, segc_ref, segr_ref, g_in_ref, g_ref,
    key_grad, value_grad,
):
    length = p_ref.shape[0]
    scale = 1.0 / math.sqrt(ATT_DIM)
    keys = turned(p_ref[:, col.key[0] : col.key[1]], cos_ref[...], sin_ref[...]).astype(HALF)
    values = p_ref[:, col.value[0] : col.value[1]].astype(HALF)
    key_grad[...] = jnp.zeros_like(key_grad)
    value_grad[...] = jnp.zeros_like(value_grad)
    for block in range(length // ATT_BLOCK):
        rows = slice(block * ATT_BLOCK, (block + 1) * ATT_BLOCK)
        end = (block + 1) * ATT_BLOCK
        place = iota((ATT_BLOCK, end), 0) + block * ATT_BLOCK
        allowed = (place >= iota((ATT_BLOCK, end), 1)) & (segc_ref[rows, :] == segr_ref[:, :end])
        blocked = jnp.where(allowed, 0.0, MASKED)
        cosine, sine = cos_ref[rows, :], sin_ref[rows, :]
        for head in range(heads):
            lanes = slice(head * ATT_DIM, (head + 1) * ATT_DIM)
            query = (turned(p_ref[rows, lanes], cosine, sine) * scale).astype(HALF)
            weights = jnp.exp(mm_nt(query, keys[:end]) + blocked - lse_ref[rows, lanes][:, 0:1])
            grad_low = go_ref[rows, lanes].astype(HALF)
            delta = jnp.sum(grad_low.astype(FULL) * out_ref[rows, lanes].astype(FULL), 1, keepdims=True)
            grad_scores = (weights * (mm_nt(grad_low, values[:end]) - delta)).astype(HALF)
            value_grad[:end, :] += mm_tn(weights.astype(HALF), grad_low)
            key_grad[:end, :] += mm_tn(grad_scores, query)
            grad_query = mm(grad_scores, keys[:end]) * scale
            g_ref[rows, lanes] = turned(grad_query, cosine, -sine).astype(HALF)
    g_ref[:, col.key[0] : col.key[1]] = turned(key_grad[...], cos_ref[...], -sin_ref[...]).astype(HALF)
    g_ref[:, col.value[0] : col.value[1]] = value_grad[...].astype(HALF)


def attend_backward(col, heads, packed, attended, lse, grad_attended, tables, segments, grads):
    length = packed.shape[0]
    width = heads * ATT_DIM
    whole = lambda i: (0, 0)
    return pl.pallas_call(
        functools.partial(attend_backward_kernel, col, heads),
        grid=(1,),
        in_specs=[
            pl.BlockSpec((length, col.attention), whole),
            pl.BlockSpec((length, width), whole),
            pl.BlockSpec((length, width), whole),
            pl.BlockSpec((length, width), whole),
            pl.BlockSpec((length, ATT_DIM), whole),
            pl.BlockSpec((length, ATT_DIM), whole),
            pl.BlockSpec((length, 1), whole),
            pl.BlockSpec((1, length), whole),
            pl.BlockSpec(memory_space=pl.ANY),
        ],
        out_specs=pl.BlockSpec((length, col.attention), whole),
        out_shape=jax.ShapeDtypeStruct(grads.shape, grads.dtype),
        scratch_shapes=[pltpu.VMEM((length, ATT_DIM), FULL), pltpu.VMEM((length, ATT_DIM), FULL)],
        input_output_aliases={8: 0},
        cost_estimate=pl.CostEstimate(flops=5_000_000_000, bytes_accessed=10_000_000, transcendentals=2_000_000),
        compiler_params=pltpu.CompilerParams(vmem_limit_bytes=48 * 2**20),
    )(
        packed, attended, lse, grad_attended, tables[0], tables[1], segments[:, None], segments[None, :], grads
    )


def rope_tables(length):
    half = ATT_DIM // 2
    positions = jnp.arange(length, dtype=FULL)
    frequency = ROPE_BASE ** (-jnp.arange(half, dtype=FULL) / half)
    angles = positions[:, None] * frequency[None, :]
    cosine, sine = jnp.cos(angles), jnp.sin(angles)
    return jnp.concatenate([cosine, cosine], 1), jnp.concatenate([-sine, sine], 1)


MESH = pl.DeviceIdType.MESH
TILE = 256


class Line:
    def __init__(self, count):
        self.count = count
        self.me = lax.axis_index("tensor")
        self.has_left = self.me > 0
        self.has_right = self.me < count - 1

    def greet(self):
        barrier = pltpu.get_barrier_semaphore()
        for present, shift in ((self.has_left, -1), (self.has_right, 1)):

            @pl.when(present)
            def _():
                pl.semaphore_signal(
                    barrier, inc=1, device_id={"tensor": self.me + shift}, device_id_type=MESH
                )

        inside = self.has_left & self.has_right

        @pl.when(inside)
        def _():
            pl.semaphore_wait(barrier, 2)

        @pl.when(jnp.logical_not(inside))
        def _():
            pl.semaphore_wait(barrier, 1)

    def copy(self, source, target, sends, receives, at, side):
        return pltpu.make_async_remote_copy(
            src_ref=source,
            dst_ref=target,
            send_sem=sends.at[at],
            recv_sem=receives.at[at],
            device_id={"tensor": self.me + (1 if side == 0 else -1)},
            device_id_type=MESH,
        )

    def place(self, side):
        return self.me if side == 0 else self.count - 1 - self.me

    def ahead(self, side, distance):
        return self.me + distance if side == 0 else self.me - distance

    def next_there(self, side):
        return self.has_right if side == 0 else self.has_left

    def last_there(self, side):
        return self.has_left if side == 0 else self.has_right


class Scatter:
    def __init__(self, line, parts, rows, span, slots, sends, receives):
        self.line, self.parts, self.rows, self.span = line, parts, rows, span
        self.slots, self.sends, self.receives = slots, sends, receives

    def own(self, owner, chunk):
        return self.parts[pl.ds(pl.multiple_of(owner * self.rows + chunk * self.span, 16), self.span), :]

    def transfer(self, side, chunk, hop):
        return self.line.copy(
            self.slots.at[side, chunk, hop - 1],
            self.slots.at[side, chunk, hop],
            self.sends,
            self.receives,
            (side, chunk, hop - 1),
            side,
        )

    def hop(self, chunk, hop):
        line = self.line
        for side in (0, 1):
            place = line.place(side)
            slot = self.slots.at[side, chunk, hop - 1]
            owner = line.ahead(side, line.count - hop)

            @pl.when(place == 0)
            def _():
                slot[...] = self.own(owner, chunk).astype(slot.dtype)

            if hop > 1:

                @pl.when((place > 0) & (place <= hop - 1))
                def _():
                    self.transfer(side, chunk, hop - 1).wait_recv()
                    slot[...] = (slot[...].astype(FULL) + self.own(owner, chunk)).astype(slot.dtype)

            @pl.when(place <= hop - 1)
            def _():
                self.transfer(side, chunk, hop).start()

    def finish(self, chunk, total):
        line = self.line
        total[...] = self.own(line.me, chunk)
        last = line.count - 1
        for side in (0, 1):

            @pl.when(line.last_there(side))
            def _():
                self.transfer(side, chunk, last).wait_recv()
                total[...] += self.slots[side, chunk, last].astype(FULL)

    def drain(self, chunk):
        for hop in range(1, self.line.count):
            for side in (0, 1):

                @pl.when(self.line.place(side) <= hop - 1)
                def _():
                    self.transfer(side, chunk, hop).wait_send()


class Gather:
    def __init__(self, line, whole, rows, span, sends, receives):
        self.line, self.whole, self.rows, self.span = line, whole, rows, span
        self.sends, self.receives = sends, receives

    def at(self, owner, chunk):
        return self.whole.at[pl.ds(pl.multiple_of(owner * self.rows + chunk * self.span, 16), self.span), :]

    def transfer(self, side, chunk, hop):
        piece = self.at(self.line.ahead(1 - side, hop - 1), chunk)
        return self.line.copy(piece, piece, self.sends, self.receives, (side, chunk, hop - 1), side)

    def arrival(self, side, chunk, hop):
        piece = self.at(self.line.ahead(1 - side, hop), chunk)
        return self.line.copy(piece, piece, self.sends, self.receives, (side, chunk, hop - 1), side)

    def send(self, chunk, hop):
        line = self.line
        for side in (0, 1):

            @pl.when(line.next_there(side) & (line.place(side) >= hop - 1))
            def _():
                self.transfer(side, chunk, hop).start()

    def receive(self, chunk, hop):
        line = self.line
        for side in (0, 1):

            @pl.when(line.place(side) >= hop)
            def _():
                self.arrival(side, chunk, hop).wait_recv()

    def step(self, chunk, hop):
        line = self.line
        for side in (0, 1):

            @pl.when(line.place(side) >= hop)
            def _():
                self.arrival(side, chunk, hop).wait_recv()

            if hop < line.count - 1:

                @pl.when(line.next_there(side) & (line.place(side) >= hop))
                def _():
                    self.transfer(side, chunk, hop + 1).start()

    def drain(self, chunk):
        line = self.line
        for hop in range(1, line.count):
            for side in (0, 1):

                @pl.when(line.next_there(side) & (line.place(side) >= hop - 1))
                def _():
                    self.transfer(side, chunk, hop).wait_send()


def project(line, left, right, parts, rows, forward, block):
    owner = jnp.where(line.me < line.count // 2, line.count - 1 - block, block)
    at = pl.ds(pl.multiple_of(owner * rows, 16), rows)

    def tile(index, carry):
        lanes = pl.ds(pl.multiple_of(index * TILE, TILE), TILE)
        if forward:
            parts[at, lanes] = mm(left[at, :], right[:, lanes])
        else:
            parts[at, lanes] = mm_nt(left[at, :], right[lanes, :])
        return carry

    lax.fori_loop(0, parts.shape[1] // TILE, tile, 0)


def relay(line, scatter, gather, chunks, lag, work, rows_done):
    last = line.count - 1
    work(0)
    turns = lag * (chunks - 1) + last + 1 + (0 if gather is None else last)
    for turn in range(turns):
        for chunk in range(chunks):
            hop = turn - lag * chunk + 1
            if 1 <= hop <= last:
                scatter.hop(chunk, hop)
            elif hop == last + 1:
                rows_done(chunk)
                if gather is not None:
                    gather.send(chunk, 1)
            elif gather is not None and last + 1 < hop <= 2 * last + 1:
                gather.step(chunk, hop - last - 1)
        if turn == 0:
            lax.fori_loop(1, line.count, lambda block, carry: (work(block), carry)[1], 0)
    for chunk in range(chunks):
        scatter.drain(chunk)
        if gather is not None:
            gather.drain(chunk)


def norm_below(value, above, gain):
    inverse = lax.rsqrt(jnp.mean(value * value, -1, keepdims=True) + EPSILON)
    plain = value * inverse
    scaled = above * gain
    below = inverse * (scaled - plain * jnp.mean(scaled * plain, -1, keepdims=True))
    return below, jnp.sum(above * plain, 0, keepdims=True)


def mix_kernel(count, chunks, lag, rows, left, right, hidden, gain, out, middle, parts, total, slots, s0, s1, s2, s3):
    line = Line(count)
    span = rows // chunks
    line.greet()
    scatter = Scatter(line, parts, rows, span, slots, s0, s1)
    gather = Gather(line, out, rows, span, s2, s3)

    def rows_done(chunk):
        at = pl.ds(chunk * span, span)
        scatter.finish(chunk, total)
        value = total[...] + hidden[at, :].astype(FULL)
        middle[at, :] = value
        inverse = lax.rsqrt(jnp.mean(value * value, -1, keepdims=True) + EPSILON)
        gather.at(line.me, chunk)[...] = (value * inverse * gain[...]).astype(HALF)

    relay(line, scatter, gather, chunks, lag, functools.partial(project, line, left, right, parts, rows, True), rows_done)


def ffn_grad_kernel(count, chunks, lag, rows, left, right, middle, cotangent, gain, out, grad_middle, gain_grad, parts, total, slots, s0, s1, s2, s3):
    line = Line(count)
    span = rows // chunks
    line.greet()
    scatter = Scatter(line, parts, rows, span, slots, s0, s1)
    gather = Gather(line, out, rows, span, s2, s3)
    gain_grad[...] = jnp.zeros_like(gain_grad)

    def rows_done(chunk):
        at = pl.ds(chunk * span, span)
        scatter.finish(chunk, total)
        below, part = norm_below(middle[at, :], total[...], gain[...])
        gain_grad[...] += part
        result = cotangent[at, :].astype(FULL) + below
        grad_middle[at, :] = result
        gather.at(line.me, chunk)[...] = result.astype(HALF)

    relay(line, scatter, gather, chunks, lag, functools.partial(project, line, left, right, parts, rows, False), rows_done)


def relay_call(kernel, name, count, chunks, lag, collective, operands, rows, features, extra_out, flops):
    span = rows // chunks
    vmem = pl.BlockSpec(memory_space=pltpu.VMEM)
    hops = count - 1
    return pl.pallas_call(
        functools.partial(kernel, count, chunks, lag, rows),
        in_specs=[vmem] * len(operands),
        out_specs=[vmem] * (1 + len(extra_out)),
        out_shape=[jax.ShapeDtypeStruct((count * rows, features), HALF)] + extra_out,
        scratch_shapes=[
            pltpu.VMEM((count * rows, features), FULL),
            pltpu.VMEM((span, features), FULL),
            pltpu.VMEM((2, chunks, count, span, features), HALF),
        ]
        + [pltpu.SemaphoreType.DMA((2, chunks, hops))] * 4,
        name=name,
        cost_estimate=pl.CostEstimate(flops=flops, bytes_accessed=20_000_000, transcendentals=0),
        compiler_params=pltpu.CompilerParams(
            collective_id=collective, has_side_effects=True, vmem_limit_bytes=56 * 2**20
        ),
    )(*operands)


def mix_rows(count, chunks, lag, branches, weight_out, hidden, gain):
    rows, features = hidden.shape
    return relay_call(
        mix_kernel, "mix_rows", count, chunks, lag, 1, (branches, weight_out, hidden, gain), rows, features,
        [jax.ShapeDtypeStruct((rows, features), FULL)], 100_000_000_000,
    )


def ffn_grad_rows(count, chunks, lag, grad_gate, weight_up, middle, cotangent, gain):
    rows, features = middle.shape
    return relay_call(
        ffn_grad_kernel, "ffn_grad_rows", count, chunks, lag, 2, (grad_gate, weight_up, middle, cotangent, gain),
        rows, features,
        [jax.ShapeDtypeStruct((rows, features), FULL), jax.ShapeDtypeStruct((1, features), FULL)], 100_000_000_000,
    )


def gather_kernel(count, rows, own, out, own_sem, s0, s1):
    line = Line(count)
    keep = pltpu.make_async_copy(own, out.at[pl.ds(pl.multiple_of(line.me * rows, 16), rows), :], own_sem)
    keep.start()
    line.greet()
    keep.wait()
    gather = Gather(line, out, rows, rows, s0, s1)
    gather.send(0, 1)
    for hop in range(1, count):
        gather.step(0, hop)
    gather.drain(0)


def line_gather(count, collective, own):
    rows, features = own.shape
    vmem = pl.BlockSpec(memory_space=pltpu.VMEM)
    return pl.pallas_call(
        functools.partial(gather_kernel, count, rows),
        in_specs=[vmem],
        out_specs=vmem,
        out_shape=jax.ShapeDtypeStruct((count * rows, features), own.dtype),
        scratch_shapes=[pltpu.SemaphoreType.DMA(())] + [pltpu.SemaphoreType.DMA((2, 1, count - 1))] * 2,
        name="line_gather",
        cost_estimate=pl.CostEstimate(flops=80_000_000_000, bytes_accessed=20_000_000, transcendentals=0),
        compiler_params=pltpu.CompilerParams(
            collective_id=collective, has_side_effects=True, vmem_limit_bytes=48 * 2**20
        ),
    )(own)


def input_grad_kernel(count, chunks, lag, rows, left, right, hidden, grad_middle, gain, out, gain_grad, parts, total, slots, s0, s1):
    line = Line(count)
    span = rows // chunks
    line.greet()
    scatter = Scatter(line, parts, rows, span, slots, s0, s1)
    gain_grad[...] = jnp.zeros_like(gain_grad)

    def rows_done(chunk):
        at = pl.ds(chunk * span, span)
        scatter.finish(chunk, total)
        value = hidden[at, :].astype(FULL)
        below, part = norm_below(value, total[...], gain[...])
        gain_grad[...] += part
        out[at, :] = grad_middle[at, :] + below

    relay(line, scatter, None, chunks, lag, functools.partial(project, line, left, right, parts, rows, False), rows_done)


def input_grad_rows(count, chunks, lag, grads, weight_in, hidden, grad_middle, gain):
    rows, features = hidden.shape
    span = rows // chunks
    vmem = pl.BlockSpec(memory_space=pltpu.VMEM)
    operands = (grads, weight_in, hidden, grad_middle, gain)
    return pl.pallas_call(
        functools.partial(input_grad_kernel, count, chunks, lag, rows),
        in_specs=[vmem] * len(operands),
        out_specs=[vmem] * 2,
        out_shape=[
            jax.ShapeDtypeStruct((rows, features), FULL),
            jax.ShapeDtypeStruct((1, features), FULL),
        ],
        scratch_shapes=[
            pltpu.VMEM((count * rows, features), FULL),
            pltpu.VMEM((span, features), FULL),
            pltpu.VMEM((2, chunks, count, span, features), HALF),
        ]
        + [pltpu.SemaphoreType.DMA((2, chunks, count - 1))] * 2,
        name="input_grad_rows",
        cost_estimate=pl.CostEstimate(flops=80_000_000_000, bytes_accessed=20_000_000, transcendentals=0),
        compiler_params=pltpu.CompilerParams(
            collective_id=3, has_side_effects=True, vmem_limit_bytes=56 * 2**20
        ),
    )(*operands)


CHUNKS = 4
LAG = 2


def gather_rows(pieces):
    return lax.all_gather(pieces, "tensor", axis=0, tiled=True)


def sum_rows(pieces):
    return lax.psum_scatter(pieces, "tensor", scatter_dimension=0, tiled=True).astype(FULL)


def norm_forward(values, gain_vals):
    inverse = lax.rsqrt(jnp.mean(values * values, -1, keepdims=True) + EPSILON)
    plain = values * inverse
    return plain, inverse, plain * gain_vals


def silu_parts(gate_input):
    sigmoid_vals = jax.nn.sigmoid(gate_input)
    return gate_input * sigmoid_vals, sigmoid_vals * (1.0 + gate_input * (1.0 - sigmoid_vals))


def dot_tn(a, b):
    return jnp.einsum("sa,sb->ab", a, b, preferred_element_type=FULL)


def dot_nt(a, b):
    return jnp.einsum("sb,ab->sa", a, b, preferred_element_type=FULL)


def body(
    hidden_in,
    segments,
    norm_gain,
    mamba_in,
    step_weight,
    state_weight,
    decay_log,
    step_bias,
    skip_gain,
    gated_gain,
    query_weight,
    keyval_weight,
    mamba_out,
    attn_out,
    ffn_gain,
    gate_up,
    down_weight,
    cotangent,
):
    tensor_index = lax.axis_index("tensor")
    count = lax.axis_size("tensor")
    heads = decay_log.shape[0]
    width = mamba_in.shape[2]
    state_size = state_weight.shape[2]
    query_width = query_weight.shape[1]
    qheads = query_width // ATT_DIM
    units = gate_up.shape[2]
    rows_local = hidden_in.shape[0]
    block = norm_gain.shape[0]
    group_size = ATT_HEADS // KV_HEADS
    kv_head = tensor_index * qheads // group_size
    col = Columns(query_width, width, state_size)

    own_keyval = lax.dynamic_slice_in_dim(keyval_weight, kv_head * ATT_DIM, ATT_DIM, 2)
    spare = LANES - heads - 2
    packed_in = jnp.concatenate(
        [
            query_weight,
            own_keyval[:, 0],
            own_keyval[:, 1],
            mamba_in[:, 0],
            mamba_in[:, 1],
            state_weight[:, 0],
            state_weight[:, 1],
            step_weight,
            jnp.zeros((block, spare), HALF),
            norm_gain[:, None],
            ffn_gain[:, None],
        ],
        1,
    )
    weight_in = lax.all_gather(packed_in, "dp", axis=0, tiled=True)
    hidden_rows = line_gather(count, 0, hidden_in)
    weight_out = lax.all_gather(jnp.concatenate([mamba_out, attn_out], 0), "dp", axis=1, tiled=True)
    weight_up = lax.all_gather(gate_up.reshape(block, 2 * units), "dp", axis=0, tiled=True)
    weight_down = lax.all_gather(down_weight, "dp", axis=1, tiled=True)
    grad_rows = gather_rows(cotangent)

    gain_one = weight_in[:, col.total - 2].astype(FULL)
    gain_two = weight_in[:, col.total - 1].astype(FULL)
    sequence = norm_forward(hidden_rows.astype(FULL), gain_one)[2].astype(HALF)
    length = sequence.shape[0]
    packed = jnp.dot(sequence, weight_in, preferred_element_type=FULL)
    head_params = jnp.pad(
        jnp.stack([decay_log, step_bias, skip_gain]), ((0, 5), (0, LANES - heads))
    )
    tables = rope_tables(length)

    scan_y, states, gated_vals, squares = scan_forward(
        col, heads, state_size, packed, segments, head_params
    )
    square_sum = lax.psum(squares[:, 0], "tensor")
    gated_inverse = lax.rsqrt(square_sum / (MAMBA_HEADS * HEAD_DIM) + EPSILON)[:, None]
    attended, lse = attend_forward(col, qheads, packed, tables, segments)
    gated_scale = gated_gain.astype(FULL)
    gated_plain = gated_vals * gated_inverse
    branches = jnp.concatenate([(gated_plain * gated_scale).astype(HALF), attended], 1)
    ffn_rows, middle = mix_rows(count, CHUNKS, LAG, branches, weight_out, hidden_in, gain_two[None, :])
    gate_vals = jnp.dot(ffn_rows, weight_up, preferred_element_type=FULL)
    gate_part, up_part = gate_vals[:, :units], gate_vals[:, units:]
    silu_gate, silu_slope = silu_parts(gate_part)
    activated = (silu_gate * up_part).astype(HALF)
    grad_act = dot_nt(grad_rows, weight_down)
    grad_gate = jnp.concatenate(
        [grad_act * up_part * silu_slope, grad_act * silu_gate], 1
    ).astype(HALF)
    up_grad = dot_tn(ffn_rows, grad_gate).astype(HALF)
    down_grad = dot_tn(activated, grad_rows).astype(HALF)
    grad_gate, up_grad, down_grad = lax.optimization_barrier((grad_gate, up_grad, down_grad))
    gate_share = lax.psum_scatter(up_grad, "dp", scatter_dimension=0, tiled=True)
    down_share = lax.psum_scatter(down_grad, "dp", scatter_dimension=1, tiled=True)
    grad_mixed, grad_middle, ffn_gain_part = ffn_grad_rows(
        count, CHUNKS, LAG, grad_gate, weight_up, middle, cotangent, gain_two[None, :]
    )
    ffn_out = sum_rows(jnp.dot(activated, weight_down))
    hidden_out = (middle + ffn_out).astype(HALF)

    grad_branches = dot_nt(grad_mixed, weight_out)
    out_grad = dot_tn(branches, grad_mixed).astype(HALF)
    out_share = lax.psum_scatter(out_grad, "dp", scatter_dimension=1, tiled=True)
    grad_mamba = grad_branches[:, :width]
    product_sum = lax.psum(jnp.sum(grad_mamba * gated_scale * gated_plain, -1), "tensor")[:, None]
    grads, gain_part, skip_part, head_part = scan_backward(
        col,
        heads,
        state_size,
        packed,
        scan_y,
        states,
        grad_mamba,
        gated_inverse,
        product_sum,
        gated_scale[None, :],
        segments,
        head_params,
    )
    grads = attend_backward(
        col, qheads, packed, attended, lse, grad_branches[:, width:], tables, segments, grads
    )
    in_grad = dot_tn(sequence, grads).astype(HALF)
    grads, in_grad = lax.optimization_barrier((grads, in_grad))
    in_share = lax.psum_scatter(in_grad, "dp", scatter_dimension=0, tiled=True)
    hidden_grad, norm_gain_part = input_grad_rows(
        count, 2, 1, grads, weight_in, hidden_in, grad_middle, gain_one[None, :]
    )

    keyval_part = jnp.stack(
        [in_share[:, slice(*col.key)], in_share[:, slice(*col.value)]], 1
    )
    keyval_grad = lax.dynamic_update_slice_in_dim(
        jnp.zeros(keyval_weight.shape, HALF), keyval_part, kv_head * ATT_DIM, 2
    ).reshape(block, -1)
    shared = lax.psum(
        jnp.concatenate([in_share[:, col.inmap[0] : col.outmap[1]], keyval_grad], 1), "tensor"
    ).astype(FULL)
    state_weight_grad = shared[:, : 2 * state_size].reshape(state_weight.shape)
    keyval_weight_grad = shared[:, 2 * state_size :].reshape(keyval_weight.shape)

    gains = lax.psum(jnp.concatenate([norm_gain_part, ffn_gain_part]), ("dp", "tensor"))
    dp_index = lax.axis_index("dp")
    gains = lax.dynamic_slice_in_dim(gains, dp_index * block, block, 1)
    head_sums = lax.psum(
        jnp.concatenate(
            [
                head_part[0, :heads],
                head_part[1, :heads],
                skip_part.reshape(heads, HEAD_DIM).sum(1),
                gain_part[0],
            ]
        ),
        "dp",
    )
    inner_grad = jnp.stack([in_share[:, slice(*col.gate)], in_share[:, slice(*col.drive)]], 1)
    return (
        hidden_out,
        hidden_grad,
        gains[0],
        inner_grad.astype(FULL),
        in_share[:, col.step[0] : col.step[0] + heads].astype(FULL),
        state_weight_grad,
        head_sums[:heads],
        head_sums[heads : 2 * heads],
        head_sums[2 * heads : 3 * heads],
        head_sums[3 * heads :],
        in_share[:, slice(*col.query)].astype(FULL),
        keyval_weight_grad,
        out_share[:width].astype(FULL),
        out_share[width:].astype(FULL),
        gains[1],
        gate_share.reshape(gate_up.shape).astype(FULL),
        down_share.astype(FULL),
    )


def solution(mesh):
    rows = P(("dp", "tensor"), None)
    weights_in = P("dp", None, "tensor")
    return jax.shard_map(
        body,
        mesh=mesh,
        in_specs=(
            rows,
            P("dp"),
            P("dp"),
            weights_in,
            P("dp", "tensor"),
            P("dp", None, None),
            P("tensor"),
            P("tensor"),
            P("tensor"),
            P("tensor"),
            P("dp", "tensor"),
            P("dp", None, None),
            P("tensor", "dp"),
            P("tensor", "dp"),
            P("dp"),
            weights_in,
            P("tensor", "dp"),
            rows,
        ),
        out_specs=(
            rows,
            rows,
            P("dp"),
            weights_in,
            P("dp", "tensor"),
            P("dp", None, None),
            P("tensor"),
            P("tensor"),
            P("tensor"),
            P("tensor"),
            P("dp", "tensor"),
            P("dp", None, None),
            P("tensor", "dp"),
            P("tensor", "dp"),
            P("dp"),
            weights_in,
            P("tensor", "dp"),
        ),
        check_vma=False,
    )
```

```python
import functools
import math
import jax
import jax.numpy as jnp
from jax import lax
from jax.experimental import pallas as pl
from jax.experimental.pallas import tpu as pltpu
from jax.sharding import PartitionSpec as P

MAMBA_HEADS = 48
HEAD_DIM = 64
ATT_HEADS = 8
KV_HEADS = 2
ATT_DIM = 128
STRETCH = 128
ATT_BLOCK = 256
EPSILON = 1e-05
PRECISE = lax.Precision.HIGHEST
ROPE_BASE = 10000.0
LANES = 128
MASKED = -1e30
HALF = jnp.bfloat16
FULL = jnp.float32


def mm(a, b):
    return jnp.dot(a, b, preferred_element_type=FULL)


def mm_nt(a, b):
    return lax.dot_general(a, b, (((1,), (1,)), ((), ())), preferred_element_type=FULL)


def mm_tn(a, b):
    return lax.dot_general(a, b, (((0,), (0,)), ((), ())), preferred_element_type=FULL)


def softplus(v):
    return jnp.maximum(v, 0.0) + jnp.log1p(jnp.exp(-jnp.abs(v)))


def sigmoid(v):
    return 1.0 / (1.0 + jnp.exp(-v))


def iota(shape, dim):
    return lax.broadcasted_iota(jnp.int32, shape, dim)


def halves(left, right, size):
    return jnp.where(iota((size, LANES), 1) < HEAD_DIM, left, right)


def as_row(values):
    return jnp.broadcast_to(values, (LANES, LANES)).T[0:1, :]


def as_column(values):
    return jnp.broadcast_to(values, (LANES, LANES)).T[:, 0:1]


def stacked_pair(pair):
    low = iota(pair.shape, 1) < HEAD_DIM
    zero = jnp.zeros_like(pair)
    return jnp.concatenate([jnp.where(low, pair, zero), jnp.where(low, zero, pair)], 0)


class Columns:
    def __init__(self, query, width, state):
        self.query = (0, query)
        self.key = (query, query + ATT_DIM)
        self.value = (query + ATT_DIM, query + 2 * ATT_DIM)
        start = query + 2 * ATT_DIM
        self.attention = start
        self.gate = (start, start + width)
        self.drive = (start + width, start + 2 * width)
        start += 2 * width
        self.inmap = (start, start + state)
        self.outmap = (start + state, start + 2 * state)
        start += 2 * state
        self.step = (start, start + LANES)
        self.total = start + 2 * LANES


def stretch_common(col, packed, segc_ref, segr_ref, head_ref, before):
    span = STRETCH
    raw = packed[:, col.step[0] : col.step[1]] + head_ref[1:2, :]
    step = softplus(raw)
    keep = -jnp.exp(head_ref[0:1, :]) * step
    row, column = iota((span, span), 0), iota((span, span), 1)
    running = jnp.dot(
        (row >= column).astype(FULL), keep, precision=PRECISE, preferred_element_type=FULL
    )
    segc, segr = segc_ref[...], segr_ref[0]
    causal = (row >= column) & (segc == segr)
    blocked = jnp.where(causal, 0.0, MASKED)
    live = (segc == before).astype(FULL)
    last = segc[span - 1 : span, :]
    tail = (segc == last).astype(FULL)
    old = (last == before).astype(FULL)
    return raw, step, keep, running, running.T, blocked, live, tail, old


def pair_decay(pair, running, running_t, blocked, live, tail, old):
    span = STRETCH
    a, b = 2 * pair, 2 * pair + 1
    col_a = jnp.broadcast_to(running[:, a : a + 1], (span, LANES))
    col_b = jnp.broadcast_to(running[:, b : b + 1], (span, LANES))
    decay_a = jnp.exp(col_a - running_t[a : a + 1, :] + blocked)
    decay_b = jnp.exp(col_b - running_t[b : b + 1, :] + blocked)
    both = halves(col_a, col_b, span)
    last = both[span - 1 : span, :]
    into = jnp.exp(both) * live
    weight = jnp.exp(last - both) * tail
    keep_old = jnp.exp(last) * old
    return decay_a, decay_b, into, weight, keep_old


def scan_forward_kernel(col, heads, p_ref, segc_ref, segr_ref, head_ref, y_ref, states_ref, gated_ref, square_ref, state, before):
    index = pl.program_id(0)
    span = STRETCH

    @pl.when(index == 0)
    def _():
        state[...] = jnp.zeros_like(state)
        before[...] = jnp.full_like(before, -1)

    raw, step, keep, running, running_t, blocked, live, tail, old = stretch_common(
        col, p_ref, segc_ref, segr_ref, head_ref, before[...]
    )
    inmap = p_ref[:, col.inmap[0] : col.inmap[1]].astype(HALF)
    outmap = p_ref[:, col.outmap[0] : col.outmap[1]].astype(HALF)
    inmap_t = inmap.T
    scores = mm_nt(outmap, inmap)
    square = jnp.zeros((span, 1), FULL)
    for pair in range(heads // 2):
        at = pair * LANES
        lanes = slice(at, at + LANES)
        decay_a, decay_b, into, weight, keep_old = pair_decay(
            pair, running, running_t, blocked, live, tail, old
        )
        drive = p_ref[:, col.drive[0] + at : col.drive[0] + at + LANES]
        gate = p_ref[:, col.gate[0] + at : col.gate[0] + at + LANES]
        driven = drive * halves(step[:, 2 * pair : 2 * pair + 1], step[:, 2 * pair + 1 : 2 * pair + 2], span)
        driven_low = driven.astype(HALF)
        mix = jnp.concatenate([(decay_a * scores).astype(HALF), (decay_b * scores).astype(HALF)], 1)
        held = state[:, lanes]
        held_low = held.astype(HALF)
        states_ref[0, :, lanes] = held_low
        result = mm(mix, stacked_pair(driven_low)) + mm(outmap, held_low) * into
        state[:, lanes] = held * keep_old + mm(inmap_t, (driven_low.astype(FULL) * weight).astype(HALF))
        y_ref[:, lanes] = result
        skip = halves(head_ref[2:3, 2 * pair : 2 * pair + 1], head_ref[2:3, 2 * pair + 1 : 2 * pair + 2], 1)
        gated = (result + skip * drive) * (gate * sigmoid(gate))
        gated_ref[:, lanes] = gated
        square = square + jnp.sum(gated * gated, 1, keepdims=True)
    square_ref[pl.ds(index, 1), :] = as_row(square)
    before[...] = segc_ref[span - 1 : span, :]


def scan_forward(col, heads, state_size, packed, segments, head_params):
    length = packed.shape[0]
    width = heads * HEAD_DIM
    count = length // STRETCH
    return pl.pallas_call(
        functools.partial(scan_forward_kernel, col, heads),
        grid=(count,),
        in_specs=[
            pl.BlockSpec((STRETCH, col.total), lambda i: (i, 0)),
            pl.BlockSpec((STRETCH, 1), lambda i: (i, 0)),
            pl.BlockSpec((1, 1, STRETCH), lambda i: (i, 0, 0)),
            pl.BlockSpec((8, LANES), lambda i: (0, 0)),
        ],
        out_specs=[
            pl.BlockSpec((STRETCH, width), lambda i: (i, 0)),
            pl.BlockSpec((1, state_size, width), lambda i: (i, 0, 0)),
            pl.BlockSpec((STRETCH, width), lambda i: (i, 0)),
            pl.BlockSpec((count, LANES), lambda i: (0, 0)),
        ],
        out_shape=[
            jax.ShapeDtypeStruct((length, width), FULL),
            jax.ShapeDtypeStruct((count, state_size, width), HALF),
            jax.ShapeDtypeStruct((length, width), FULL),
            jax.ShapeDtypeStruct((count, LANES), FULL),
        ],
        scratch_shapes=[pltpu.VMEM((state_size, width), FULL), pltpu.VMEM((1, 1), jnp.int32)],
        name="scan_forward",
        cost_estimate=pl.CostEstimate(flops=16_000_000_000, bytes_accessed=30_000_000, transcendentals=0),
        compiler_params=pltpu.CompilerParams(vmem_limit_bytes=48 * 2**20),
    )(packed, segments[:, None], segments.reshape(count, 1, STRETCH), head_params)


def scan_backward_kernel(
    col, heads, total_width, p_ref, y_ref, states_ref, gm_ref, inv_ref, prod_ref, gain_ref,
    segc_ref, segr_ref, segb_ref, head_ref, ag_ref, g_ref, gain_grad_ref, skip_grad_ref, head_grad_ref, future,
):
    step_index = pl.program_id(0)
    count = pl.num_programs(0)
    span = STRETCH

    @pl.when(step_index == 0)
    def _():
        future[...] = jnp.zeros_like(future)
        gain_grad_ref[...] = jnp.zeros_like(gain_grad_ref)
        skip_grad_ref[...] = jnp.zeros_like(skip_grad_ref)
        head_grad_ref[...] = jnp.zeros_like(head_grad_ref)

    before = jnp.where(step_index == count - 1, -1, segb_ref[span - 1 : span, :])
    raw, step, keep, running, running_t, blocked, live, tail, old = stretch_common(
        col, p_ref, segc_ref, segr_ref, head_ref, before
    )
    inmap = p_ref[:, col.inmap[0] : col.inmap[1]].astype(HALF)
    outmap = p_ref[:, col.outmap[0] : col.outmap[1]].astype(HALF)
    outmap_t = outmap.T
    scores = mm_nt(outmap, inmap)
    lane = iota((span, LANES), 1)
    head_lane = iota((1, LANES), 1)
    paired = jnp.zeros((span, span), FULL)
    grad_in = jnp.zeros(inmap.shape, FULL)
    grad_out = jnp.zeros(outmap.shape, FULL)
    grad_running = jnp.zeros((span, LANES), FULL)
    grad_step = jnp.zeros((span, LANES), FULL)
    grad_last = jnp.zeros((1, LANES), FULL)
    chunk = pl.ds(count - 1 - step_index, 1)
    inverse = as_column(lax.rsqrt(inv_ref[chunk, :] * (1.0 / total_width) + EPSILON))
    product = as_column(prod_ref[chunk, :] * (1.0 / total_width))
    for pair in range(heads // 2):
        at = pair * LANES
        lanes = slice(at, at + LANES)
        a, b = 2 * pair, 2 * pair + 1
        decay_a, decay_b, into, weight, keep_old = pair_decay(
            pair, running, running_t, blocked, live, tail, old
        )
        drive = p_ref[:, col.drive[0] + at : col.drive[0] + at + LANES]
        gate = p_ref[:, col.gate[0] + at : col.gate[0] + at + LANES]
        result = y_ref[:, lanes]
        skip = halves(head_ref[2:3, a : a + 1], head_ref[2:3, b : b + 1], 1)
        sig = sigmoid(gate)
        silu = gate * sig
        ssm = result + skip * drive
        plain = ssm * silu * inverse
        grad_above = gm_ref[:, lanes].astype(FULL)
        gain_grad_ref[:, lanes] += jnp.sum(grad_above * plain, 0, keepdims=True)
        grad_gated = inverse * (grad_above * gain_ref[:, lanes] - plain * product)
        g_ref[:, col.gate[0] + at : col.gate[0] + at + LANES] = (
            grad_gated * ssm * (sig * (1.0 + gate * (1.0 - sig)))
        ).astype(HALF)
        grad_y = grad_gated * silu
        grad_y_low = grad_y.astype(HALF)
        grad_y = grad_y_low.astype(FULL)
        step_pair = halves(step[:, a : a + 1], step[:, b : b + 1], span)
        driven_low = (drive * step_pair).astype(HALF)
        driven = driven_low.astype(FULL)
        grad_rows = stacked_pair(grad_y_low)
        inner = mm_nt(grad_rows, driven_low)
        paired = paired + decay_a * inner[:span] + decay_b * inner[span:]
        mix = jnp.concatenate([(decay_a * scores).astype(HALF), (decay_b * scores).astype(HALF)], 0)
        later = future[:, lanes]
        later_low = later.astype(HALF)
        held_low = states_ref[0, :, lanes]
        reach = mm(inmap, later_low) * weight
        grad_driven = mm_tn(mix, grad_rows) + reach
        weighted = (driven * weight).astype(HALF)
        spread = (grad_y * into).astype(HALF)
        grad_in = grad_in + mm_nt(weighted, later_low)
        grad_out = grad_out + mm_nt(spread, held_low)
        future[:, lanes] = later * keep_old + mm(outmap_t, spread)
        g_ref[:, col.drive[0] + at : col.drive[0] + at + LANES] = (
            step_pair * grad_driven + skip * grad_y
        ).astype(HALF)
        skip_grad_ref[:, lanes] += jnp.sum(grad_y * drive, 0, keepdims=True)
        turn = grad_y * result - driven * grad_driven
        left = lane < HEAD_DIM
        from_drive = drive * grad_driven
        ends = jnp.sum(driven * reach, 0, keepdims=True) + keep_old * jnp.sum(
            later * held_low.astype(FULL), 0, keepdims=True
        )
        for head, mask in ((a, left), (b, ~left)):
            grad_running = grad_running + jnp.where(
                lane == head, jnp.sum(jnp.where(mask, turn, 0.0), 1, keepdims=True), 0.0
            )
            grad_step = grad_step + jnp.where(
                lane == head, jnp.sum(jnp.where(mask, from_drive, 0.0), 1, keepdims=True), 0.0
            )
            grad_last = grad_last + jnp.where(
                head_lane == head, jnp.sum(jnp.where(mask[0:1], ends, 0.0), 1, keepdims=True), 0.0
            )
    paired = paired.astype(HALF)
    grad_out = grad_out + mm(paired, inmap)
    grad_in = grad_in + mm_tn(paired, outmap)
    g_ref[:, col.inmap[0] : col.inmap[1]] = grad_in.astype(HALF)
    g_ref[:, col.outmap[0] : col.outmap[1]] = grad_out.astype(HALF)
    row, column = iota((span, span), 0), iota((span, span), 1)
    grad_keep = (
        jnp.dot((row <= column).astype(FULL), grad_running, precision=PRECISE, preferred_element_type=FULL)
        + grad_last
    )
    grad_raw = (grad_step - grad_keep * jnp.exp(head_ref[0:1, :])) * sigmoid(raw)
    grad_raw = jnp.where(lane < heads, grad_raw, 0.0)
    g_ref[:, col.step[0] : col.step[1]] = grad_raw.astype(HALF)
    g_ref[:, col.step[1] : col.total] = jnp.zeros((span, col.total - col.step[1]), HALF)
    g_ref[:, 0 : col.attention] = ag_ref[...]
    head_grad_ref[0:1, :] += jnp.sum(keep * grad_keep, 0, keepdims=True)
    head_grad_ref[1:2, :] += jnp.sum(grad_raw, 0, keepdims=True)


def scan_backward(
    col, heads, state_size, packed, y, states, grad_mamba, squares, product, gain, segments, head_params, attention_grads
):
    length = packed.shape[0]
    width = heads * HEAD_DIM
    count = length // STRETCH
    back = lambda i: (count - 1 - i, 0)
    return pl.pallas_call(
        functools.partial(scan_backward_kernel, col, heads, MAMBA_HEADS * HEAD_DIM),
        grid=(count,),
        in_specs=[
            pl.BlockSpec((STRETCH, col.total), back),
            pl.BlockSpec((STRETCH, width), back),
            pl.BlockSpec((1, state_size, width), lambda i: (count - 1 - i, 0, 0)),
            pl.BlockSpec((STRETCH, width), back),
            pl.BlockSpec((count, LANES), lambda i: (0, 0)),
            pl.BlockSpec((count, LANES), lambda i: (0, 0)),
            pl.BlockSpec((1, width), lambda i: (0, 0)),
            pl.BlockSpec((STRETCH, 1), back),
            pl.BlockSpec((1, 1, STRETCH), lambda i: (count - 1 - i, 0, 0)),
            pl.BlockSpec((STRETCH, 1), lambda i: (jnp.maximum(count - 2 - i, 0), 0)),
            pl.BlockSpec((8, LANES), lambda i: (0, 0)),
            pl.BlockSpec((STRETCH, col.attention), back),
        ],
        out_specs=[
            pl.BlockSpec((STRETCH, col.total), back),
            pl.BlockSpec((1, width), lambda i: (0, 0)),
            pl.BlockSpec((1, width), lambda i: (0, 0)),
            pl.BlockSpec((8, LANES), lambda i: (0, 0)),
        ],
        out_shape=[
            jax.ShapeDtypeStruct((length, col.total), HALF),
            jax.ShapeDtypeStruct((1, width), FULL),
            jax.ShapeDtypeStruct((1, width), FULL),
            jax.ShapeDtypeStruct((8, LANES), FULL),
        ],
        scratch_shapes=[pltpu.VMEM((state_size, width), FULL)],
        name="scan_backward",
        cost_estimate=pl.CostEstimate(flops=24_000_000_000, bytes_accessed=40_000_000, transcendentals=0),
        compiler_params=pltpu.CompilerParams(vmem_limit_bytes=48 * 2**20),
    )(
        packed, y, states, grad_mamba, squares, product, gain, segments[:, None],
        segments.reshape(count, 1, STRETCH), segments[:, None], head_params, attention_grads,
    )


def turned(values, cosine, sine):
    return values * cosine + pltpu.roll(values, ATT_DIM // 2, 1) * sine


def attend_forward_kernel(
    col, heads, peers, p_ref, cos_ref, sin_ref, segc_ref, segr_ref, own_ref, out_ref, lse_ref, sum_ref, held, sends, receives
):
    length = p_ref.shape[0]
    finish = spread(peers, own_ref, held, sends, receives)
    scale = 1.0 / math.sqrt(ATT_DIM)
    keys = turned(p_ref[:, col.key[0] : col.key[1]], cos_ref[...], sin_ref[...]).astype(HALF)
    values = p_ref[:, col.value[0] : col.value[1]].astype(HALF)
    for block in range(length // ATT_BLOCK):
        rows = slice(block * ATT_BLOCK, (block + 1) * ATT_BLOCK)
        end = (block + 1) * ATT_BLOCK
        place = iota((ATT_BLOCK, end), 0) + block * ATT_BLOCK
        allowed = (place >= iota((ATT_BLOCK, end), 1)) & (segc_ref[rows, :] == segr_ref[:, :end])
        blocked = jnp.where(allowed, 0.0, MASKED)
        for head in range(heads):
            lanes = slice(head * ATT_DIM, (head + 1) * ATT_DIM)
            query = (turned(p_ref[rows, lanes], cos_ref[rows, :], sin_ref[rows, :]) * scale).astype(HALF)
            scores = mm_nt(query, keys[:end]) + blocked
            highest = jnp.max(scores, 1, keepdims=True)
            weights = jnp.exp(scores - highest)
            total = jnp.sum(weights, 1, keepdims=True)
            out_ref[rows, lanes] = (mm(weights.astype(HALF), values[:end]) / total).astype(HALF)
            lse_ref[rows, lanes] = jnp.broadcast_to(highest + jnp.log(total), (ATT_BLOCK, ATT_DIM))
    finish(sum_ref)


def exchange_scratch(peers, shape):
    return [
        pltpu.VMEM((peers,) + shape, FULL),
        pltpu.SemaphoreType.DMA((peers,)),
        pltpu.SemaphoreType.DMA((peers,)),
    ]


def spread(peers, own_ref, held, sends, receives):
    me = lax.axis_index("tensor")
    barrier = pltpu.get_barrier_semaphore()
    others = [lax.rem(me + distance, peers) for distance in range(1, peers)]
    for other in others:
        pl.semaphore_signal(barrier, inc=1, device_id={"tensor": other}, device_id_type=pl.DeviceIdType.MESH)
    pl.semaphore_wait(barrier, peers - 1)

    def copy(distance):
        return pltpu.make_async_remote_copy(
            src_ref=own_ref,
            dst_ref=held.at[distance],
            send_sem=sends.at[distance],
            recv_sem=receives.at[distance],
            device_id={"tensor": others[distance - 1]},
            device_id_type=pl.DeviceIdType.MESH,
        )

    for distance in range(1, peers):
        copy(distance).start()

    def finish(sum_ref):
        sum_ref[...] = own_ref[...]
        for distance in range(1, peers):
            copy(distance).wait()
            sum_ref[...] += held[distance]

    return finish


def attend_forward(col, heads, peers, packed, tables, segments, own):
    length = packed.shape[0]
    whole = lambda i: (0, 0)
    return pl.pallas_call(
        functools.partial(attend_forward_kernel, col, heads, peers),
        grid=(1,),
        in_specs=[
            pl.BlockSpec((length, col.attention), whole),
            pl.BlockSpec((length, ATT_DIM), whole),
            pl.BlockSpec((length, ATT_DIM), whole),
            pl.BlockSpec((length, 1), whole),
            pl.BlockSpec((1, length), whole),
            pl.BlockSpec(own.shape, whole),
        ],
        out_specs=[
            pl.BlockSpec((length, heads * ATT_DIM), whole),
            pl.BlockSpec((length, heads * ATT_DIM), whole),
            pl.BlockSpec(own.shape, whole),
        ],
        out_shape=[
            jax.ShapeDtypeStruct((length, heads * ATT_DIM), HALF),
            jax.ShapeDtypeStruct((length, heads * ATT_DIM), FULL),
            jax.ShapeDtypeStruct(own.shape, FULL),
        ],
        scratch_shapes=exchange_scratch(peers, own.shape),
        name="attend_forward",
        cost_estimate=pl.CostEstimate(flops=6_000_000_000, bytes_accessed=5_000_000, transcendentals=2_000_000),
        compiler_params=pltpu.CompilerParams(
            vmem_limit_bytes=48 * 2**20, collective_id=4, has_side_effects=True
        ),
    )(packed, tables[0], tables[1], segments[:, None], segments[None, :], own)


def attend_backward_kernel(
    col, heads, peers, p_ref, out_ref, lse_ref, go_ref, cos_ref, sin_ref, segc_ref, segr_ref, own_ref, g_ref, sum_ref,
    key_grad, value_grad, held, sends, receives,
):
    length = p_ref.shape[0]
    finish = spread(peers, own_ref, held, sends, receives)
    scale = 1.0 / math.sqrt(ATT_DIM)
    keys = turned(p_ref[:, col.key[0] : col.key[1]], cos_ref[...], sin_ref[...]).astype(HALF)
    values = p_ref[:, col.value[0] : col.value[1]].astype(HALF)
    key_grad[...] = jnp.zeros_like(key_grad)
    value_grad[...] = jnp.zeros_like(value_grad)
    for block in range(length // ATT_BLOCK):
        rows = slice(block * ATT_BLOCK, (block + 1) * ATT_BLOCK)
        end = (block + 1) * ATT_BLOCK
        place = iota((ATT_BLOCK, end), 0) + block * ATT_BLOCK
        allowed = (place >= iota((ATT_BLOCK, end), 1)) & (segc_ref[rows, :] == segr_ref[:, :end])
        blocked = jnp.where(allowed, 0.0, MASKED)
        cosine, sine = cos_ref[rows, :], sin_ref[rows, :]
        for head in range(heads):
            lanes = slice(head * ATT_DIM, (head + 1) * ATT_DIM)
            query = (turned(p_ref[rows, lanes], cosine, sine) * scale).astype(HALF)
            weights = jnp.exp(mm_nt(query, keys[:end]) + blocked - lse_ref[rows, lanes][:, 0:1])
            grad_low = go_ref[rows, lanes].astype(HALF)
            delta = jnp.sum(grad_low.astype(FULL) * out_ref[rows, lanes].astype(FULL), 1, keepdims=True)
            grad_scores = (weights * (mm_nt(grad_low, values[:end]) - delta)).astype(HALF)
            value_grad[:end, :] += mm_tn(weights.astype(HALF), grad_low)
            key_grad[:end, :] += mm_tn(grad_scores, query)
            grad_query = mm(grad_scores, keys[:end]) * scale
            g_ref[rows, lanes] = turned(grad_query, cosine, -sine).astype(HALF)
    g_ref[:, col.key[0] : col.key[1]] = turned(key_grad[...], cos_ref[...], -sin_ref[...]).astype(HALF)
    g_ref[:, col.value[0] : col.value[1]] = value_grad[...].astype(HALF)
    finish(sum_ref)


def attend_backward(col, heads, peers, packed, attended, lse, grad_branches, tables, segments, own):
    length = packed.shape[0]
    width = heads * ATT_DIM
    whole = lambda i: (0, 0)
    return pl.pallas_call(
        functools.partial(attend_backward_kernel, col, heads, peers),
        grid=(1,),
        in_specs=[
            pl.BlockSpec((length, col.attention), whole),
            pl.BlockSpec((length, width), whole),
            pl.BlockSpec((length, width), whole),
            pl.BlockSpec((length, width), lambda i: (0, grad_branches.shape[1] // width - 1)),
            pl.BlockSpec((length, ATT_DIM), whole),
            pl.BlockSpec((length, ATT_DIM), whole),
            pl.BlockSpec((length, 1), whole),
            pl.BlockSpec((1, length), whole),
            pl.BlockSpec(own.shape, whole),
        ],
        out_specs=[pl.BlockSpec((length, col.attention), whole), pl.BlockSpec(own.shape, whole)],
        out_shape=[
            jax.ShapeDtypeStruct((length, col.attention), HALF),
            jax.ShapeDtypeStruct(own.shape, FULL),
        ],
        scratch_shapes=[pltpu.VMEM((length, ATT_DIM), FULL), pltpu.VMEM((length, ATT_DIM), FULL)]
        + exchange_scratch(peers, own.shape),
        name="attend_backward",
        cost_estimate=pl.CostEstimate(flops=8_000_000_000, bytes_accessed=10_000_000, transcendentals=2_000_000),
        compiler_params=pltpu.CompilerParams(
            vmem_limit_bytes=48 * 2**20, collective_id=5, has_side_effects=True
        ),
    )(
        packed, attended, lse, grad_branches, tables[0], tables[1], segments[:, None], segments[None, :], own
    )


def rope_tables(length):
    half = ATT_DIM // 2
    positions = jnp.arange(length, dtype=FULL)
    frequency = ROPE_BASE ** (-jnp.arange(half, dtype=FULL) / half)
    angles = positions[:, None] * frequency[None, :]
    cosine, sine = jnp.cos(angles), jnp.sin(angles)
    return jnp.concatenate([cosine, cosine], 1), jnp.concatenate([-sine, sine], 1)


def weight_grads_kernel(first, left_one, left_two, right_one, right_two, out):
    index = pl.program_id(0)

    @pl.when(index < first)
    def _():
        out[...] = mm_tn(left_one[...], right_one[...]).astype(out.dtype)

    @pl.when(index >= first)
    def _():
        out[...] = mm_tn(left_two[...], right_two[...]).astype(out.dtype)


def weight_grads(left_one, right_one, left_two, right_two, name):
    length, features = left_one.shape
    one, two = right_one.shape[1], right_two.shape[1]
    tile = max(size for size in (512, 256, 128) if one % size == 0 and two % size == 0)
    first = one // tile
    return pl.pallas_call(
        functools.partial(weight_grads_kernel, first),
        grid=((one + two) // tile,),
        in_specs=[
            pl.BlockSpec((length, features), lambda i: (0, 0)),
            pl.BlockSpec((length, features), lambda i: (0, 0)),
            pl.BlockSpec((length, tile), lambda i: (0, jnp.minimum(i, first - 1))),
            pl.BlockSpec((length, tile), lambda i: (0, jnp.maximum(i - first, 0))),
        ],
        out_specs=pl.BlockSpec((features, tile), lambda i: (0, i)),
        out_shape=jax.ShapeDtypeStruct((features, one + two), HALF),
        name=name,
        cost_estimate=pl.CostEstimate(
            flops=2 * length * features * (one + two), bytes_accessed=40_000_000, transcendentals=0
        ),
        compiler_params=pltpu.CompilerParams(vmem_limit_bytes=56 * 2**20),
    )(left_one, left_two, right_one, right_two)


class Plane:
    def __init__(self, peers, source, whole, sends, receives):
        self.peers, self.source, self.whole = peers, source, whole
        self.sends, self.receives = sends, receives
        self.me = lax.axis_index("dp")
        self.rows = source.shape[0]
        self.width = source.shape[1]
        self.half = self.width // (2 * LANES) * LANES
        outer = [1 << bit for bit in range(1, peers.bit_length() - 1)]
        self.orders = [outer, outer[::-1]]
        self.steps = len(outer)

    def greet(self, barrier):
        for bit in [1] + self.orders[0]:
            pl.semaphore_signal(
                barrier, inc=1, device_id={"dp": self.me ^ bit}, device_id_type=MESH
            )
        return 1 + self.steps

    def held(self, side, step):
        order = self.orders[side]
        if step == 0:
            return [0]
        bit, before = order[step - 1], [0]
        for earlier in order[: step - 1]:
            before = before + [offset ^ earlier for offset in before]
        return [offset ^ bit for offset in before]

    def lanes(self, side):
        return pl.ds(0, self.half) if side == 0 else pl.ds(self.half, self.width - self.half)

    def block(self, side, offset):
        at = pl.ds(pl.multiple_of((self.me ^ offset) * self.rows, 16), self.rows)
        return self.whole.at[at, self.lanes(side)]

    def copy(self, side, bit, offset):
        source = self.source.at[:, self.lanes(side)] if offset == 0 else self.block(side, offset)
        at = (side, bit.bit_length() - 1, offset)
        return pltpu.make_async_remote_copy(
            src_ref=source,
            dst_ref=self.block(side, offset),
            send_sem=self.sends.at[at],
            recv_sem=self.receives.at[at],
            device_id={"dp": self.me ^ bit},
            device_id_type=MESH,
        )

    def arrival(self, side, bit, offset):
        at = (side, bit.bit_length() - 1, offset)
        return pltpu.make_async_remote_copy(
            src_ref=self.block(side, offset ^ bit),
            dst_ref=self.block(side, offset ^ bit),
            send_sem=self.sends.at[at],
            recv_sem=self.receives.at[at],
            device_id={"dp": self.me ^ bit},
            device_id_type=MESH,
        )

    def sent(self, side, step):
        blocks = []
        for earlier in range(step):
            blocks += self.held(side, earlier)
        return blocks

    def start(self):
        for side in (0, 1):
            if self.steps:
                self.copy(side, self.orders[side][0], 0).start()
        for side in (0, 1):
            self.copy(side, 1, 0).start()

    def advance(self, step):
        for side in (0, 1):
            bit = self.orders[side][step - 1]
            for offset in self.held(side, step):
                self.arrival(side, bit, offset ^ bit).wait_recv()
        for side in (0, 1):
            if step < self.steps:
                following = self.orders[side][step]
                for offset in self.sent(side, step + 1):
                    self.copy(side, following, offset).start()
        for side in (0, 1):
            for offset in self.held(side, step):
                self.copy(side, 1, offset).start()

    def finish(self):
        for side in (0, 1):
            for offset in self.sent(side, self.steps + 1):
                self.arrival(side, 1, offset).wait_recv()

    def drain(self):
        for side in (0, 1):
            for offset in self.sent(side, self.steps + 1):
                self.copy(side, 1, offset).wait_send()
            for step in range(1, self.steps + 1):
                for offset in self.sent(side, step):
                    self.copy(side, self.orders[side][step - 1], offset).wait_send()


class Swarm:
    def __init__(self, peers, count):
        self.peers, self.count = peers, count
        self.at_dp, self.at_tensor = lax.axis_index("dp"), lax.axis_index("tensor")

    def greet(self):
        barrier = pltpu.get_barrier_semaphore()
        for offset in range(1, self.peers):
            pl.semaphore_signal(barrier, inc=1, device_id={"dp": self.at_dp ^ offset}, device_id_type=MESH)
        for distance in range(1, self.count):
            pl.semaphore_signal(
                barrier, inc=1, device_id={"tensor": lax.rem(self.at_tensor + distance, self.count)}, device_id_type=MESH
            )
        pl.semaphore_wait(barrier, self.peers + self.count - 2)

    def along_dp(self, source_of, held, sends, receives):
        return [
            pltpu.make_async_remote_copy(
                src_ref=source_of(self.at_dp ^ offset),
                dst_ref=held.at[offset],
                send_sem=sends.at[offset],
                recv_sem=receives.at[offset],
                device_id={"dp": self.at_dp ^ offset},
                device_id_type=MESH,
            )
            for offset in range(1, self.peers)
        ]

    def along_tensor(self, source, held, sends, receives):
        return [
            pltpu.make_async_remote_copy(
                src_ref=source,
                dst_ref=held.at[distance],
                send_sem=sends.at[distance],
                recv_sem=receives.at[distance],
                device_id={"tensor": lax.rem(self.at_tensor + distance, self.count)},
                device_id_type=MESH,
            )
            for distance in range(1, self.count)
        ]


def plane_semaphores(peers):
    return [pltpu.SemaphoreType.DMA((2, max(peers.bit_length() - 1, 1), peers))] * 2


MESH = pl.DeviceIdType.MESH
TILE = 256


class Line:
    def __init__(self, count):
        self.count = count
        self.me = lax.axis_index("tensor")
        self.has_left = self.me > 0
        self.has_right = self.me < count - 1

    def greet(self, plane=None):
        barrier = pltpu.get_barrier_semaphore()
        extra = 0 if plane is None else plane.greet(barrier)
        for present, shift in ((self.has_left, -1), (self.has_right, 1)):

            @pl.when(present)
            def _():
                pl.semaphore_signal(
                    barrier, inc=1, device_id={"tensor": self.me + shift}, device_id_type=MESH
                )

        inside = self.has_left & self.has_right

        @pl.when(inside)
        def _():
            pl.semaphore_wait(barrier, 2 + extra)

        @pl.when(jnp.logical_not(inside))
        def _():
            pl.semaphore_wait(barrier, 1 + extra)

    def copy(self, source, target, sends, receives, at, side):
        return pltpu.make_async_remote_copy(
            src_ref=source,
            dst_ref=target,
            send_sem=sends.at[at],
            recv_sem=receives.at[at],
            device_id={"tensor": self.me + (1 if side == 0 else -1)},
            device_id_type=MESH,
        )

    def place(self, side):
        return self.me if side == 0 else self.count - 1 - self.me

    def ahead(self, side, distance):
        return self.me + distance if side == 0 else self.me - distance

    def next_there(self, side):
        return self.has_right if side == 0 else self.has_left

    def last_there(self, side):
        return self.has_left if side == 0 else self.has_right


class Scatter:
    def __init__(self, line, parts, rows, span, slots, sends, receives):
        self.line, self.parts, self.rows, self.span = line, parts, rows, span
        self.slots, self.sends, self.receives = slots, sends, receives

    def own(self, owner, chunk):
        return self.parts[pl.ds(pl.multiple_of(owner * self.rows + chunk * self.span, 16), self.span), :]

    def transfer(self, side, chunk, hop):
        return self.line.copy(
            self.slots.at[side, chunk, hop - 1],
            self.slots.at[side, chunk, hop],
            self.sends,
            self.receives,
            (side, chunk, hop - 1),
            side,
        )

    def hop(self, chunk, hop):
        line = self.line
        for side in (0, 1):
            place = line.place(side)
            slot = self.slots.at[side, chunk, hop - 1]
            owner = line.ahead(side, line.count - hop)

            @pl.when(place == 0)
            def _():
                slot[...] = self.own(owner, chunk).astype(slot.dtype)

            if hop > 1:

                @pl.when((place > 0) & (place <= hop - 1))
                def _():
                    self.transfer(side, chunk, hop - 1).wait_recv()
                    slot[...] = (slot[...].astype(FULL) + self.own(owner, chunk).astype(FULL)).astype(
                        slot.dtype
                    )

            @pl.when(place <= hop - 1)
            def _():
                self.transfer(side, chunk, hop).start()

    def finish(self, chunk, total):
        line = self.line
        total[...] = self.own(line.me, chunk).astype(FULL)
        last = line.count - 1
        for side in (0, 1):

            @pl.when(line.last_there(side))
            def _():
                self.transfer(side, chunk, last).wait_recv()
                total[...] += self.slots[side, chunk, last].astype(FULL)

    def drain(self, chunk):
        for hop in range(1, self.line.count):
            for side in (0, 1):

                @pl.when(self.line.place(side) <= hop - 1)
                def _():
                    self.transfer(side, chunk, hop).wait_send()


class Gather:
    def __init__(self, line, whole, rows, span, sends, receives):
        self.line, self.whole, self.rows, self.span = line, whole, rows, span
        self.sends, self.receives = sends, receives

    def at(self, owner, chunk):
        return self.whole.at[pl.ds(pl.multiple_of(owner * self.rows + chunk * self.span, 16), self.span), :]

    def transfer(self, side, chunk, hop):
        piece = self.at(self.line.ahead(1 - side, hop - 1), chunk)
        return self.line.copy(piece, piece, self.sends, self.receives, (side, chunk, hop - 1), side)

    def arrival(self, side, chunk, hop):
        piece = self.at(self.line.ahead(1 - side, hop), chunk)
        return self.line.copy(piece, piece, self.sends, self.receives, (side, chunk, hop - 1), side)

    def send(self, chunk, hop):
        line = self.line
        for side in (0, 1):

            @pl.when(line.next_there(side) & (line.place(side) >= hop - 1))
            def _():
                self.transfer(side, chunk, hop).start()

    def receive(self, chunk, hop):
        line = self.line
        for side in (0, 1):

            @pl.when(line.place(side) >= hop)
            def _():
                self.arrival(side, chunk, hop).wait_recv()

    def step(self, chunk, hop):
        line = self.line
        for side in (0, 1):

            @pl.when(line.place(side) >= hop)
            def _():
                self.arrival(side, chunk, hop).wait_recv()

            if hop < line.count - 1:

                @pl.when(line.next_there(side) & (line.place(side) >= hop))
                def _():
                    self.transfer(side, chunk, hop + 1).start()

    def drain(self, chunk):
        line = self.line
        for hop in range(1, line.count):
            for side in (0, 1):

                @pl.when(line.next_there(side) & (line.place(side) >= hop - 1))
                def _():
                    self.transfer(side, chunk, hop).wait_send()


def project(line, left, right, parts, rows, forward):
    upper = line.me < line.count // 2
    far = jnp.where(upper, line.count - 1, 0) * rows
    rest = jnp.where(upper, 0, 1) * rows

    def block(start, size):
        at = pl.ds(pl.multiple_of(start, 16), size)

        def tile(index, carry):
            lanes = pl.ds(pl.multiple_of(index * TILE, TILE), TILE)
            if forward:
                parts[at, lanes] = mm(left[at, :], right[:, lanes]).astype(parts.dtype)
            else:
                parts[at, lanes] = mm_nt(left[at, :], right[lanes, : left.shape[1]]).astype(parts.dtype)
            return carry

        lax.fori_loop(0, parts.shape[1] // TILE, tile, 0)

    return (lambda: block(far, rows)), (lambda: block(rest, (line.count - 1) * rows))


def relay(line, scatter, gather, chunks, lag, rows_done, first=None, second=None, events=None, received=None):
    last = line.count - 1
    if first is not None:
        first()
    turns = lag * (chunks - 1) + last + 1 + (0 if gather is None else last)
    for turn in range(turns):
        arrived = []
        for chunk in range(chunks):
            hop = turn - lag * chunk + 1
            if 1 <= hop <= last:
                scatter.hop(chunk, hop)
            elif hop == last + 1:
                rows_done(chunk)
                if gather is not None:
                    gather.send(chunk, 1)
            elif gather is not None and last + 1 < hop <= 2 * last + 1:
                gather.step(chunk, hop - last - 1)
                if hop == 2 * last + 1:
                    arrived.append(chunk)
        if turn == 0 and second is not None:
            second()
        if events is not None and turn in events:
            events[turn]()
        if received is not None:
            for chunk in arrived:
                received(chunk)
    for chunk in range(chunks):
        scatter.drain(chunk)
        if gather is not None:
            gather.drain(chunk)


def norm_below(value, above, gain):
    inverse = lax.rsqrt(jnp.mean(value * value, -1, keepdims=True) + EPSILON)
    plain = value * inverse
    scaled = above * gain
    below = inverse * (scaled - plain * jnp.mean(scaled * plain, -1, keepdims=True))
    return below, jnp.sum(above * plain, 0, keepdims=True)


def ffn_kernel(
    count, peers, chunks, lag, rows, units,
    left, right, hidden, gain, cot_rows, local_weight,
    out, activated, grad_gate, parts, out_parts, middle,
    weight, slots, total, part_rows, part_cot, part_gate, part_act, own_sem, s0, s1, s2, s3, p0, p1,
):
    line = Line(count)
    span = rows // chunks
    features = hidden.shape[1]
    plane = Plane(peers, local_weight, weight, p0, p1)
    keep_weight = pltpu.make_async_copy(
        local_weight, weight.at[pl.ds(pl.multiple_of(plane.me * plane.rows, 16), plane.rows), :], own_sem
    )
    keep_weight.start()
    line.greet(plane)
    plane.start()
    scatter = Scatter(line, parts, rows, span, slots, s0, s1)
    gather = Gather(line, out, rows, span, s2, s3)

    def rows_done(chunk):
        at = pl.ds(chunk * span, span)
        scatter.finish(chunk, total)
        value = total[...] + hidden[at, :].astype(FULL)
        middle[at, :] = value
        inverse = lax.rsqrt(jnp.mean(value * value, -1, keepdims=True) + EPSILON)
        gather.at(line.me, chunk)[...] = (value * inverse * gain[...]).astype(HALF)

    def received(chunk):
        if chunk == 0:
            plane.finish()
            keep_weight.wait()
        here = [pl.ds(owner * rows + chunk * span, span) for owner in range(count)]
        there = [slice(owner * span, (owner + 1) * span) for owner in range(count)]
        for source, target in zip(here, there):
            part_rows[target, :] = out[source, :]
            part_cot[target, :] = cot_rows[source, :]

        def gates(index, carry):
            lanes = pl.ds(pl.multiple_of(index * TILE, TILE), TILE)
            upper = pl.ds(pl.multiple_of(units + index * TILE, TILE), TILE)
            lower = pl.ds(pl.multiple_of(2 * units + index * TILE, TILE), TILE)
            gate = mm(part_rows[...], weight[:, lanes])
            up = mm(part_rows[...], weight[:, upper])
            grad_act = mm(part_cot[...], weight[:, lower])
            sig = sigmoid(gate)
            silu = gate * sig
            act = (silu * up).astype(HALF)
            grad_one = (grad_act * up * (sig * (1.0 + gate * (1.0 - sig)))).astype(HALF)
            grad_two = (grad_act * silu).astype(HALF)
            part_gate[:, lanes] = grad_one
            part_gate[:, upper] = grad_two
            part_act[:, lanes] = act
            for source, target in zip(there, here):
                activated[target, lanes] = act[source, :]
                grad_gate[target, lanes] = grad_one[source, :]
                grad_gate[target, upper] = grad_two[source, :]
            return carry

        lax.fori_loop(0, units // TILE, gates, 0)

        def back(index, carry):
            lanes = pl.ds(pl.multiple_of(index * TILE, TILE), TILE)
            result = mm_nt(part_gate[...], weight[lanes, : 2 * units]).astype(parts.dtype)
            for source, target in zip(there, here):
                parts[target, lanes] = result[source, :]
            result = mm_nt(part_act[...], weight[lanes, 2 * units :]).astype(out_parts.dtype)
            for source, target in zip(there, here):
                out_parts[target, lanes] = result[source, :]
            return carry

        lax.fori_loop(0, features // TILE, back, 0)

    last = count - 1
    events = {}
    for step in range(1, plane.steps + 1):
        events[min(2 + 3 * (step - 1), 2 * last - 1 - (plane.steps - step))] = functools.partial(plane.advance, step)
    first, second = project(line, left, right, parts, rows, True)
    relay(line, scatter, gather, chunks, lag, rows_done, first, second, events, received)
    plane.drain()


def ffn_rows_call(count, peers, chunks, lag, branches, weight_out, hidden, gain, cot_rows, local_weight):
    rows, features = hidden.shape
    length = count * rows
    units = local_weight.shape[1] // 3
    span = rows // chunks
    vmem = pl.BlockSpec(memory_space=pltpu.VMEM)
    return pl.pallas_call(
        functools.partial(ffn_kernel, count, peers, chunks, lag, rows, units),
        in_specs=[vmem] * 5 + [pl.BlockSpec(memory_space=pl.ANY)],
        out_specs=[vmem] * 6,
        out_shape=[
            jax.ShapeDtypeStruct((length, features), HALF),
            jax.ShapeDtypeStruct((length, units), HALF),
            jax.ShapeDtypeStruct((length, 2 * units), HALF),
            jax.ShapeDtypeStruct((length, features), HALF),
            jax.ShapeDtypeStruct((length, features), HALF),
            jax.ShapeDtypeStruct((rows, features), FULL),
        ],
        scratch_shapes=[
            pltpu.VMEM((peers * local_weight.shape[0], 3 * units), HALF),
            pltpu.VMEM((2, chunks, count, span, features), HALF),
            pltpu.VMEM((span, features), FULL),
            pltpu.VMEM((count * span, features), HALF),
            pltpu.VMEM((count * span, features), HALF),
            pltpu.VMEM((count * span, 2 * units), HALF),
            pltpu.VMEM((count * span, units), HALF),
            pltpu.SemaphoreType.DMA(()),
        ]
        + [pltpu.SemaphoreType.DMA((2, chunks, count - 1))] * 4
        + plane_semaphores(peers),
        name="ffn_rows",
        cost_estimate=pl.CostEstimate(flops=150_000_000_000, bytes_accessed=40_000_000, transcendentals=0),
        compiler_params=pltpu.CompilerParams(
            collective_id=1, has_side_effects=True, vmem_limit_bytes=61 * 2**20
        ),
    )(branches, weight_out, hidden, gain, cot_rows, local_weight)


def ffn_grad_kernel(
    count, chunks, lag, rows, parts, middle, cotangent, gain, out, grad_middle, gain_grad, total, slots, s0, s1, s2, s3
):
    line = Line(count)
    span = rows // chunks
    line.greet()
    scatter = Scatter(line, parts, rows, span, slots, s0, s1)
    gather = Gather(line, out, rows, span, s2, s3)
    gain_grad[...] = jnp.zeros_like(gain_grad)

    def rows_done(chunk):
        at = pl.ds(chunk * span, span)
        scatter.finish(chunk, total)
        below, part = norm_below(middle[at, :], total[...], gain[...])
        gain_grad[...] += part
        result = cotangent[at, :].astype(FULL) + below
        grad_middle[at, :] = result
        gather.at(line.me, chunk)[...] = result.astype(HALF)

    relay(line, scatter, gather, chunks, lag, rows_done)


def ffn_grad_rows(count, chunks, lag, parts, middle, cotangent, gain):
    rows, features = middle.shape
    span = rows // chunks
    vmem = pl.BlockSpec(memory_space=pltpu.VMEM)
    operands = (parts, middle, cotangent, gain)
    return pl.pallas_call(
        functools.partial(ffn_grad_kernel, count, chunks, lag, rows),
        in_specs=[vmem] * len(operands),
        out_specs=[vmem] * 3,
        out_shape=[
            jax.ShapeDtypeStruct((count * rows, features), HALF),
            jax.ShapeDtypeStruct((rows, features), FULL),
            jax.ShapeDtypeStruct((1, features), FULL),
        ],
        scratch_shapes=[
            pltpu.VMEM((span, features), FULL),
            pltpu.VMEM((2, chunks, count, span, features), HALF),
        ]
        + [pltpu.SemaphoreType.DMA((2, chunks, count - 1))] * 4,
        name="ffn_grad_rows",
        cost_estimate=pl.CostEstimate(flops=100_000_000_000, bytes_accessed=20_000_000, transcendentals=0),
        compiler_params=pltpu.CompilerParams(
            collective_id=2, has_side_effects=True, vmem_limit_bytes=56 * 2**20
        ),
    )(*operands)


def entry_kernel(
    count, peers, rows, own, gains, query, keyval, mamba, state, step, kv_lanes,
    out, weight, all_gains, raw, local, held, own_sems, s0, s1, p0, p1, g0, g1,
):
    line = Line(count)
    swarm = Swarm(peers, count)
    plane = Plane(peers, local, weight, p0, p1)
    block = gains.shape[1]
    keep = pltpu.make_async_copy(own, raw.at[pl.ds(pl.multiple_of(line.me * rows, 16), rows), :], own_sems.at[0])
    keep.start()
    swarm.greet()
    keep.wait()
    gather = Gather(line, raw, rows, rows, s0, s1)
    gather.send(0, 1)
    sent = swarm.along_dp(lambda device: gains, held, g0, g1)
    for copy in sent:
        copy.start()
    start = 0
    shared = pl.ds(pl.multiple_of(kv_lanes(line.me), ATT_DIM), ATT_DIM)
    for part in (query[...], keyval[:, 0, shared], keyval[:, 1, shared], mamba[:, 0, :], mamba[:, 1, :],
                 state[:, 0, :], state[:, 1, :], step[...]):
        local[:, start : start + part.shape[1]] = part
        start += part.shape[1]
    keep_weight = pltpu.make_async_copy(
        local, weight.at[pl.ds(pl.multiple_of(plane.me * plane.rows, 16), plane.rows), :], own_sems.at[1]
    )
    keep_weight.start()
    plane.start()
    held[0] = gains[...]
    for copy in sent:
        copy.wait()
    for offset in range(peers):
        lanes = pl.ds(pl.multiple_of((swarm.at_dp ^ offset) * block, block), block)
        all_gains[:, lanes] = held[offset]

    def normed(owner):
        at = pl.ds(pl.multiple_of(owner * rows, 16), rows)
        value = raw[at, :].astype(FULL)
        inverse = lax.rsqrt(jnp.mean(value * value, -1, keepdims=True) + EPSILON)
        out[at, :] = (value * inverse * all_gains[0:1, :]).astype(HALF)

    normed(line.me)
    for hop in range(1, count):
        gather.step(0, hop)
        if hop <= plane.steps:
            plane.advance(hop)
        for side in (0, 1):

            @pl.when(line.place(side) >= hop)
            def _():
                normed(line.ahead(1 - side, hop))

    for extra in range(count, plane.steps + 1):
        plane.advance(extra)
    plane.finish()
    gather.drain(0)
    plane.drain()
    keep_weight.wait()


def entry(count, peers, own, gains, query, keyval, mamba, state, step, kv_lanes):
    rows, features = own.shape
    block = query.shape[0]
    total = query.shape[1] + 2 * ATT_DIM + 2 * mamba.shape[2] + 2 * state.shape[2] + step.shape[1]
    vmem, anywhere = pl.BlockSpec(memory_space=pltpu.VMEM), pl.BlockSpec(memory_space=pl.ANY)
    return pl.pallas_call(
        lambda *refs: entry_kernel(count, peers, rows, *refs[:7], kv_lanes, *refs[7:]),
        in_specs=[vmem] * 7,
        out_specs=[vmem, anywhere, vmem],
        out_shape=[
            jax.ShapeDtypeStruct((count * rows, features), own.dtype),
            jax.ShapeDtypeStruct((peers * block, total), HALF),
            jax.ShapeDtypeStruct((gains.shape[0], peers * block), FULL),
        ],
        scratch_shapes=[
            pltpu.VMEM((count * rows, features), HALF),
            pltpu.VMEM((block, total), HALF),
            pltpu.VMEM((peers,) + gains.shape, FULL),
            pltpu.SemaphoreType.DMA((2,)),
        ]
        + [pltpu.SemaphoreType.DMA((2, 1, count - 1))] * 2
        + plane_semaphores(peers)
        + [pltpu.SemaphoreType.DMA((peers,))] * 2,
        name="entry",
        cost_estimate=pl.CostEstimate(flops=80_000_000_000, bytes_accessed=20_000_000, transcendentals=0),
        compiler_params=pltpu.CompilerParams(
            collective_id=0, has_side_effects=True, vmem_limit_bytes=48 * 2**20
        ),
    )(own, gains, query, keyval, mamba, state, step)


def input_grad_kernel(
    count, peers, chunks, lag, rows, left, right, hidden, grad_middle, gain, ffn_gain_grad, head_rows,
    out, gain_out, head_out,
    parts, total, slots, gain_rows, held_heads, held_dp, held_tensor, gain_sum, s0, s1, h0, h1, d0, d1, t0, t1,
):
    line = Line(count)
    swarm = Swarm(peers, count)
    span = rows // chunks
    block = gain_out.shape[1]
    swarm.greet()
    heads_sent = swarm.along_dp(lambda device: head_rows, held_heads, h0, h1)
    for copy in heads_sent:
        copy.start()
    scatter = Scatter(line, parts, rows, span, slots, s0, s1)
    gain_rows[...] = jnp.zeros_like(gain_rows)
    gain_rows[1:2, :] = ffn_gain_grad[...]

    def rows_done(chunk):
        at = pl.ds(chunk * span, span)
        scatter.finish(chunk, total)
        value = hidden[at, :].astype(FULL)
        below, part = norm_below(value, total[...], gain[...])
        gain_rows[0:1, :] += part
        out[at, :] = grad_middle[at, :] + below

    first, second = project(line, left, right, parts, rows, False)
    relay(line, scatter, None, chunks, lag, rows_done, first, second)
    own_lanes = lambda device: pl.ds(pl.multiple_of(device * block, block), block)
    gains_sent = swarm.along_dp(lambda device: gain_rows.at[:, own_lanes(device)], held_dp, d0, d1)
    for copy in gains_sent:
        copy.start()
    head_out[...] = head_rows[...]
    for offset, copy in enumerate(heads_sent):
        copy.wait()
        head_out[...] += held_heads[offset + 1]
    gain_sum[...] = gain_rows[:, own_lanes(swarm.at_dp)]
    for offset, copy in enumerate(gains_sent):
        copy.wait()
        gain_sum[...] += held_dp[offset + 1]
    last_sent = swarm.along_tensor(gain_sum, held_tensor, t0, t1)
    for copy in last_sent:
        copy.start()
    gain_out[...] = gain_sum[...]
    for distance, copy in enumerate(last_sent):
        copy.wait()
        gain_out[...] += held_tensor[distance + 1]


def input_grad_rows(count, peers, chunks, lag, grads, weight_in, hidden, grad_middle, gain, ffn_gain_grad, head_rows):
    rows, features = hidden.shape
    span = rows // chunks
    block = features // peers
    vmem = pl.BlockSpec(memory_space=pltpu.VMEM)
    operands = (grads, weight_in, hidden, grad_middle, gain, ffn_gain_grad, head_rows)
    return pl.pallas_call(
        functools.partial(input_grad_kernel, count, peers, chunks, lag, rows),
        in_specs=[vmem] * len(operands),
        out_specs=[vmem] * 3,
        out_shape=[
            jax.ShapeDtypeStruct((rows, features), FULL),
            jax.ShapeDtypeStruct((8, block), FULL),
            jax.ShapeDtypeStruct(head_rows.shape, FULL),
        ],
        scratch_shapes=[
            pltpu.VMEM((count * rows, features), HALF),
            pltpu.VMEM((span, features), FULL),
            pltpu.VMEM((2, chunks, count, span, features), HALF),
            pltpu.VMEM((8, features), FULL),
            pltpu.VMEM((peers,) + head_rows.shape, FULL),
            pltpu.VMEM((peers, 8, block), FULL),
            pltpu.VMEM((count, 8, block), FULL),
            pltpu.VMEM((8, block), FULL),
        ]
        + [pltpu.SemaphoreType.DMA((2, chunks, count - 1))] * 2
        + [pltpu.SemaphoreType.DMA((peers,))] * 4
        + [pltpu.SemaphoreType.DMA((count,))] * 2,
        name="input_grad_rows",
        cost_estimate=pl.CostEstimate(flops=80_000_000_000, bytes_accessed=20_000_000, transcendentals=0),
        compiler_params=pltpu.CompilerParams(
            collective_id=3, has_side_effects=True, vmem_limit_bytes=56 * 2**20
        ),
    )(*operands)


CHUNKS = 4
LAG = 2


def sum_rows(pieces):
    return lax.psum_scatter(pieces, "tensor", scatter_dimension=0, tiled=True).astype(FULL)


def dot_nt(a, b):
    return jnp.einsum("sb,ab->sa", a, b, preferred_element_type=FULL)


def body(
    hidden_in,
    segments,
    norm_gain,
    mamba_in,
    step_weight,
    state_weight,
    decay_log,
    step_bias,
    skip_gain,
    gated_gain,
    query_weight,
    keyval_weight,
    mamba_out,
    attn_out,
    ffn_gain,
    gate_up,
    down_weight,
    cotangent,
):
    tensor_index = lax.axis_index("tensor")
    count, peers = lax.axis_size("tensor"), lax.axis_size("dp")
    heads = decay_log.shape[0]
    width = mamba_in.shape[2]
    state_size = state_weight.shape[2]
    query_width = query_weight.shape[1]
    qheads = query_width // ATT_DIM
    units = gate_up.shape[2]
    rows_local = hidden_in.shape[0]
    block = norm_gain.shape[0]
    group_size = ATT_HEADS // KV_HEADS
    kv_head = tensor_index * qheads // group_size
    col = Columns(query_width, width, state_size)

    gains = jnp.pad(jnp.stack([norm_gain, ffn_gain]).astype(FULL), ((0, 6), (0, 0)))
    step_padded = jnp.pad(step_weight, ((0, 0), (0, 2 * LANES - heads)))
    sequence, weight_in, gains = entry(
        count,
        peers,
        hidden_in,
        gains,
        query_weight,
        keyval_weight,
        mamba_in,
        state_weight,
        step_padded,
        lambda place: (place * qheads // group_size) * ATT_DIM,
    )
    gain_one, gain_two = gains[0:1], gains[1:2]
    weight_out = lax.all_gather(jnp.concatenate([mamba_out, attn_out], 0), "dp", axis=1, tiled=True)
    local_ffn = jnp.concatenate([gate_up.reshape(block, 2 * units), down_weight.T], 1)
    sequence, cotangent_late, weight_out = lax.optimization_barrier((sequence, cotangent, weight_out))
    cot_rows = lax.all_gather(cotangent_late, "tensor", axis=0, tiled=True)
    length = sequence.shape[0]
    packed = jnp.dot(sequence, weight_in, preferred_element_type=FULL)
    head_params = jnp.pad(
        jnp.stack([decay_log, step_bias, skip_gain]), ((0, 5), (0, LANES - heads))
    )
    tables = rope_tables(length)

    scan_y, states, gated_vals, squares = scan_forward(
        col, heads, state_size, packed, segments, head_params
    )
    attended, lse, squares = attend_forward(col, qheads, count, packed, tables, segments, squares)
    gated_inverse = lax.rsqrt(squares / (MAMBA_HEADS * HEAD_DIM) + EPSILON).reshape(length, 1)
    gated_scale = gated_gain.astype(FULL)
    gated_plain = gated_vals * gated_inverse
    branches = jnp.concatenate([(gated_plain * gated_scale).astype(HALF), attended], 1)
    ffn_rows, activated, grad_gate, ffn_parts, out_parts, middle = ffn_rows_call(
        count, peers, CHUNKS, LAG, branches, weight_out, hidden_in, gain_two, cot_rows, local_ffn
    )
    ffn_grad = weight_grads(ffn_rows, grad_gate, cot_rows, activated, "ffn_weight_grads")
    ffn_parts, ffn_grad = lax.optimization_barrier((ffn_parts, ffn_grad))
    ffn_share = lax.psum_scatter(ffn_grad, "dp", scatter_dimension=0, tiled=True)
    grad_mixed, grad_middle, ffn_gain_part = ffn_grad_rows(
        count, CHUNKS, LAG, ffn_parts, middle, cotangent, gain_two
    )
    grad_mixed, ffn_share, out_parts = lax.optimization_barrier((grad_mixed, ffn_share, out_parts))
    ffn_out = sum_rows(out_parts)
    grad_branches = dot_nt(grad_mixed, weight_out)
    product_sum = jnp.sum(grad_branches[:, :width] * gated_scale * gated_plain, -1).reshape(-1, LANES)
    attention_grads, product_sum = attend_backward(
        col, qheads, count, packed, attended, lse, grad_branches, tables, segments, product_sum
    )
    grads, gain_part, skip_part, head_part = scan_backward(
        col,
        heads,
        state_size,
        packed,
        scan_y,
        states,
        grad_branches,
        squares,
        product_sum,
        gated_scale[None, :],
        segments,
        head_params,
        attention_grads,
    )
    in_grad = weight_grads(sequence, grads, grad_mixed, branches, "in_out_weight_grads")
    grads, in_grad, ffn_out = lax.optimization_barrier((grads, in_grad, ffn_out))
    in_share = lax.psum_scatter(in_grad, "dp", scatter_dimension=0, tiled=True)
    head_sums = jnp.concatenate(
        [
            gain_part[0],
            head_part[0, :heads],
            head_part[1, :heads],
            skip_part.reshape(heads, HEAD_DIM).sum(1),
        ]
    )
    head_rows = jnp.pad(head_sums, (0, 8 * LANES - head_sums.shape[0])).reshape(8, LANES)
    hidden_grad, gain_grads, head_rows = input_grad_rows(
        count, peers, 2, 1, grads, weight_in, hidden_in, grad_middle, gain_one, ffn_gain_part, head_rows
    )
    head_sums = head_rows.reshape(-1)
    hidden_grad, ffn_out, ffn_share = lax.optimization_barrier((hidden_grad, ffn_out, ffn_share))
    hidden_out = (middle + ffn_out).astype(HALF)
    out_share = in_share[:, col.total :].T

    keyval_part = jnp.stack(
        [in_share[:, slice(*col.key)], in_share[:, slice(*col.value)]], 1
    )
    keyval_grad = lax.dynamic_update_slice_in_dim(
        jnp.zeros(keyval_weight.shape, HALF), keyval_part, kv_head * ATT_DIM, 2
    ).reshape(block, -1)
    shared = lax.psum(
        jnp.concatenate([in_share[:, col.inmap[0] : col.outmap[1]], keyval_grad], 1), "tensor"
    ).astype(FULL)
    state_weight_grad = shared[:, : 2 * state_size].reshape(state_weight.shape)
    keyval_weight_grad = shared[:, 2 * state_size :].reshape(keyval_weight.shape)

    inner_grad = jnp.stack([in_share[:, slice(*col.gate)], in_share[:, slice(*col.drive)]], 1)
    return (
        hidden_out,
        hidden_grad,
        gain_grads[0],
        inner_grad.astype(FULL),
        in_share[:, col.step[0] : col.step[0] + heads].astype(FULL),
        state_weight_grad,
        head_sums[width : width + heads],
        head_sums[width + heads : width + 2 * heads],
        head_sums[width + 2 * heads : width + 3 * heads],
        head_sums[:width],
        in_share[:, slice(*col.query)].astype(FULL),
        keyval_weight_grad,
        out_share[:width].astype(FULL),
        out_share[width:].astype(FULL),
        gain_grads[1],
        ffn_share[:, : 2 * units].reshape(gate_up.shape).astype(FULL),
        ffn_share[:, 2 * units :].T.astype(FULL),
    )


def solution(mesh):
    rows = P(("dp", "tensor"), None)
    weights_in = P("dp", None, "tensor")
    return jax.shard_map(
        body,
        mesh=mesh,
        in_specs=(
            rows,
            P("dp"),
            P("dp"),
            weights_in,
            P("dp", "tensor"),
            P("dp", None, None),
            P("tensor"),
            P("tensor"),
            P("tensor"),
            P("tensor"),
            P("dp", "tensor"),
            P("dp", None, None),
            P("tensor", "dp"),
            P("tensor", "dp"),
            P("dp"),
            weights_in,
            P("tensor", "dp"),
            rows,
        ),
        out_specs=(
            rows,
            rows,
            P("dp"),
            weights_in,
            P("dp", "tensor"),
            P("dp", None, None),
            P("tensor"),
            P("tensor"),
            P("tensor"),
            P("tensor"),
            P("dp", "tensor"),
            P("dp", None, None),
            P("tensor", "dp"),
            P("tensor", "dp"),
            P("dp"),
            weights_in,
            P("tensor", "dp"),
        ),
        check_vma=False,
    )
```

```python
import functools
import math
import jax
import jax.numpy as jnp
from jax import lax
from jax.experimental import pallas as pl
from jax.experimental.pallas import tpu as pltpu
from jax.sharding import PartitionSpec as P

MAMBA_HEADS = 48
HEAD_DIM = 64
ATT_HEADS = 8
KV_HEADS = 2
ATT_DIM = 128
STRETCH = 128
ATT_BLOCK = 256
EPSILON = 1e-05
PRECISE = lax.Precision.HIGHEST
ROPE_BASE = 10000.0
LANES = 128
MASKED = -1e30
HALF = jnp.bfloat16
FULL = jnp.float32


def mm(a, b):
    return jnp.dot(a, b, preferred_element_type=FULL)


def mm_nt(a, b):
    return lax.dot_general(a, b, (((1,), (1,)), ((), ())), preferred_element_type=FULL)


def mm_tn(a, b):
    return lax.dot_general(a, b, (((0,), (0,)), ((), ())), preferred_element_type=FULL)


def softplus(v):
    return jnp.maximum(v, 0.0) + jnp.log1p(jnp.exp(-jnp.abs(v)))


def sigmoid(v):
    return 1.0 / (1.0 + jnp.exp(-v))


def iota(shape, dim):
    return lax.broadcasted_iota(jnp.int32, shape, dim)


def halves(left, right, size):
    return jnp.where(iota((size, LANES), 1) < HEAD_DIM, left, right)


def as_row(values):
    return jnp.broadcast_to(values, (LANES, LANES)).T[0:1, :]


def as_column(values):
    return jnp.broadcast_to(values, (LANES, LANES)).T[:, 0:1]


def stacked_pair(pair):
    low = iota(pair.shape, 1) < HEAD_DIM
    zero = jnp.zeros_like(pair)
    return jnp.concatenate([jnp.where(low, pair, zero), jnp.where(low, zero, pair)], 0)


class Columns:
    def __init__(self, query, width, state):
        self.query = (0, query)
        self.key = (query, query + ATT_DIM)
        self.value = (query + ATT_DIM, query + 2 * ATT_DIM)
        start = query + 2 * ATT_DIM
        self.attention = start
        self.gate = (start, start + width)
        self.drive = (start + width, start + 2 * width)
        start += 2 * width
        self.inmap = (start, start + state)
        self.outmap = (start + state, start + 2 * state)
        start += 2 * state
        self.step = (start, start + LANES)
        self.total = start + 2 * LANES


def stretch_common(col, packed, segc_ref, segr_ref, head_ref, before):
    span = STRETCH
    raw = packed[:, col.step[0] : col.step[1]] + head_ref[1:2, :]
    step = softplus(raw)
    keep = -jnp.exp(head_ref[0:1, :]) * step
    row, column = iota((span, span), 0), iota((span, span), 1)
    running = jnp.dot(
        (row >= column).astype(FULL), keep, precision=PRECISE, preferred_element_type=FULL
    )
    segc, segr = segc_ref[...], segr_ref[0]
    causal = (row >= column) & (segc == segr)
    blocked = jnp.where(causal, 0.0, MASKED)
    live = (segc == before).astype(FULL)
    last = segc[span - 1 : span, :]
    tail = (segc == last).astype(FULL)
    old = (last == before).astype(FULL)
    return raw, step, keep, running, running.T, blocked, live, tail, old


def pair_decay(pair, running, running_t, blocked, live, tail, old):
    span = STRETCH
    a, b = 2 * pair, 2 * pair + 1
    col_a = jnp.broadcast_to(running[:, a : a + 1], (span, LANES))
    col_b = jnp.broadcast_to(running[:, b : b + 1], (span, LANES))
    decay_a = jnp.exp(col_a - running_t[a : a + 1, :] + blocked)
    decay_b = jnp.exp(col_b - running_t[b : b + 1, :] + blocked)
    both = halves(col_a, col_b, span)
    last = both[span - 1 : span, :]
    into = jnp.exp(both) * live
    weight = jnp.exp(last - both) * tail
    keep_old = jnp.exp(last) * old
    return decay_a, decay_b, into, weight, keep_old


def scan_forward_kernel(col, heads, p_ref, segc_ref, segr_ref, head_ref, y_ref, states_ref, gated_ref, square_ref, state, before):
    index = pl.program_id(0)
    span = STRETCH

    @pl.when(index == 0)
    def _():
        state[...] = jnp.zeros_like(state)
        before[...] = jnp.full_like(before, -1)

    raw, step, keep, running, running_t, blocked, live, tail, old = stretch_common(
        col, p_ref, segc_ref, segr_ref, head_ref, before[...]
    )
    inmap = p_ref[:, col.inmap[0] : col.inmap[1]].astype(HALF)
    outmap = p_ref[:, col.outmap[0] : col.outmap[1]].astype(HALF)
    inmap_t = inmap.T
    scores = mm_nt(outmap, inmap)
    square = jnp.zeros((span, 1), FULL)
    for pair in range(heads // 2):
        at = pair * LANES
        lanes = slice(at, at + LANES)
        decay_a, decay_b, into, weight, keep_old = pair_decay(
            pair, running, running_t, blocked, live, tail, old
        )
        drive = p_ref[:, col.drive[0] + at : col.drive[0] + at + LANES]
        gate = p_ref[:, col.gate[0] + at : col.gate[0] + at + LANES]
        driven = drive * halves(step[:, 2 * pair : 2 * pair + 1], step[:, 2 * pair + 1 : 2 * pair + 2], span)
        driven_low = driven.astype(HALF)
        mix = jnp.concatenate([(decay_a * scores).astype(HALF), (decay_b * scores).astype(HALF)], 1)
        held = state[:, lanes]
        held_low = held.astype(HALF)
        states_ref[0, :, lanes] = held_low
        result = mm(mix, stacked_pair(driven_low)) + mm(outmap, held_low) * into
        state[:, lanes] = held * keep_old + mm(inmap_t, (driven_low.astype(FULL) * weight).astype(HALF))
        y_ref[:, lanes] = result
        skip = halves(head_ref[2:3, 2 * pair : 2 * pair + 1], head_ref[2:3, 2 * pair + 1 : 2 * pair + 2], 1)
        gated = (result + skip * drive) * (gate * sigmoid(gate))
        gated_ref[:, lanes] = gated
        square = square + jnp.sum(gated * gated, 1, keepdims=True)
    square_ref[pl.ds(index, 1), :] = as_row(square)
    before[...] = segc_ref[span - 1 : span, :]


def scan_forward(col, heads, state_size, packed, segments, head_params):
    length = packed.shape[0]
    width = heads * HEAD_DIM
    count = length // STRETCH
    return pl.pallas_call(
        functools.partial(scan_forward_kernel, col, heads),
        grid=(count,),
        in_specs=[
            pl.BlockSpec((STRETCH, col.total), lambda i: (i, 0)),
            pl.BlockSpec((STRETCH, 1), lambda i: (i, 0)),
            pl.BlockSpec((1, 1, STRETCH), lambda i: (i, 0, 0)),
            pl.BlockSpec((8, LANES), lambda i: (0, 0)),
        ],
        out_specs=[
            pl.BlockSpec((STRETCH, width), lambda i: (i, 0)),
            pl.BlockSpec((1, state_size, width), lambda i: (i, 0, 0)),
            pl.BlockSpec((STRETCH, width), lambda i: (i, 0)),
            pl.BlockSpec((count, LANES), lambda i: (0, 0)),
        ],
        out_shape=[
            jax.ShapeDtypeStruct((length, width), FULL),
            jax.ShapeDtypeStruct((count, state_size, width), HALF),
            jax.ShapeDtypeStruct((length, width), FULL),
            jax.ShapeDtypeStruct((count, LANES), FULL),
        ],
        scratch_shapes=[pltpu.VMEM((state_size, width), FULL), pltpu.VMEM((1, 1), jnp.int32)],
        name="scan_forward",
        cost_estimate=pl.CostEstimate(flops=16_000_000_000, bytes_accessed=30_000_000, transcendentals=0),
        compiler_params=pltpu.CompilerParams(vmem_limit_bytes=48 * 2**20),
    )(packed, segments[:, None], segments.reshape(count, 1, STRETCH), head_params)


def scan_backward_kernel(
    col, heads, total_width, p_ref, y_ref, states_ref, gm_ref, inv_ref, prod_ref, gain_ref,
    segc_ref, segr_ref, segb_ref, head_ref, ag_ref, g_ref, gain_grad_ref, skip_grad_ref, head_grad_ref, future,
):
    step_index = pl.program_id(0)
    count = pl.num_programs(0)
    span = STRETCH

    @pl.when(step_index == 0)
    def _():
        future[...] = jnp.zeros_like(future)
        gain_grad_ref[...] = jnp.zeros_like(gain_grad_ref)
        skip_grad_ref[...] = jnp.zeros_like(skip_grad_ref)
        head_grad_ref[...] = jnp.zeros_like(head_grad_ref)

    before = jnp.where(step_index == count - 1, -1, segb_ref[span - 1 : span, :])
    raw, step, keep, running, running_t, blocked, live, tail, old = stretch_common(
        col, p_ref, segc_ref, segr_ref, head_ref, before
    )
    inmap = p_ref[:, col.inmap[0] : col.inmap[1]].astype(HALF)
    outmap = p_ref[:, col.outmap[0] : col.outmap[1]].astype(HALF)
    outmap_t = outmap.T
    scores = mm_nt(outmap, inmap)
    lane = iota((span, LANES), 1)
    head_lane = iota((1, LANES), 1)
    paired = jnp.zeros((span, span), FULL)
    grad_in = jnp.zeros(inmap.shape, FULL)
    grad_out = jnp.zeros(outmap.shape, FULL)
    grad_running = jnp.zeros((span, LANES), FULL)
    grad_step = jnp.zeros((span, LANES), FULL)
    grad_last = jnp.zeros((1, LANES), FULL)
    chunk = pl.ds(count - 1 - step_index, 1)
    inverse = as_column(lax.rsqrt(inv_ref[chunk, :] * (1.0 / total_width) + EPSILON))
    product = as_column(prod_ref[chunk, :] * (1.0 / total_width))
    for pair in range(heads // 2):
        at = pair * LANES
        lanes = slice(at, at + LANES)
        a, b = 2 * pair, 2 * pair + 1
        decay_a, decay_b, into, weight, keep_old = pair_decay(
            pair, running, running_t, blocked, live, tail, old
        )
        drive = p_ref[:, col.drive[0] + at : col.drive[0] + at + LANES]
        gate = p_ref[:, col.gate[0] + at : col.gate[0] + at + LANES]
        result = y_ref[:, lanes]
        skip = halves(head_ref[2:3, a : a + 1], head_ref[2:3, b : b + 1], 1)
        sig = sigmoid(gate)
        silu = gate * sig
        ssm = result + skip * drive
        plain = ssm * silu * inverse
        grad_above = gm_ref[:, lanes].astype(FULL)
        gain_grad_ref[:, lanes] += jnp.sum(grad_above * plain, 0, keepdims=True)
        grad_gated = inverse * (grad_above * gain_ref[:, lanes] - plain * product)
        g_ref[:, col.gate[0] + at : col.gate[0] + at + LANES] = (
            grad_gated * ssm * (sig * (1.0 + gate * (1.0 - sig)))
        ).astype(HALF)
        grad_y = grad_gated * silu
        grad_y_low = grad_y.astype(HALF)
        grad_y = grad_y_low.astype(FULL)
        step_pair = halves(step[:, a : a + 1], step[:, b : b + 1], span)
        driven_low = (drive * step_pair).astype(HALF)
        driven = driven_low.astype(FULL)
        grad_rows = stacked_pair(grad_y_low)
        inner = mm_nt(grad_rows, driven_low)
        paired = paired + decay_a * inner[:span] + decay_b * inner[span:]
        mix = jnp.concatenate([(decay_a * scores).astype(HALF), (decay_b * scores).astype(HALF)], 0)
        later = future[:, lanes]
        later_low = later.astype(HALF)
        held_low = states_ref[0, :, lanes]
        reach = mm(inmap, later_low) * weight
        grad_driven = mm_tn(mix, grad_rows) + reach
        weighted = (driven * weight).astype(HALF)
        spread = (grad_y * into).astype(HALF)
        grad_in = grad_in + mm_nt(weighted, later_low)
        grad_out = grad_out + mm_nt(spread, held_low)
        future[:, lanes] = later * keep_old + mm(outmap_t, spread)
        g_ref[:, col.drive[0] + at : col.drive[0] + at + LANES] = (
            step_pair * grad_driven + skip * grad_y
        ).astype(HALF)
        skip_grad_ref[:, lanes] += jnp.sum(grad_y * drive, 0, keepdims=True)
        turn = grad_y * result - driven * grad_driven
        left = lane < HEAD_DIM
        from_drive = drive * grad_driven
        ends = jnp.sum(driven * reach, 0, keepdims=True) + keep_old * jnp.sum(
            later * held_low.astype(FULL), 0, keepdims=True
        )
        for head, mask in ((a, left), (b, ~left)):
            grad_running = grad_running + jnp.where(
                lane == head, jnp.sum(jnp.where(mask, turn, 0.0), 1, keepdims=True), 0.0
            )
            grad_step = grad_step + jnp.where(
                lane == head, jnp.sum(jnp.where(mask, from_drive, 0.0), 1, keepdims=True), 0.0
            )
            grad_last = grad_last + jnp.where(
                head_lane == head, jnp.sum(jnp.where(mask[0:1], ends, 0.0), 1, keepdims=True), 0.0
            )
    paired = paired.astype(HALF)
    grad_out = grad_out + mm(paired, inmap)
    grad_in = grad_in + mm_tn(paired, outmap)
    g_ref[:, col.inmap[0] : col.inmap[1]] = grad_in.astype(HALF)
    g_ref[:, col.outmap[0] : col.outmap[1]] = grad_out.astype(HALF)
    row, column = iota((span, span), 0), iota((span, span), 1)
    grad_keep = (
        jnp.dot((row <= column).astype(FULL), grad_running, precision=PRECISE, preferred_element_type=FULL)
        + grad_last
    )
    grad_raw = (grad_step - grad_keep * jnp.exp(head_ref[0:1, :])) * sigmoid(raw)
    grad_raw = jnp.where(lane < heads, grad_raw, 0.0)
    g_ref[:, col.step[0] : col.step[1]] = grad_raw.astype(HALF)
    g_ref[:, col.step[1] : col.total] = jnp.zeros((span, col.total - col.step[1]), HALF)
    g_ref[:, 0 : col.attention] = ag_ref[...]
    head_grad_ref[0:1, :] += jnp.sum(keep * grad_keep, 0, keepdims=True)
    head_grad_ref[1:2, :] += jnp.sum(grad_raw, 0, keepdims=True)


def scan_backward(
    col, heads, state_size, packed, y, states, grad_mamba, squares, product, gain, segments, head_params, attention_grads
):
    length = packed.shape[0]
    width = heads * HEAD_DIM
    count = length // STRETCH
    back = lambda i: (count - 1 - i, 0)
    return pl.pallas_call(
        functools.partial(scan_backward_kernel, col, heads, MAMBA_HEADS * HEAD_DIM),
        grid=(count,),
        in_specs=[
            pl.BlockSpec((STRETCH, col.total), back),
            pl.BlockSpec((STRETCH, width), back),
            pl.BlockSpec((1, state_size, width), lambda i: (count - 1 - i, 0, 0)),
            pl.BlockSpec((STRETCH, width), back),
            pl.BlockSpec((count, LANES), lambda i: (0, 0)),
            pl.BlockSpec((count, LANES), lambda i: (0, 0)),
            pl.BlockSpec((1, width), lambda i: (0, 0)),
            pl.BlockSpec((STRETCH, 1), back),
            pl.BlockSpec((1, 1, STRETCH), lambda i: (count - 1 - i, 0, 0)),
            pl.BlockSpec((STRETCH, 1), lambda i: (jnp.maximum(count - 2 - i, 0), 0)),
            pl.BlockSpec((8, LANES), lambda i: (0, 0)),
            pl.BlockSpec((STRETCH, col.attention), back),
        ],
        out_specs=[
            pl.BlockSpec((STRETCH, col.total), back),
            pl.BlockSpec((1, width), lambda i: (0, 0)),
            pl.BlockSpec((1, width), lambda i: (0, 0)),
            pl.BlockSpec((8, LANES), lambda i: (0, 0)),
        ],
        out_shape=[
            jax.ShapeDtypeStruct((length, col.total), HALF),
            jax.ShapeDtypeStruct((1, width), FULL),
            jax.ShapeDtypeStruct((1, width), FULL),
            jax.ShapeDtypeStruct((8, LANES), FULL),
        ],
        scratch_shapes=[pltpu.VMEM((state_size, width), FULL)],
        name="scan_backward",
        cost_estimate=pl.CostEstimate(flops=24_000_000_000, bytes_accessed=40_000_000, transcendentals=0),
        compiler_params=pltpu.CompilerParams(vmem_limit_bytes=48 * 2**20),
    )(
        packed, y, states, grad_mamba, squares, product, gain, segments[:, None],
        segments.reshape(count, 1, STRETCH), segments[:, None], head_params, attention_grads,
    )


def turned(values, cosine, sine):
    return values * cosine + pltpu.roll(values, ATT_DIM // 2, 1) * sine


def attend_forward_kernel(
    col, heads, peers, p_ref, cos_ref, sin_ref, segc_ref, segr_ref, own_ref, out_ref, lse_ref, sum_ref, held, sends, receives
):
    length = p_ref.shape[0]
    finish = spread(peers, own_ref, held, sends, receives)
    scale = 1.0 / math.sqrt(ATT_DIM)
    keys = turned(p_ref[:, col.key[0] : col.key[1]], cos_ref[...], sin_ref[...]).astype(HALF)
    values = p_ref[:, col.value[0] : col.value[1]].astype(HALF)
    for block in range(length // ATT_BLOCK):
        rows = slice(block * ATT_BLOCK, (block + 1) * ATT_BLOCK)
        end = (block + 1) * ATT_BLOCK
        place = iota((ATT_BLOCK, end), 0) + block * ATT_BLOCK
        allowed = (place >= iota((ATT_BLOCK, end), 1)) & (segc_ref[rows, :] == segr_ref[:, :end])
        blocked = jnp.where(allowed, 0.0, MASKED)
        for head in range(heads):
            lanes = slice(head * ATT_DIM, (head + 1) * ATT_DIM)
            query = (turned(p_ref[rows, lanes], cos_ref[rows, :], sin_ref[rows, :]) * scale).astype(HALF)
            scores = mm_nt(query, keys[:end]) + blocked
            highest = jnp.max(scores, 1, keepdims=True)
            weights = jnp.exp(scores - highest)
            total = jnp.sum(weights, 1, keepdims=True)
            out_ref[rows, lanes] = (mm(weights.astype(HALF), values[:end]) / total).astype(HALF)
            lse_ref[rows, lanes] = jnp.broadcast_to(highest + jnp.log(total), (ATT_BLOCK, ATT_DIM))
    finish(sum_ref)


def exchange_scratch(peers, shape):
    return [
        pltpu.VMEM((peers,) + shape, FULL),
        pltpu.SemaphoreType.DMA((peers,)),
        pltpu.SemaphoreType.DMA((peers,)),
    ]


def spread(peers, own_ref, held, sends, receives):
    me = lax.axis_index("tensor")
    barrier = pltpu.get_barrier_semaphore()
    others = [lax.rem(me + distance, peers) for distance in range(1, peers)]
    for other in others:
        pl.semaphore_signal(barrier, inc=1, device_id={"tensor": other}, device_id_type=pl.DeviceIdType.MESH)
    pl.semaphore_wait(barrier, peers - 1)

    def copy(distance):
        return pltpu.make_async_remote_copy(
            src_ref=own_ref,
            dst_ref=held.at[distance],
            send_sem=sends.at[distance],
            recv_sem=receives.at[distance],
            device_id={"tensor": others[distance - 1]},
            device_id_type=pl.DeviceIdType.MESH,
        )

    for distance in range(1, peers):
        copy(distance).start()

    def finish(sum_ref):
        sum_ref[...] = own_ref[...]
        for distance in range(1, peers):
            copy(distance).wait()
            sum_ref[...] += held[distance]

    return finish


def attend_forward(col, heads, peers, packed, tables, segments, own):
    length = packed.shape[0]
    whole = lambda i: (0, 0)
    return pl.pallas_call(
        functools.partial(attend_forward_kernel, col, heads, peers),
        grid=(1,),
        in_specs=[
            pl.BlockSpec((length, col.attention), whole),
            pl.BlockSpec((length, ATT_DIM), whole),
            pl.BlockSpec((length, ATT_DIM), whole),
            pl.BlockSpec((length, 1), whole),
            pl.BlockSpec((1, length), whole),
            pl.BlockSpec(own.shape, whole),
        ],
        out_specs=[
            pl.BlockSpec((length, heads * ATT_DIM), whole),
            pl.BlockSpec((length, heads * ATT_DIM), whole),
            pl.BlockSpec(own.shape, whole),
        ],
        out_shape=[
            jax.ShapeDtypeStruct((length, heads * ATT_DIM), HALF),
            jax.ShapeDtypeStruct((length, heads * ATT_DIM), FULL),
            jax.ShapeDtypeStruct(own.shape, FULL),
        ],
        scratch_shapes=exchange_scratch(peers, own.shape),
        name="attend_forward",
        cost_estimate=pl.CostEstimate(flops=6_000_000_000, bytes_accessed=5_000_000, transcendentals=2_000_000),
        compiler_params=pltpu.CompilerParams(
            vmem_limit_bytes=48 * 2**20, collective_id=4, has_side_effects=True
        ),
    )(packed, tables[0], tables[1], segments[:, None], segments[None, :], own)


def attend_backward_kernel(
    col, heads, peers, p_ref, out_ref, lse_ref, go_ref, cos_ref, sin_ref, segc_ref, segr_ref, own_ref, g_ref, sum_ref,
    key_grad, value_grad, held, sends, receives,
):
    length = p_ref.shape[0]
    finish = spread(peers, own_ref, held, sends, receives)
    scale = 1.0 / math.sqrt(ATT_DIM)
    keys = turned(p_ref[:, col.key[0] : col.key[1]], cos_ref[...], sin_ref[...]).astype(HALF)
    values = p_ref[:, col.value[0] : col.value[1]].astype(HALF)
    key_grad[...] = jnp.zeros_like(key_grad)
    value_grad[...] = jnp.zeros_like(value_grad)
    for block in range(length // ATT_BLOCK):
        rows = slice(block * ATT_BLOCK, (block + 1) * ATT_BLOCK)
        end = (block + 1) * ATT_BLOCK
        place = iota((ATT_BLOCK, end), 0) + block * ATT_BLOCK
        allowed = (place >= iota((ATT_BLOCK, end), 1)) & (segc_ref[rows, :] == segr_ref[:, :end])
        blocked = jnp.where(allowed, 0.0, MASKED)
        cosine, sine = cos_ref[rows, :], sin_ref[rows, :]
        for head in range(heads):
            lanes = slice(head * ATT_DIM, (head + 1) * ATT_DIM)
            query = (turned(p_ref[rows, lanes], cosine, sine) * scale).astype(HALF)
            weights = jnp.exp(mm_nt(query, keys[:end]) + blocked - lse_ref[rows, lanes][:, 0:1])
            grad_low = go_ref[rows, lanes].astype(HALF)
            delta = jnp.sum(grad_low.astype(FULL) * out_ref[rows, lanes].astype(FULL), 1, keepdims=True)
            grad_scores = (weights * (mm_nt(grad_low, values[:end]) - delta)).astype(HALF)
            value_grad[:end, :] += mm_tn(weights.astype(HALF), grad_low)
            key_grad[:end, :] += mm_tn(grad_scores, query)
            grad_query = mm(grad_scores, keys[:end]) * scale
            g_ref[rows, lanes] = turned(grad_query, cosine, -sine).astype(HALF)
    g_ref[:, col.key[0] : col.key[1]] = turned(key_grad[...], cos_ref[...], -sin_ref[...]).astype(HALF)
    g_ref[:, col.value[0] : col.value[1]] = value_grad[...].astype(HALF)
    finish(sum_ref)


def attend_backward(col, heads, peers, packed, attended, lse, grad_branches, tables, segments, own):
    length = packed.shape[0]
    width = heads * ATT_DIM
    whole = lambda i: (0, 0)
    return pl.pallas_call(
        functools.partial(attend_backward_kernel, col, heads, peers),
        grid=(1,),
        in_specs=[
            pl.BlockSpec((length, col.attention), whole),
            pl.BlockSpec((length, width), whole),
            pl.BlockSpec((length, width), whole),
            pl.BlockSpec((length, width), lambda i: (0, grad_branches.shape[1] // width - 1)),
            pl.BlockSpec((length, ATT_DIM), whole),
            pl.BlockSpec((length, ATT_DIM), whole),
            pl.BlockSpec((length, 1), whole),
            pl.BlockSpec((1, length), whole),
            pl.BlockSpec(own.shape, whole),
        ],
        out_specs=[pl.BlockSpec((length, col.attention), whole), pl.BlockSpec(own.shape, whole)],
        out_shape=[
            jax.ShapeDtypeStruct((length, col.attention), HALF),
            jax.ShapeDtypeStruct(own.shape, FULL),
        ],
        scratch_shapes=[pltpu.VMEM((length, ATT_DIM), FULL), pltpu.VMEM((length, ATT_DIM), FULL)]
        + exchange_scratch(peers, own.shape),
        name="attend_backward",
        cost_estimate=pl.CostEstimate(flops=8_000_000_000, bytes_accessed=10_000_000, transcendentals=2_000_000),
        compiler_params=pltpu.CompilerParams(
            vmem_limit_bytes=48 * 2**20, collective_id=5, has_side_effects=True
        ),
    )(
        packed, attended, lse, grad_branches, tables[0], tables[1], segments[:, None], segments[None, :], own
    )


def rope_tables(length):
    half = ATT_DIM // 2
    positions = jnp.arange(length, dtype=FULL)
    frequency = ROPE_BASE ** (-jnp.arange(half, dtype=FULL) / half)
    angles = positions[:, None] * frequency[None, :]
    cosine, sine = jnp.cos(angles), jnp.sin(angles)
    return jnp.concatenate([cosine, cosine], 1), jnp.concatenate([-sine, sine], 1)


class Plane:
    def __init__(self, peers, source, whole, sends, receives):
        self.peers, self.source, self.whole = peers, source, whole
        self.sends, self.receives = sends, receives
        self.me = lax.axis_index("dp")
        self.rows = source.shape[0]
        self.width = source.shape[1]
        self.half = self.width // (2 * LANES) * LANES
        outer = [1 << bit for bit in range(1, peers.bit_length() - 1)]
        self.orders = [outer, outer[::-1]]
        self.steps = len(outer)

    def greet(self, barrier):
        for bit in [1] + self.orders[0]:
            pl.semaphore_signal(
                barrier, inc=1, device_id={"dp": self.me ^ bit}, device_id_type=MESH
            )
        return 1 + self.steps

    def held(self, side, step):
        order = self.orders[side]
        if step == 0:
            return [0]
        bit, before = order[step - 1], [0]
        for earlier in order[: step - 1]:
            before = before + [offset ^ earlier for offset in before]
        return [offset ^ bit for offset in before]

    def lanes(self, side):
        return pl.ds(0, self.half) if side == 0 else pl.ds(self.half, self.width - self.half)

    def block(self, side, offset):
        at = pl.ds(pl.multiple_of((self.me ^ offset) * self.rows, 16), self.rows)
        return self.whole.at[at, self.lanes(side)]

    def copy(self, side, bit, offset):
        source = self.source.at[:, self.lanes(side)] if offset == 0 else self.block(side, offset)
        at = (side, bit.bit_length() - 1, offset)
        return pltpu.make_async_remote_copy(
            src_ref=source,
            dst_ref=self.block(side, offset),
            send_sem=self.sends.at[at],
            recv_sem=self.receives.at[at],
            device_id={"dp": self.me ^ bit},
            device_id_type=MESH,
        )

    def arrival(self, side, bit, offset):
        at = (side, bit.bit_length() - 1, offset)
        return pltpu.make_async_remote_copy(
            src_ref=self.block(side, offset ^ bit),
            dst_ref=self.block(side, offset ^ bit),
            send_sem=self.sends.at[at],
            recv_sem=self.receives.at[at],
            device_id={"dp": self.me ^ bit},
            device_id_type=MESH,
        )

    def sent(self, side, step):
        blocks = []
        for earlier in range(step):
            blocks += self.held(side, earlier)
        return blocks

    def start(self):
        for side in (0, 1):
            if self.steps:
                self.copy(side, self.orders[side][0], 0).start()
        for side in (0, 1):
            self.copy(side, 1, 0).start()

    def advance(self, step):
        for side in (0, 1):
            bit = self.orders[side][step - 1]
            for offset in self.held(side, step):
                self.arrival(side, bit, offset ^ bit).wait_recv()
        for side in (0, 1):
            if step < self.steps:
                following = self.orders[side][step]
                for offset in self.sent(side, step + 1):
                    self.copy(side, following, offset).start()
        for side in (0, 1):
            for offset in self.held(side, step):
                self.copy(side, 1, offset).start()

    def finish(self):
        for side in (0, 1):
            for offset in self.sent(side, self.steps + 1):
                self.arrival(side, 1, offset).wait_recv()

    def drain(self):
        for side in (0, 1):
            for offset in self.sent(side, self.steps + 1):
                self.copy(side, 1, offset).wait_send()
            for step in range(1, self.steps + 1):
                for offset in self.sent(side, step):
                    self.copy(side, self.orders[side][step - 1], offset).wait_send()


class Swarm:
    def __init__(self, peers, count):
        self.peers, self.count = peers, count
        self.at_dp, self.at_tensor = lax.axis_index("dp"), lax.axis_index("tensor")

    def greet(self):
        barrier = pltpu.get_barrier_semaphore()
        for offset in range(1, self.peers):
            pl.semaphore_signal(barrier, inc=1, device_id={"dp": self.at_dp ^ offset}, device_id_type=MESH)
        for distance in range(1, self.count):
            pl.semaphore_signal(
                barrier, inc=1, device_id={"tensor": lax.rem(self.at_tensor + distance, self.count)}, device_id_type=MESH
            )
        pl.semaphore_wait(barrier, self.peers + self.count - 2)

    def along_dp(self, source_of, held, sends, receives):
        return [
            pltpu.make_async_remote_copy(
                src_ref=source_of(self.at_dp ^ offset),
                dst_ref=held.at[offset],
                send_sem=sends.at[offset],
                recv_sem=receives.at[offset],
                device_id={"dp": self.at_dp ^ offset},
                device_id_type=MESH,
            )
            for offset in range(1, self.peers)
        ]

    def along_tensor(self, source, held, sends, receives):
        return [
            pltpu.make_async_remote_copy(
                src_ref=source,
                dst_ref=held.at[distance],
                send_sem=sends.at[distance],
                recv_sem=receives.at[distance],
                device_id={"tensor": lax.rem(self.at_tensor + distance, self.count)},
                device_id_type=MESH,
            )
            for distance in range(1, self.count)
        ]


def plane_semaphores(peers):
    return [pltpu.SemaphoreType.DMA((2, max(peers.bit_length() - 1, 1), peers))] * 2


MESH = pl.DeviceIdType.MESH
TILE = 256
WIDE = 512


class Line:
    def __init__(self, count):
        self.count = count
        self.me = lax.axis_index("tensor")
        self.has_left = self.me > 0
        self.has_right = self.me < count - 1

    def greet(self, plane=None):
        barrier = pltpu.get_barrier_semaphore()
        extra = 0 if plane is None else plane.greet(barrier)
        for present, shift in ((self.has_left, -1), (self.has_right, 1)):

            @pl.when(present)
            def _():
                pl.semaphore_signal(
                    barrier, inc=1, device_id={"tensor": self.me + shift}, device_id_type=MESH
                )

        inside = self.has_left & self.has_right

        @pl.when(inside)
        def _():
            pl.semaphore_wait(barrier, 2 + extra)

        @pl.when(jnp.logical_not(inside))
        def _():
            pl.semaphore_wait(barrier, 1 + extra)

    def copy(self, source, target, sends, receives, at, side):
        return pltpu.make_async_remote_copy(
            src_ref=source,
            dst_ref=target,
            send_sem=sends.at[at],
            recv_sem=receives.at[at],
            device_id={"tensor": self.me + (1 if side == 0 else -1)},
            device_id_type=MESH,
        )

    def place(self, side):
        return self.me if side == 0 else self.count - 1 - self.me

    def ahead(self, side, distance):
        return self.me + distance if side == 0 else self.me - distance

    def next_there(self, side):
        return self.has_right if side == 0 else self.has_left

    def last_there(self, side):
        return self.has_left if side == 0 else self.has_right


class Scatter:
    def __init__(self, line, parts, rows, span, slots, sends, receives):
        self.line, self.parts, self.rows, self.span = line, parts, rows, span
        self.slots, self.sends, self.receives = slots, sends, receives

    def own(self, owner, chunk):
        return self.parts.at[pl.ds(pl.multiple_of(owner * self.rows + chunk * self.span, 16), self.span), :]

    def transfer(self, side, chunk, hop, source=None):
        target = self.slots.at[side, chunk, hop - 1]
        return self.line.copy(
            target if source is None else source, target, self.sends, self.receives, (side, chunk, hop - 1), side
        )

    def hop(self, chunk, hop):
        line = self.line
        for side in (0, 1):
            place = line.place(side)
            owner = line.ahead(side, line.count - hop)

            @pl.when(place == 0)
            def _():
                self.transfer(side, chunk, hop, self.own(owner, chunk)).start()

            if hop > 1:

                @pl.when((place > 0) & (place <= hop - 1))
                def _():
                    slot = self.slots.at[side, chunk, hop - 2]
                    self.transfer(side, chunk, hop - 1).wait_recv()
                    slot[...] = (slot[...].astype(FULL) + self.own(owner, chunk)[...].astype(FULL)).astype(slot.dtype)
                    self.transfer(side, chunk, hop, slot).start()

    def finish(self, chunk, total):
        line = self.line
        total[...] = self.own(line.me, chunk)[...].astype(FULL)
        last = line.count - 1
        for side in (0, 1):

            @pl.when(line.last_there(side))
            def _():
                self.transfer(side, chunk, last).wait_recv()
                total[...] += self.slots[side, chunk, last - 1].astype(FULL)

    def drain(self, chunk):
        for hop in range(1, self.line.count):
            for side in (0, 1):

                @pl.when(self.line.place(side) <= hop - 1)
                def _():
                    self.transfer(side, chunk, hop).wait_send()


class Gather:
    def __init__(self, line, whole, rows, span, sends, receives):
        self.line, self.whole, self.rows, self.span = line, whole, rows, span
        self.sends, self.receives = sends, receives

    def at(self, owner, chunk):
        return self.whole.at[pl.ds(pl.multiple_of(owner * self.rows + chunk * self.span, 16), self.span), :]

    def transfer(self, side, chunk, hop):
        piece = self.at(self.line.ahead(1 - side, hop - 1), chunk)
        return self.line.copy(piece, piece, self.sends, self.receives, (side, chunk, hop - 1), side)

    def arrival(self, side, chunk, hop):
        piece = self.at(self.line.ahead(1 - side, hop), chunk)
        return self.line.copy(piece, piece, self.sends, self.receives, (side, chunk, hop - 1), side)

    def send(self, chunk, hop):
        line = self.line
        for side in (0, 1):

            @pl.when(line.next_there(side) & (line.place(side) >= hop - 1))
            def _():
                self.transfer(side, chunk, hop).start()

    def receive(self, chunk, hop):
        line = self.line
        for side in (0, 1):

            @pl.when(line.place(side) >= hop)
            def _():
                self.arrival(side, chunk, hop).wait_recv()

    def step(self, chunk, hop):
        line = self.line
        for side in (0, 1):

            @pl.when(line.place(side) >= hop)
            def _():
                self.arrival(side, chunk, hop).wait_recv()

            if hop < line.count - 1:

                @pl.when(line.next_there(side) & (line.place(side) >= hop))
                def _():
                    self.transfer(side, chunk, hop + 1).start()

    def drain(self, chunk):
        line = self.line
        for hop in range(1, line.count):
            for side in (0, 1):

                @pl.when(line.next_there(side) & (line.place(side) >= hop - 1))
                def _():
                    self.transfer(side, chunk, hop).wait_send()


def project(line, left, right, parts, rows, forward):
    upper = line.me < line.count // 2
    far = jnp.where(upper, line.count - 1, 0) * rows
    rest = jnp.where(upper, 0, 1) * rows

    def block(start, size):
        at = pl.ds(pl.multiple_of(start, 16), size)

        def tile(index, carry):
            lanes = pl.ds(pl.multiple_of(index * TILE, TILE), TILE)
            if forward:
                parts[at, lanes] = mm(left[at, :], right[:, lanes]).astype(parts.dtype)
            else:
                parts[at, lanes] = mm_nt(left[at, :], right[lanes, : left.shape[1]]).astype(parts.dtype)
            return carry

        lax.fori_loop(0, parts.shape[1] // TILE, tile, 0)

    return (lambda: block(far, rows)), (lambda: block(rest, (line.count - 1) * rows))


def relay(line, scatter, gather, chunks, lag, rows_done, first=None, second=None, events=None, received=None):
    last = line.count - 1
    if first is not None:
        first()
    turns = lag * (chunks - 1) + last + 1 + (0 if gather is None else last)
    for turn in range(turns):
        arrived = []
        for chunk in range(chunks):
            hop = turn - lag * chunk + 1
            if 1 <= hop <= last:
                scatter.hop(chunk, hop)
            elif hop == last + 1:
                rows_done(chunk)
                if gather is not None:
                    gather.send(chunk, 1)
            elif gather is not None and last + 1 < hop <= 2 * last + 1:
                gather.step(chunk, hop - last - 1)
                if hop == 2 * last + 1:
                    arrived.append(chunk)
        if turn == 0 and second is not None:
            second()
        if events is not None and turn in events:
            events[turn]()
        if received is not None:
            for chunk in arrived:
                scatter.drain(chunk)
                received(chunk)
    for chunk in range(chunks):
        if received is None:
            scatter.drain(chunk)
        if gather is not None:
            gather.drain(chunk)


def norm_below(value, above, gain):
    inverse = lax.rsqrt(jnp.mean(value * value, -1, keepdims=True) + EPSILON)
    plain = value * inverse
    scaled = above * gain
    below = inverse * (scaled - plain * jnp.mean(scaled * plain, -1, keepdims=True))
    return below, jnp.sum(above * plain, 0, keepdims=True)


def ffn_kernel(
    count, peers, chunks, lag, rows, units,
    left, right, hidden, gain, cot_rows, local_weight,
    out, activated, grad_gate, parts, out_parts, middle,
    weight, slots, total, part_rows, part_cot, part_gate, part_act, own_sem, s0, s1, s2, s3, p0, p1,
):
    line = Line(count)
    span = rows // chunks
    features = hidden.shape[1]
    plane = Plane(peers, local_weight, weight, p0, p1)
    keep_weight = pltpu.make_async_copy(
        local_weight, weight.at[pl.ds(pl.multiple_of(plane.me * plane.rows, 16), plane.rows), :], own_sem
    )
    keep_weight.start()
    line.greet(plane)
    plane.start()
    scatter = Scatter(line, parts, rows, span, slots, s0, s1)
    gather = Gather(line, out, rows, span, s2, s3)

    def rows_done(chunk):
        at = pl.ds(chunk * span, span)
        scatter.finish(chunk, total)
        value = total[...] + hidden[at, :].astype(FULL)
        middle[at, :] = value
        inverse = lax.rsqrt(jnp.mean(value * value, -1, keepdims=True) + EPSILON)
        gather.at(line.me, chunk)[...] = (value * inverse * gain[...]).astype(HALF)

    def received(chunk):
        if chunk == 0:
            plane.finish()
            keep_weight.wait()
        here = [pl.ds(owner * rows + chunk * span, span) for owner in range(count)]
        there = [slice(owner * span, (owner + 1) * span) for owner in range(count)]
        for source, target in zip(here, there):
            part_rows[target, :] = out[source, :]
            part_cot[target, :] = cot_rows[source, :]

        def gates(index, carry):
            lanes = pl.ds(pl.multiple_of(index * WIDE, WIDE), WIDE)
            upper = pl.ds(pl.multiple_of(units + index * WIDE, WIDE), WIDE)
            lower = pl.ds(pl.multiple_of(2 * units + index * WIDE, WIDE), WIDE)
            gate = mm(part_rows[...], weight[:, lanes])
            up = mm(part_rows[...], weight[:, upper])
            grad_act = mm(part_cot[...], weight[:, lower])
            sig = sigmoid(gate)
            silu = gate * sig
            act = (silu * up).astype(HALF)
            grad_one = (grad_act * up * (sig * (1.0 + gate * (1.0 - sig)))).astype(HALF)
            grad_two = (grad_act * silu).astype(HALF)
            part_gate[:, lanes] = grad_one
            part_gate[:, upper] = grad_two
            part_act[:, lanes] = act
            for source, target in zip(there, here):
                activated[target, lanes] = act[source, :]
                grad_gate[target, lanes] = grad_one[source, :]
                grad_gate[target, upper] = grad_two[source, :]
            return carry

        lax.fori_loop(0, units // WIDE, gates, 0)

        def back(index, carry):
            lanes = pl.ds(pl.multiple_of(index * WIDE, WIDE), WIDE)
            result = mm_nt(part_gate[...], weight[lanes, : 2 * units]).astype(parts.dtype)
            for source, target in zip(there, here):
                parts[target, lanes] = result[source, :]
            result = mm_nt(part_act[...], weight[lanes, 2 * units :]).astype(out_parts.dtype)
            for source, target in zip(there, here):
                out_parts[target, lanes] = result[source, :]
            return carry

        lax.fori_loop(0, features // WIDE, back, 0)

    last = count - 1
    events = {}
    for step in range(1, plane.steps + 1):
        events[min(2 + 3 * (step - 1), 2 * last - 1 - (plane.steps - step))] = functools.partial(plane.advance, step)
    first, second = project(line, left, right, parts, rows, True)
    relay(line, scatter, gather, chunks, lag, rows_done, first, second, events, received)
    plane.drain()


def ffn_rows_call(count, peers, chunks, lag, branches, weight_out, hidden, gain, cot_rows, local_weight):
    rows, features = hidden.shape
    length = count * rows
    units = local_weight.shape[1] // 3
    span = rows // chunks
    vmem = pl.BlockSpec(memory_space=pltpu.VMEM)
    return pl.pallas_call(
        functools.partial(ffn_kernel, count, peers, chunks, lag, rows, units),
        in_specs=[vmem] * 5 + [pl.BlockSpec(memory_space=pl.ANY)],
        out_specs=[vmem] * 6,
        out_shape=[
            jax.ShapeDtypeStruct((length, features), HALF),
            jax.ShapeDtypeStruct((length, units), HALF),
            jax.ShapeDtypeStruct((length, 2 * units), HALF),
            jax.ShapeDtypeStruct((length, features), HALF),
            jax.ShapeDtypeStruct((length, features), HALF),
            jax.ShapeDtypeStruct((rows, features), FULL),
        ],
        scratch_shapes=[
            pltpu.VMEM((peers * local_weight.shape[0], 3 * units), HALF),
            pltpu.VMEM((2, chunks, count - 1, span, features), HALF),
            pltpu.VMEM((span, features), FULL),
            pltpu.VMEM((count * span, features), HALF),
            pltpu.VMEM((count * span, features), HALF),
            pltpu.VMEM((count * span, 2 * units), HALF),
            pltpu.VMEM((count * span, units), HALF),
            pltpu.SemaphoreType.DMA(()),
        ]
        + [pltpu.SemaphoreType.DMA((2, chunks, count - 1))] * 4
        + plane_semaphores(peers),
        name="ffn_rows",
        cost_estimate=pl.CostEstimate(flops=150_000_000_000, bytes_accessed=40_000_000, transcendentals=0),
        compiler_params=pltpu.CompilerParams(
            collective_id=1, has_side_effects=True, vmem_limit_bytes=61 * 2**20
        ),
    )(branches, weight_out, hidden, gain, cot_rows, local_weight)


def entry_kernel(
    count, peers, rows, own, gains, query, keyval, mamba, state, step, kv_lanes,
    out, weight, all_gains, raw, local, held, own_sems, s0, s1, p0, p1, g0, g1,
):
    line = Line(count)
    swarm = Swarm(peers, count)
    plane = Plane(peers, local, weight, p0, p1)
    block = gains.shape[1]
    keep = pltpu.make_async_copy(own, raw.at[pl.ds(pl.multiple_of(line.me * rows, 16), rows), :], own_sems.at[0])
    keep.start()
    swarm.greet()
    keep.wait()
    gather = Gather(line, raw, rows, rows, s0, s1)
    gather.send(0, 1)
    sent = swarm.along_dp(lambda device: gains, held, g0, g1)
    for copy in sent:
        copy.start()
    start = 0
    shared = pl.ds(pl.multiple_of(kv_lanes(line.me), ATT_DIM), ATT_DIM)
    for part in (query[...], keyval[:, 0, shared], keyval[:, 1, shared], mamba[:, 0, :], mamba[:, 1, :],
                 state[:, 0, :], state[:, 1, :], step[...]):
        local[:, start : start + part.shape[1]] = part
        start += part.shape[1]
    keep_weight = pltpu.make_async_copy(
        local, weight.at[pl.ds(pl.multiple_of(plane.me * plane.rows, 16), plane.rows), :], own_sems.at[1]
    )
    keep_weight.start()
    plane.start()
    held[0] = gains[...]
    for copy in sent:
        copy.wait()
    for offset in range(peers):
        lanes = pl.ds(pl.multiple_of((swarm.at_dp ^ offset) * block, block), block)
        all_gains[:, lanes] = held[offset]

    def normed(owner):
        at = pl.ds(pl.multiple_of(owner * rows, 16), rows)
        value = raw[at, :].astype(FULL)
        inverse = lax.rsqrt(jnp.mean(value * value, -1, keepdims=True) + EPSILON)
        out[at, :] = (value * inverse * all_gains[0:1, :]).astype(HALF)

    normed(line.me)
    for hop in range(1, count):
        gather.step(0, hop)
        if hop <= plane.steps:
            plane.advance(hop)
        for side in (0, 1):

            @pl.when(line.place(side) >= hop)
            def _():
                normed(line.ahead(1 - side, hop))

    for extra in range(count, plane.steps + 1):
        plane.advance(extra)
    plane.finish()
    gather.drain(0)
    plane.drain()
    keep_weight.wait()


def entry(count, peers, own, gains, query, keyval, mamba, state, step, kv_lanes):
    rows, features = own.shape
    block = query.shape[0]
    total = query.shape[1] + 2 * ATT_DIM + 2 * mamba.shape[2] + 2 * state.shape[2] + step.shape[1]
    vmem, anywhere = pl.BlockSpec(memory_space=pltpu.VMEM), pl.BlockSpec(memory_space=pl.ANY)
    return pl.pallas_call(
        lambda *refs: entry_kernel(count, peers, rows, *refs[:7], kv_lanes, *refs[7:]),
        in_specs=[vmem] * 7,
        out_specs=[vmem, anywhere, vmem],
        out_shape=[
            jax.ShapeDtypeStruct((count * rows, features), own.dtype),
            jax.ShapeDtypeStruct((peers * block, total), HALF),
            jax.ShapeDtypeStruct((gains.shape[0], peers * block), FULL),
        ],
        scratch_shapes=[
            pltpu.VMEM((count * rows, features), HALF),
            pltpu.VMEM((block, total), HALF),
            pltpu.VMEM((peers,) + gains.shape, FULL),
            pltpu.SemaphoreType.DMA((2,)),
        ]
        + [pltpu.SemaphoreType.DMA((2, 1, count - 1))] * 2
        + plane_semaphores(peers)
        + [pltpu.SemaphoreType.DMA((peers,))] * 2,
        name="entry",
        cost_estimate=pl.CostEstimate(flops=80_000_000_000, bytes_accessed=20_000_000, transcendentals=0),
        compiler_params=pltpu.CompilerParams(
            collective_id=0, has_side_effects=True, vmem_limit_bytes=48 * 2**20
        ),
    )(own, gains, query, keyval, mamba, state, step)


class Fold:
    def __init__(self, peers, chunks, product, parts, held, store, sends, receives, early=()):
        self.me, self.early = lax.axis_index("dp"), list(early)
        self.peers, self.chunks = peers, chunks
        self.product, self.parts, self.held, self.store = product, parts, held, store
        self.sends, self.receives = sends, receives
        outer = [1 << bit for bit in range(1, peers.bit_length() - 1)]
        self.orders = [[1] + outer, [1] + outer[::-1]]
        self.stages = len(outer) + 2
        self.turns = chunks + 2 * (self.stages - 1)

    def greet(self, barrier):
        for bit in self.orders[0]:
            pl.semaphore_signal(
                barrier, inc=1, device_id={"dp": self.me ^ bit}, device_id_type=MESH
            )
        return len(self.orders[0])

    def column(self, chunk):
        result = chunk
        table = self.early + [at for at in range(self.chunks) if at not in self.early]
        for place, at in enumerate(table):
            if place != at:
                result = jnp.where(chunk == place, at, result)
        return result

    def kept(self, order, step):
        mask = sum(order[:step])
        return [offset for offset in range(self.peers) if not offset & mask]

    def copies(self, parity, chunk, step):
        order = self.orders[parity]
        bit = order[step]
        mine, next_kept = self.kept(order, step), self.kept(order, step + 1)
        result = []
        for offset in mine:
            if offset & bit:
                if step == 0:
                    source = self.parts.at[lax.rem(chunk, 3), self.me ^ offset]
                else:
                    source = self.held[step - 1].at[chunk, mine.index(offset)]
                place = next_kept.index(offset ^ bit)
                result.append(
                    pltpu.make_async_remote_copy(
                        src_ref=source,
                        dst_ref=self.held[step].at[chunk, place],
                        send_sem=self.sends[step].at[chunk, place],
                        recv_sem=self.receives[step].at[chunk, place],
                        device_id={"dp": self.me ^ bit},
                        device_id_type=MESH,
                    )
                )
        return result

    def stage(self, number, parity, chunk):
        order = self.orders[parity]
        if number == 0:
            self.product(self.column(chunk), self.parts.at[lax.rem(chunk, 3)])
        else:
            step = number - 1
            copies = self.copies(parity, chunk, step)
            for copy in copies:
                copy.wait_recv()
            mine, left = self.kept(order, step), self.kept(order, step + 1)
            for place, offset in enumerate(left):
                if step == 0:
                    own = self.parts[lax.rem(chunk, 3), self.me ^ offset]
                else:
                    own = self.held[step - 1][chunk, mine.index(offset)]
                value = own.astype(FULL) + self.held[step][chunk, place].astype(FULL)
                if number == self.stages - 1:
                    column = self.column(chunk)
                    for at in range(self.chunks):

                        @pl.when(column == at)
                        def _():
                            self.store(at, value)

                else:
                    self.held[step][chunk, place] = value.astype(HALF)
            if step == 0:
                for copy in copies:
                    copy.wait_send()
        if number < self.stages - 1:
            for copy in self.copies(parity, chunk, number):
                copy.start()

    def run(self, first, last):
        def pair(index, carry):
            for odd in (0, 1):
                turn = 2 * index + odd
                for number in reversed(range(self.stages)):
                    chunk = turn - 2 * number

                    @pl.when((chunk >= 0) & (chunk < self.chunks))
                    def _():
                        self.stage(number, odd, chunk)

            return carry

        lax.fori_loop(first // 2, last // 2, pair, 0)

    def drain(self):
        def pair(index, carry):
            for odd in (0, 1):
                chunk = 2 * index + odd

                @pl.when(chunk < self.chunks)
                def _():
                    for step in range(1, self.stages - 1):
                        for copy in self.copies(odd, chunk, step):
                            copy.wait_send()

            return carry

        lax.fori_loop(0, (self.chunks + 1) // 2, pair, 0)


def fold_scratch(peers, chunks, rows, width):
    steps = peers.bit_length() - 1
    sizes = [peers >> (step + 1) for step in range(steps)]
    return (
        [pltpu.VMEM((3, peers, rows, width), HALF)]
        + [pltpu.VMEM((chunks, size, rows, width), HALF) for size in sizes]
        + [pltpu.SemaphoreType.DMA((chunks, size)) for size in sizes] * 2
    )


def final_kernel(
    count, peers, chunks, rows, kv_owner, col, heads, width,
    left, weight_in, hidden, grad_middle, gain, ffn_gain_grad, head_rows, sequence, grad_mixed, branches,
    out, gain_out, head_out, query_out, inner_out, step_out, state_out, keyval_out, mamba_out, attn_out,
    parts, total, slots, gain_rows, held_heads, held_dp, held_tensor, gain_sum, tiles, gathered, fold_parts, *rest,
):
    steps = peers.bit_length() - 1
    held, fold_sends, fold_receives = rest[:steps], rest[steps : 2 * steps], rest[2 * steps : 3 * steps]
    s0, s1, h0, h1, d0, d1, t0, t1, tile_sems, a0, a1 = rest[3 * steps :]
    line = Line(count)
    swarm = Swarm(peers, count)
    span = rows // chunks
    block = gain_out.shape[1]
    first_chunks = left.shape[1] // width
    fold_chunks = first_chunks + branches.shape[1] // width
    swarm.greet()
    heads_sent = swarm.along_dp(lambda device: head_rows, held_heads, h0, h1)
    for copy in heads_sent:
        copy.start()
    scatter = Scatter(line, parts, rows, span, slots, s0, s1)
    gain_rows[...] = jnp.zeros_like(gain_rows)
    gain_rows[1:2, :] = ffn_gain_grad[...]

    def rows_done(chunk):
        at = pl.ds(chunk * span, span)
        scatter.finish(chunk, total)
        value = hidden[at, :].astype(FULL)
        below, part = norm_below(value, total[...], gain[...])
        gain_rows[0:1, :] += part
        out[at, :] = grad_middle[at, :] + below

    upper = line.me < line.count // 2
    pieces = parts.shape[1] // TILE

    def fetch(index):
        slot = index % 2
        return pltpu.make_async_copy(
            weight_in.at[index * TILE : (index + 1) * TILE, :], tiles.at[slot], tile_sems.at[slot]
        )

    def project_tile(start, size, index, following):
        at = pl.ds(pl.multiple_of(start, 16), size)
        if following is not None:
            fetch(following).start()
        fetch(index).wait()
        parts[at, index * TILE : (index + 1) * TILE] = mm_nt(left[at, :], tiles[index % 2]).astype(parts.dtype)

    def product(column, target):
        def fill(grad_left, grad_right, index):
            lanes = pl.ds(pl.multiple_of(index * width, width), width)
            target[...] = mm_tn(grad_left[...], grad_right[:, lanes]).astype(HALF).reshape(target.shape)

        @pl.when(column < first_chunks)
        def _():
            fill(sequence, left, column)

        @pl.when(column >= first_chunks)
        def _():
            fill(grad_mixed, branches, column - first_chunks)

    shared = (col.key, col.value, col.inmap, col.outmap)
    own_rows = pl.ds(pl.multiple_of(line.me * block, block), block)

    def store(at, value):
        for piece in range(0, width, LANES):
            begin = at * width + piece
            part = value[:, piece : piece + LANES]
            place = 0
            for start, end in shared:
                if start <= begin < end:
                    gathered[own_rows, place + begin - start : place + begin - start + LANES] = part.astype(HALF)
                place += end - start
            if begin < col.query[1]:
                query_out[:, begin : begin + LANES] = part
            for index, (start, end) in enumerate((col.gate, col.drive)):
                if start <= begin < end:
                    inner_out[:, index, begin - start : begin - start + LANES] = part
            if begin == col.step[0]:
                step_out[...] = part[:, :heads]
            if begin >= col.total:
                turned_part = part.T
                begin -= col.total
                if begin < mamba_out.shape[0]:
                    mamba_out[begin : begin + LANES, :] = turned_part
                else:
                    begin -= mamba_out.shape[0]
                    attn_out[begin : begin + LANES, :] = turned_part

    early = sorted({at for begin, end in shared for at in range(begin // width, (end - 1) // width + 1)})
    fold = Fold(peers, fold_chunks, product, fold_parts, held, store, fold_sends, fold_receives, early)
    gather = Gather(line, gathered, block, block, a0, a1)
    gains = []

    def send_gains():
        gains.extend(
            swarm.along_dp(
                lambda device: gain_rows.at[:, pl.ds(pl.multiple_of(device * block, block), block)], held_dp, d0, d1
            )
        )
        for copy in gains:
            copy.start()

    far, others = jnp.where(upper, count - 1, 0) * rows, jnp.where(upper, 0, 1) * rows
    fetch(0).start()
    for index in range(pieces):
        project_tile(far, rows, index, (index + 1) % pieces)
    for chunk in range(chunks):
        scatter.hop(chunk, 1)

    def project_others(first, last):
        for index in range(first, last):
            project_tile(others, (count - 1) * rows, index, index + 1 if index + 1 < pieces else None)

    turns = fold.turns + fold.turns % 2
    early_done = len(early) + 2 * (fold.stages - 1)
    early_done += early_done % 2
    half = pieces // 2
    line_steps = [functools.partial(project_others, 0, half), functools.partial(project_others, half, pieces)]
    line_steps += [functools.partial(scatter.hop, chunk, hop) for hop in range(2, count) for chunk in range(chunks)]
    line_steps += [functools.partial(rows_done, chunk) for chunk in range(chunks)] + [send_gains]
    early_steps = [lambda: gather.send(0, 1)] + [functools.partial(gather.step, 0, hop) for hop in range(1, count)]
    for done in range(2, turns + 2, 2):
        fold.run(done - 2, done)
        if line_steps:
            line_steps.pop(0)()
        if done >= early_done and early_steps and (done - early_done) % 4 == 0:
            early_steps.pop(0)()
    for step in line_steps + early_steps:
        step()
    head_out[...] = head_rows[...]
    for offset, copy in enumerate(heads_sent):
        copy.wait()
        head_out[...] += held_heads[offset + 1]
    gain_sum[...] = gain_rows[:, pl.ds(pl.multiple_of(swarm.at_dp * block, block), block)]
    for offset, copy in enumerate(gains):
        copy.wait()
        gain_sum[...] += held_dp[offset + 1]
    last_sent = swarm.along_tensor(gain_sum, held_tensor, t0, t1)
    for copy in last_sent:
        copy.start()
    pair = 2 * ATT_DIM
    state = (gathered.shape[1] - pair) // 2
    for part in range(2):
        lanes = slice(pair + part * state, pair + (part + 1) * state)
        whole = gathered[0:block, lanes].astype(FULL)
        for owner in range(1, count):
            whole = whole + gathered[owner * block : (owner + 1) * block, lanes].astype(FULL)
        state_out[:, part, :] = whole
    for head in range(KV_HEADS):
        for part in range(2):
            lanes = slice(part * ATT_DIM, (part + 1) * ATT_DIM)
            value = jnp.zeros((block, ATT_DIM), FULL)
            for owner in range(count):
                if kv_owner(owner) == head:
                    value = value + gathered[owner * block : (owner + 1) * block, lanes].astype(FULL)
            keyval_out[:, part, head * ATT_DIM : (head + 1) * ATT_DIM] = value
    gain_out[...] = gain_sum[...]
    for distance, copy in enumerate(last_sent):
        copy.wait()
        gain_out[...] += held_tensor[distance + 1]
    for chunk in range(chunks):
        scatter.drain(chunk)
    gather.drain(0)
    fold.drain()


def final_rows(
    count, peers, chunks, kv_owner, col, heads, width, grads, weight_in, hidden, grad_middle, gain, ffn_gain_grad,
    head_rows, sequence, grad_mixed, branches,
):
    rows, features = hidden.shape
    span = rows // chunks
    block = features // peers
    one, two = grads.shape[1], branches.shape[1]
    tile = 256 if one % 256 == 0 and two % 256 == 0 else 128
    fold_chunks = (one + two) // tile
    vmem = pl.BlockSpec(memory_space=pltpu.VMEM)
    state = col.inmap[1] - col.inmap[0]
    operands = (
        grads, weight_in, hidden, grad_middle, gain, ffn_gain_grad, head_rows, sequence, grad_mixed, branches
    )
    outputs = [
        (rows, features),
        (8, block),
        head_rows.shape,
        (block, col.query[1]),
        (block, 2, width),
        (block, heads),
        (block, 2, state),
        (block, 2, KV_HEADS * ATT_DIM),
        (width, block),
        (two - width, block),
    ]
    return pl.pallas_call(
        functools.partial(final_kernel, count, peers, chunks, rows, kv_owner, col, heads, tile),
        in_specs=[vmem, pl.BlockSpec(memory_space=pl.ANY)] + [vmem] * (len(operands) - 2),
        out_specs=[vmem] * len(outputs),
        out_shape=[jax.ShapeDtypeStruct(shape, FULL) for shape in outputs],
        scratch_shapes=[
            pltpu.VMEM((count * rows, features), HALF),
            pltpu.VMEM((span, features), FULL),
            pltpu.VMEM((2, chunks, count - 1, span, features), HALF),
            pltpu.VMEM((8, features), FULL),
            pltpu.VMEM((peers,) + head_rows.shape, FULL),
            pltpu.VMEM((peers, 8, block), FULL),
            pltpu.VMEM((count, 8, block), FULL),
            pltpu.VMEM((8, block), FULL),
            pltpu.VMEM((2, TILE, one), HALF),
            pltpu.VMEM((count * block, 2 * (ATT_DIM + state)), HALF),
        ]
        + fold_scratch(peers, fold_chunks, block, tile)
        + [pltpu.SemaphoreType.DMA((2, chunks, count - 1))] * 2
        + [pltpu.SemaphoreType.DMA((peers,))] * 4
        + [pltpu.SemaphoreType.DMA((count,))] * 2
        + [pltpu.SemaphoreType.DMA((2,))]
        + [pltpu.SemaphoreType.DMA((2, 1, count - 1))] * 2,
        name="final_rows",
        cost_estimate=pl.CostEstimate(flops=80_000_000_000, bytes_accessed=20_000_000, transcendentals=0),
        compiler_params=pltpu.CompilerParams(
            collective_id=3, has_side_effects=True, vmem_limit_bytes=62 * 2**20
        ),
    )(*operands)


def ffn_grad_kernel(
    count, peers, chunks, lag, rows, width,
    parts, middle, cotangent, gain, ffn_rows, grad_gate, cot_rows, activated,
    out, grad_middle, gain_grad, up_out, down_out,
    total, slots, fold_parts, *rest,
):
    steps = peers.bit_length() - 1
    held, fold_sends, fold_receives = rest[:steps], rest[steps : 2 * steps], rest[2 * steps : 3 * steps]
    s0, s1, s2, s3 = rest[3 * steps :]
    line = Line(count)
    span = rows // chunks
    units = activated.shape[1]
    first_chunks = 2 * units // width

    def product(column, target):
        def fill(grad_left, grad_right, index):
            lanes = pl.ds(pl.multiple_of(index * width, width), width)
            target[...] = mm_tn(grad_left[...], grad_right[:, lanes]).astype(HALF).reshape(target.shape)

        @pl.when(column < first_chunks)
        def _():
            fill(ffn_rows, grad_gate, column)

        @pl.when(column >= first_chunks)
        def _():
            fill(cot_rows, activated, column - first_chunks)

    def store(at, value):
        begin = at * width
        if begin < 2 * units:
            up_out[:, begin // units, begin % units : begin % units + width] = value
        else:
            down_out[begin - 2 * units : begin - 2 * units + width, :] = value.T

    fold = Fold(peers, 3 * units // width, product, fold_parts, held, store, fold_sends, fold_receives)
    line.greet(fold)
    scatter = Scatter(line, parts, rows, span, slots, s0, s1)
    gather = Gather(line, out, rows, span, s2, s3)
    gain_grad[...] = jnp.zeros_like(gain_grad)

    def rows_done(chunk):
        at = pl.ds(chunk * span, span)
        scatter.finish(chunk, total)
        below, part = norm_below(middle[at, :], total[...], gain[...])
        gain_grad[...] += part
        result = cotangent[at, :].astype(FULL) + below
        grad_middle[at, :] = result
        gather.at(line.me, chunk)[...] = result.astype(HALF)

    turns = lag * (chunks - 1) + 2 * (count - 1) + 1
    pairs = (fold.turns + 1) // 2
    ends = [min(pairs, -(-pairs * (turn + 1) // (turns - 2))) for turn in range(turns)]
    events = {
        turn: functools.partial(fold.run, 2 * (ends[turn - 1] if turn else 0), 2 * ends[turn]) for turn in range(turns)
    }
    relay(line, scatter, gather, chunks, lag, rows_done, events=events)
    fold.drain()


def ffn_grad_rows(count, peers, chunks, lag, parts, middle, cotangent, gain, ffn_rows, grad_gate, cot_rows, activated):
    rows, features = middle.shape
    span = rows // chunks
    block = features // peers
    units = activated.shape[1]
    width = 256
    vmem = pl.BlockSpec(memory_space=pltpu.VMEM)
    operands = (parts, middle, cotangent, gain, ffn_rows, grad_gate, cot_rows, activated)
    return pl.pallas_call(
        functools.partial(ffn_grad_kernel, count, peers, chunks, lag, rows, width),
        in_specs=[vmem] * len(operands),
        out_specs=[vmem] * 5,
        out_shape=[
            jax.ShapeDtypeStruct((count * rows, features), HALF),
            jax.ShapeDtypeStruct((rows, features), FULL),
            jax.ShapeDtypeStruct((1, features), FULL),
            jax.ShapeDtypeStruct((block, 2, units), FULL),
            jax.ShapeDtypeStruct((units, block), FULL),
        ],
        scratch_shapes=[
            pltpu.VMEM((span, features), FULL),
            pltpu.VMEM((2, chunks, count - 1, span, features), HALF),
        ]
        + fold_scratch(peers, 3 * units // width, block, width)
        + [pltpu.SemaphoreType.DMA((2, chunks, count - 1))] * 4,
        name="ffn_grad_rows",
        cost_estimate=pl.CostEstimate(flops=100_000_000_000, bytes_accessed=20_000_000, transcendentals=0),
        compiler_params=pltpu.CompilerParams(
            collective_id=2, has_side_effects=True, vmem_limit_bytes=62 * 2**20
        ),
    )(*operands)


CHUNKS = 4
LAG = 2


def sum_rows(pieces):
    return lax.psum_scatter(pieces, "tensor", scatter_dimension=0, tiled=True).astype(FULL)


def dot_nt(a, b):
    return jnp.einsum("sb,ab->sa", a, b, preferred_element_type=FULL)


def body(
    hidden_in,
    segments,
    norm_gain,
    mamba_in,
    step_weight,
    state_weight,
    decay_log,
    step_bias,
    skip_gain,
    gated_gain,
    query_weight,
    keyval_weight,
    mamba_out,
    attn_out,
    ffn_gain,
    gate_up,
    down_weight,
    cotangent,
):
    tensor_index = lax.axis_index("tensor")
    count, peers = lax.axis_size("tensor"), lax.axis_size("dp")
    heads = decay_log.shape[0]
    width = mamba_in.shape[2]
    state_size = state_weight.shape[2]
    query_width = query_weight.shape[1]
    qheads = query_width // ATT_DIM
    units = gate_up.shape[2]
    rows_local = hidden_in.shape[0]
    block = norm_gain.shape[0]
    group_size = ATT_HEADS // KV_HEADS
    kv_head = tensor_index * qheads // group_size
    col = Columns(query_width, width, state_size)

    gains = jnp.pad(jnp.stack([norm_gain, ffn_gain]).astype(FULL), ((0, 6), (0, 0)))
    step_padded = jnp.pad(step_weight, ((0, 0), (0, 2 * LANES - heads)))
    sequence, weight_in, gains = entry(
        count,
        peers,
        hidden_in,
        gains,
        query_weight,
        keyval_weight,
        mamba_in,
        state_weight,
        step_padded,
        lambda place: (place * qheads // group_size) * ATT_DIM,
    )
    gain_one, gain_two = gains[0:1], gains[1:2]
    weight_out = lax.all_gather(jnp.concatenate([mamba_out, attn_out], 0), "dp", axis=1, tiled=True)
    local_ffn = jnp.concatenate([gate_up.reshape(block, 2 * units), down_weight.T], 1)
    sequence, cotangent_late, weight_out = lax.optimization_barrier((sequence, cotangent, weight_out))
    cot_rows = lax.all_gather(cotangent_late, "tensor", axis=0, tiled=True)
    length = sequence.shape[0]
    packed = jnp.dot(sequence, weight_in, preferred_element_type=FULL)
    head_params = jnp.pad(
        jnp.stack([decay_log, step_bias, skip_gain]), ((0, 5), (0, LANES - heads))
    )
    tables = rope_tables(length)

    scan_y, states, gated_vals, squares = scan_forward(
        col, heads, state_size, packed, segments, head_params
    )
    attended, lse, squares = attend_forward(col, qheads, count, packed, tables, segments, squares)
    gated_inverse = lax.rsqrt(squares / (MAMBA_HEADS * HEAD_DIM) + EPSILON).reshape(length, 1)
    gated_scale = gated_gain.astype(FULL)
    gated_plain = gated_vals * gated_inverse
    branches = jnp.concatenate([(gated_plain * gated_scale).astype(HALF), attended], 1)
    ffn_rows, activated, grad_gate, ffn_parts, out_parts, middle = ffn_rows_call(
        count, peers, CHUNKS, LAG, branches, weight_out, hidden_in, gain_two, cot_rows, local_ffn
    )
    grad_mixed, grad_middle, ffn_gain_part, gate_up_grad, down_weight_grad = ffn_grad_rows(
        count, peers, CHUNKS, LAG, ffn_parts, middle, cotangent, gain_two, ffn_rows, grad_gate, cot_rows, activated
    )
    grad_mixed, out_parts = lax.optimization_barrier((grad_mixed, out_parts))
    ffn_out = sum_rows(out_parts)
    grad_branches = dot_nt(grad_mixed, weight_out)
    product_sum = jnp.sum(grad_branches[:, :width] * gated_scale * gated_plain, -1).reshape(-1, LANES)
    attention_grads, product_sum = attend_backward(
        col, qheads, count, packed, attended, lse, grad_branches, tables, segments, product_sum
    )
    grads, gain_part, skip_part, head_part = scan_backward(
        col,
        heads,
        state_size,
        packed,
        scan_y,
        states,
        grad_branches,
        squares,
        product_sum,
        gated_scale[None, :],
        segments,
        head_params,
        attention_grads,
    )
    head_sums = jnp.concatenate(
        [
            gain_part[0],
            head_part[0, :heads],
            head_part[1, :heads],
            skip_part.reshape(heads, HEAD_DIM).sum(1),
        ]
    )
    head_rows = jnp.pad(head_sums, (0, 8 * LANES - head_sums.shape[0])).reshape(8, LANES)
    (
        hidden_grad,
        gain_grads,
        head_rows,
        query_grad,
        inner_grad,
        step_grad,
        state_grad,
        keyval_grad,
        mamba_out_grad,
        attn_out_grad,
    ) = final_rows(
        count,
        peers,
        2,
        lambda place: place * qheads // group_size,
        col,
        heads,
        width,
        grads,
        weight_in,
        hidden_in,
        grad_middle,
        gain_one,
        ffn_gain_part,
        head_rows,
        sequence,
        grad_mixed,
        branches,
    )
    head_sums = head_rows.reshape(-1)
    hidden_out = (middle + ffn_out).astype(HALF)
    return (
        hidden_out,
        hidden_grad,
        gain_grads[0],
        inner_grad,
        step_grad,
        state_grad,
        head_sums[width : width + heads],
        head_sums[width + heads : width + 2 * heads],
        head_sums[width + 2 * heads : width + 3 * heads],
        head_sums[:width],
        query_grad,
        keyval_grad,
        mamba_out_grad,
        attn_out_grad,
        gain_grads[1],
        gate_up_grad,
        down_weight_grad,
    )


def solution(mesh):
    rows = P(("dp", "tensor"), None)
    weights_in = P("dp", None, "tensor")
    return jax.shard_map(
        body,
        mesh=mesh,
        in_specs=(
            rows,
            P("dp"),
            P("dp"),
            weights_in,
            P("dp", "tensor"),
            P("dp", None, None),
            P("tensor"),
            P("tensor"),
            P("tensor"),
            P("tensor"),
            P("dp", "tensor"),
            P("dp", None, None),
            P("tensor", "dp"),
            P("tensor", "dp"),
            P("dp"),
            weights_in,
            P("tensor", "dp"),
            rows,
        ),
        out_specs=(
            rows,
            rows,
            P("dp"),
            weights_in,
            P("dp", "tensor"),
            P("dp", None, None),
            P("tensor"),
            P("tensor"),
            P("tensor"),
            P("tensor"),
            P("dp", "tensor"),
            P("dp", None, None),
            P("tensor", "dp"),
            P("tensor", "dp"),
            P("dp"),
            weights_in,
            P("tensor", "dp"),
        ),
        check_vma=False,
    )
```

```python
import functools
import math
import jax
import jax.numpy as jnp
from jax import lax
from jax.experimental import pallas as pl
from jax.experimental.pallas import tpu as pltpu
from jax.sharding import PartitionSpec as P

MAMBA_HEADS = 48
HEAD_DIM = 64
ATT_HEADS = 8
KV_HEADS = 2
ATT_DIM = 128
STRETCH = 128
ATT_BLOCK = 256
EPSILON = 1e-05
PRECISE = lax.Precision.HIGHEST
ROPE_BASE = 10000.0
LANES = 128
MASKED = -1e30
HALF = jnp.bfloat16
FULL = jnp.float32


def mm(a, b):
    return jnp.dot(a, b, preferred_element_type=FULL)


def mm_nt(a, b):
    return lax.dot_general(a, b, (((1,), (1,)), ((), ())), preferred_element_type=FULL)


def mm_tn(a, b):
    return lax.dot_general(a, b, (((0,), (0,)), ((), ())), preferred_element_type=FULL)


def softplus(v):
    return jnp.maximum(v, 0.0) + jnp.log1p(jnp.exp(-jnp.abs(v)))


def sigmoid(v):
    return 1.0 / (1.0 + jnp.exp(-v))


def iota(shape, dim):
    return lax.broadcasted_iota(jnp.int32, shape, dim)


def halves(left, right, size):
    return jnp.where(iota((size, LANES), 1) < HEAD_DIM, left, right)


def as_row(values):
    return jnp.broadcast_to(values, (LANES, LANES)).T[0:1, :]


def as_column(values):
    return jnp.broadcast_to(values, (LANES, LANES)).T[:, 0:1]


def stacked_pair(pair):
    low = iota(pair.shape, 1) < HEAD_DIM
    zero = jnp.zeros_like(pair)
    return jnp.concatenate([jnp.where(low, pair, zero), jnp.where(low, zero, pair)], 0)


class Columns:
    def __init__(self, query, width, state):
        self.query = (0, query)
        self.key = (query, query + ATT_DIM)
        self.value = (query + ATT_DIM, query + 2 * ATT_DIM)
        start = query + 2 * ATT_DIM
        self.attention = start
        self.gate = (start, start + width)
        self.drive = (start + width, start + 2 * width)
        start += 2 * width
        self.inmap = (start, start + state)
        self.outmap = (start + state, start + 2 * state)
        start += 2 * state
        self.step = (start, start + LANES)
        self.total = start + 2 * LANES


def stretch_common(col, packed, segc_ref, segr_ref, head_ref, before):
    span = STRETCH
    raw = packed[:, col.step[0] : col.step[1]] + head_ref[1:2, :]
    step = softplus(raw)
    keep = -jnp.exp(head_ref[0:1, :]) * step
    row, column = iota((span, span), 0), iota((span, span), 1)
    running = jnp.dot(
        (row >= column).astype(FULL), keep, precision=PRECISE, preferred_element_type=FULL
    )
    segc, segr = segc_ref[...], segr_ref[0]
    causal = (row >= column) & (segc == segr)
    blocked = jnp.where(causal, 0.0, MASKED)
    live = (segc == before).astype(FULL)
    last = segc[span - 1 : span, :]
    tail = (segc == last).astype(FULL)
    old = (last == before).astype(FULL)
    return raw, step, keep, running, running.T, blocked, live, tail, old


def pair_decay(pair, running, running_t, blocked, live, tail, old):
    span = STRETCH
    a, b = 2 * pair, 2 * pair + 1
    col_a = jnp.broadcast_to(running[:, a : a + 1], (span, LANES))
    col_b = jnp.broadcast_to(running[:, b : b + 1], (span, LANES))
    decay_a = jnp.exp(col_a - running_t[a : a + 1, :] + blocked)
    decay_b = jnp.exp(col_b - running_t[b : b + 1, :] + blocked)
    both = halves(col_a, col_b, span)
    last = both[span - 1 : span, :]
    into = jnp.exp(both) * live
    weight = jnp.exp(last - both) * tail
    keep_old = jnp.exp(last) * old
    return decay_a, decay_b, into, weight, keep_old


def scan_forward_kernel(col, heads, p_ref, segc_ref, segr_ref, head_ref, y_ref, states_ref, gated_ref, square_ref, state, before):
    index = pl.program_id(0)
    span = STRETCH

    @pl.when(index == 0)
    def _():
        state[...] = jnp.zeros_like(state)
        before[...] = jnp.full_like(before, -1)

    raw, step, keep, running, running_t, blocked, live, tail, old = stretch_common(
        col, p_ref, segc_ref, segr_ref, head_ref, before[...]
    )
    inmap = p_ref[:, col.inmap[0] : col.inmap[1]].astype(HALF)
    outmap = p_ref[:, col.outmap[0] : col.outmap[1]].astype(HALF)
    inmap_t = inmap.T
    scores = mm_nt(outmap, inmap)
    square = jnp.zeros((span, 1), FULL)
    for pair in range(heads // 2):
        at = pair * LANES
        lanes = slice(at, at + LANES)
        decay_a, decay_b, into, weight, keep_old = pair_decay(
            pair, running, running_t, blocked, live, tail, old
        )
        drive = p_ref[:, col.drive[0] + at : col.drive[0] + at + LANES]
        gate = p_ref[:, col.gate[0] + at : col.gate[0] + at + LANES]
        driven = drive * halves(step[:, 2 * pair : 2 * pair + 1], step[:, 2 * pair + 1 : 2 * pair + 2], span)
        driven_low = driven.astype(HALF)
        mix = jnp.concatenate([(decay_a * scores).astype(HALF), (decay_b * scores).astype(HALF)], 1)
        held = state[:, lanes]
        held_low = held.astype(HALF)
        states_ref[0, :, lanes] = held_low
        result = mm(mix, stacked_pair(driven_low)) + mm(outmap, held_low) * into
        state[:, lanes] = held * keep_old + mm(inmap_t, (driven_low.astype(FULL) * weight).astype(HALF))
        y_ref[:, lanes] = result
        skip = halves(head_ref[2:3, 2 * pair : 2 * pair + 1], head_ref[2:3, 2 * pair + 1 : 2 * pair + 2], 1)
        gated = (result + skip * drive) * (gate * sigmoid(gate))
        gated_ref[:, lanes] = gated
        square = square + jnp.sum(gated * gated, 1, keepdims=True)
    square_ref[pl.ds(index, 1), :] = as_row(square)
    before[...] = segc_ref[span - 1 : span, :]


def scan_forward(col, heads, state_size, packed, segments, head_params):
    length = packed.shape[0]
    width = heads * HEAD_DIM
    count = length // STRETCH
    return pl.pallas_call(
        functools.partial(scan_forward_kernel, col, heads),
        grid=(count,),
        in_specs=[
            pl.BlockSpec((STRETCH, col.total), lambda i: (i, 0)),
            pl.BlockSpec((STRETCH, 1), lambda i: (i, 0)),
            pl.BlockSpec((1, 1, STRETCH), lambda i: (i, 0, 0)),
            pl.BlockSpec((8, LANES), lambda i: (0, 0)),
        ],
        out_specs=[
            pl.BlockSpec((STRETCH, width), lambda i: (i, 0)),
            pl.BlockSpec((1, state_size, width), lambda i: (i, 0, 0)),
            pl.BlockSpec((STRETCH, width), lambda i: (i, 0)),
            pl.BlockSpec((count, LANES), lambda i: (0, 0)),
        ],
        out_shape=[
            jax.ShapeDtypeStruct((length, width), FULL),
            jax.ShapeDtypeStruct((count, state_size, width), HALF),
            jax.ShapeDtypeStruct((length, width), FULL),
            jax.ShapeDtypeStruct((count, LANES), FULL),
        ],
        scratch_shapes=[pltpu.VMEM((state_size, width), FULL), pltpu.VMEM((1, 1), jnp.int32)],
        name="scan_forward",
        cost_estimate=pl.CostEstimate(flops=16_000_000_000, bytes_accessed=30_000_000, transcendentals=0),
        compiler_params=pltpu.CompilerParams(vmem_limit_bytes=48 * 2**20),
    )(packed, segments[:, None], segments.reshape(count, 1, STRETCH), head_params)


def scan_backward_kernel(
    col, heads, total_width, p_ref, y_ref, states_ref, gm_ref, inv_ref, prod_ref, gain_ref,
    segc_ref, segr_ref, segb_ref, head_ref, ag_ref, g_ref, gain_grad_ref, skip_grad_ref, head_grad_ref, future,
):
    step_index = pl.program_id(0)
    count = pl.num_programs(0)
    span = STRETCH

    @pl.when(step_index == 0)
    def _():
        future[...] = jnp.zeros_like(future)
        gain_grad_ref[...] = jnp.zeros_like(gain_grad_ref)
        skip_grad_ref[...] = jnp.zeros_like(skip_grad_ref)
        head_grad_ref[...] = jnp.zeros_like(head_grad_ref)

    before = jnp.where(step_index == count - 1, -1, segb_ref[span - 1 : span, :])
    raw, step, keep, running, running_t, blocked, live, tail, old = stretch_common(
        col, p_ref, segc_ref, segr_ref, head_ref, before
    )
    inmap = p_ref[:, col.inmap[0] : col.inmap[1]].astype(HALF)
    outmap = p_ref[:, col.outmap[0] : col.outmap[1]].astype(HALF)
    outmap_t = outmap.T
    scores = mm_nt(outmap, inmap)
    lane = iota((span, LANES), 1)
    head_lane = iota((1, LANES), 1)
    paired = jnp.zeros((span, span), FULL)
    grad_in = jnp.zeros(inmap.shape, FULL)
    grad_out = jnp.zeros(outmap.shape, FULL)
    grad_running = jnp.zeros((span, LANES), FULL)
    grad_step = jnp.zeros((span, LANES), FULL)
    grad_last = jnp.zeros((1, LANES), FULL)
    chunk = pl.ds(count - 1 - step_index, 1)
    inverse = as_column(lax.rsqrt(inv_ref[chunk, :] * (1.0 / total_width) + EPSILON))
    product = as_column(prod_ref[chunk, :] * (1.0 / total_width))
    for pair in range(heads // 2):
        at = pair * LANES
        lanes = slice(at, at + LANES)
        a, b = 2 * pair, 2 * pair + 1
        decay_a, decay_b, into, weight, keep_old = pair_decay(
            pair, running, running_t, blocked, live, tail, old
        )
        drive = p_ref[:, col.drive[0] + at : col.drive[0] + at + LANES]
        gate = p_ref[:, col.gate[0] + at : col.gate[0] + at + LANES]
        result = y_ref[:, lanes]
        skip = halves(head_ref[2:3, a : a + 1], head_ref[2:3, b : b + 1], 1)
        sig = sigmoid(gate)
        silu = gate * sig
        ssm = result + skip * drive
        plain = ssm * silu * inverse
        grad_above = gm_ref[:, lanes].astype(FULL)
        gain_grad_ref[:, lanes] += jnp.sum(grad_above * plain, 0, keepdims=True)
        grad_gated = inverse * (grad_above * gain_ref[:, lanes] - plain * product)
        g_ref[:, col.gate[0] + at : col.gate[0] + at + LANES] = (
            grad_gated * ssm * (sig * (1.0 + gate * (1.0 - sig)))
        ).astype(HALF)
        grad_y = grad_gated * silu
        grad_y_low = grad_y.astype(HALF)
        grad_y = grad_y_low.astype(FULL)
        step_pair = halves(step[:, a : a + 1], step[:, b : b + 1], span)
        driven_low = (drive * step_pair).astype(HALF)
        driven = driven_low.astype(FULL)
        grad_rows = stacked_pair(grad_y_low)
        inner = mm_nt(grad_rows, driven_low)
        paired = paired + decay_a * inner[:span] + decay_b * inner[span:]
        mix = jnp.concatenate([(decay_a * scores).astype(HALF), (decay_b * scores).astype(HALF)], 0)
        later = future[:, lanes]
        later_low = later.astype(HALF)
        held_low = states_ref[0, :, lanes]
        reach = mm(inmap, later_low) * weight
        grad_driven = mm_tn(mix, grad_rows) + reach
        weighted = (driven * weight).astype(HALF)
        spread = (grad_y * into).astype(HALF)
        grad_in = grad_in + mm_nt(weighted, later_low)
        grad_out = grad_out + mm_nt(spread, held_low)
        future[:, lanes] = later * keep_old + mm(outmap_t, spread)
        g_ref[:, col.drive[0] + at : col.drive[0] + at + LANES] = (
            step_pair * grad_driven + skip * grad_y
        ).astype(HALF)
        skip_grad_ref[:, lanes] += jnp.sum(grad_y * drive, 0, keepdims=True)
        turn = grad_y * result - driven * grad_driven
        left = lane < HEAD_DIM
        from_drive = drive * grad_driven
        ends = jnp.sum(driven * reach, 0, keepdims=True) + keep_old * jnp.sum(
            later * held_low.astype(FULL), 0, keepdims=True
        )
        for head, mask in ((a, left), (b, ~left)):
            grad_running = grad_running + jnp.where(
                lane == head, jnp.sum(jnp.where(mask, turn, 0.0), 1, keepdims=True), 0.0
            )
            grad_step = grad_step + jnp.where(
                lane == head, jnp.sum(jnp.where(mask, from_drive, 0.0), 1, keepdims=True), 0.0
            )
            grad_last = grad_last + jnp.where(
                head_lane == head, jnp.sum(jnp.where(mask[0:1], ends, 0.0), 1, keepdims=True), 0.0
            )
    paired = paired.astype(HALF)
    grad_out = grad_out + mm(paired, inmap)
    grad_in = grad_in + mm_tn(paired, outmap)
    g_ref[:, col.inmap[0] : col.inmap[1]] = grad_in.astype(HALF)
    g_ref[:, col.outmap[0] : col.outmap[1]] = grad_out.astype(HALF)
    row, column = iota((span, span), 0), iota((span, span), 1)
    grad_keep = (
        jnp.dot((row <= column).astype(FULL), grad_running, precision=PRECISE, preferred_element_type=FULL)
        + grad_last
    )
    grad_raw = (grad_step - grad_keep * jnp.exp(head_ref[0:1, :])) * sigmoid(raw)
    grad_raw = jnp.where(lane < heads, grad_raw, 0.0)
    g_ref[:, col.step[0] : col.step[1]] = grad_raw.astype(HALF)
    g_ref[:, col.step[1] : col.total] = jnp.zeros((span, col.total - col.step[1]), HALF)
    g_ref[:, 0 : col.attention] = ag_ref[...]
    head_grad_ref[0:1, :] += jnp.sum(keep * grad_keep, 0, keepdims=True)
    head_grad_ref[1:2, :] += jnp.sum(grad_raw, 0, keepdims=True)


def scan_backward(
    col, heads, state_size, packed, y, states, grad_mamba, squares, product, gain, segments, head_params, attention_grads
):
    length = packed.shape[0]
    width = heads * HEAD_DIM
    count = length // STRETCH
    back = lambda i: (count - 1 - i, 0)
    return pl.pallas_call(
        functools.partial(scan_backward_kernel, col, heads, MAMBA_HEADS * HEAD_DIM),
        grid=(count,),
        in_specs=[
            pl.BlockSpec((STRETCH, col.total), back),
            pl.BlockSpec((STRETCH, width), back),
            pl.BlockSpec((1, state_size, width), lambda i: (count - 1 - i, 0, 0)),
            pl.BlockSpec((STRETCH, width), back),
            pl.BlockSpec((count, LANES), lambda i: (0, 0)),
            pl.BlockSpec((count, LANES), lambda i: (0, 0)),
            pl.BlockSpec((1, width), lambda i: (0, 0)),
            pl.BlockSpec((STRETCH, 1), back),
            pl.BlockSpec((1, 1, STRETCH), lambda i: (count - 1 - i, 0, 0)),
            pl.BlockSpec((STRETCH, 1), lambda i: (jnp.maximum(count - 2 - i, 0), 0)),
            pl.BlockSpec((8, LANES), lambda i: (0, 0)),
            pl.BlockSpec((STRETCH, col.attention), back),
        ],
        out_specs=[
            pl.BlockSpec((STRETCH, col.total), back),
            pl.BlockSpec((1, width), lambda i: (0, 0)),
            pl.BlockSpec((1, width), lambda i: (0, 0)),
            pl.BlockSpec((8, LANES), lambda i: (0, 0)),
        ],
        out_shape=[
            jax.ShapeDtypeStruct((length, col.total), HALF),
            jax.ShapeDtypeStruct((1, width), FULL),
            jax.ShapeDtypeStruct((1, width), FULL),
            jax.ShapeDtypeStruct((8, LANES), FULL),
        ],
        scratch_shapes=[pltpu.VMEM((state_size, width), FULL)],
        name="scan_backward",
        cost_estimate=pl.CostEstimate(flops=24_000_000_000, bytes_accessed=40_000_000, transcendentals=0),
        compiler_params=pltpu.CompilerParams(vmem_limit_bytes=48 * 2**20),
    )(
        packed, y, states, grad_mamba, squares, product, gain, segments[:, None],
        segments.reshape(count, 1, STRETCH), segments[:, None], head_params, attention_grads,
    )


def turned(values, cosine, sine):
    return values * cosine + pltpu.roll(values, ATT_DIM // 2, 1) * sine


def attend_forward_kernel(
    col, heads, peers, p_ref, cos_ref, sin_ref, segc_ref, segr_ref, own_ref, out_ref, lse_ref, sum_ref, held, sends, receives
):
    length = p_ref.shape[0]
    finish = spread(peers, own_ref, held, sends, receives)
    scale = 1.0 / math.sqrt(ATT_DIM)
    keys = turned(p_ref[:, col.key[0] : col.key[1]], cos_ref[...], sin_ref[...]).astype(HALF)
    values = p_ref[:, col.value[0] : col.value[1]].astype(HALF)
    for block in range(length // ATT_BLOCK):
        rows = slice(block * ATT_BLOCK, (block + 1) * ATT_BLOCK)
        end = (block + 1) * ATT_BLOCK
        place = iota((ATT_BLOCK, end), 0) + block * ATT_BLOCK
        allowed = (place >= iota((ATT_BLOCK, end), 1)) & (segc_ref[rows, :] == segr_ref[:, :end])
        blocked = jnp.where(allowed, 0.0, MASKED)
        for head in range(heads):
            lanes = slice(head * ATT_DIM, (head + 1) * ATT_DIM)
            query = (turned(p_ref[rows, lanes], cos_ref[rows, :], sin_ref[rows, :]) * scale).astype(HALF)
            scores = mm_nt(query, keys[:end]) + blocked
            highest = jnp.max(scores, 1, keepdims=True)
            weights = jnp.exp(scores - highest)
            total = jnp.sum(weights, 1, keepdims=True)
            out_ref[rows, lanes] = (mm(weights.astype(HALF), values[:end]) / total).astype(HALF)
            lse_ref[rows, lanes] = jnp.broadcast_to(highest + jnp.log(total), (ATT_BLOCK, ATT_DIM))
    finish(sum_ref)


def exchange_scratch(peers, shape):
    return [
        pltpu.VMEM((peers,) + shape, FULL),
        pltpu.SemaphoreType.DMA((peers,)),
        pltpu.SemaphoreType.DMA((peers,)),
    ]


def spread(peers, own_ref, held, sends, receives):
    me = lax.axis_index("tensor")
    barrier = pltpu.get_barrier_semaphore()
    others = [lax.rem(me + distance, peers) for distance in range(1, peers)]
    for other in others:
        pl.semaphore_signal(barrier, inc=1, device_id={"tensor": other}, device_id_type=pl.DeviceIdType.MESH)
    pl.semaphore_wait(barrier, peers - 1)

    def copy(distance):
        return pltpu.make_async_remote_copy(
            src_ref=own_ref,
            dst_ref=held.at[distance],
            send_sem=sends.at[distance],
            recv_sem=receives.at[distance],
            device_id={"tensor": others[distance - 1]},
            device_id_type=pl.DeviceIdType.MESH,
        )

    for distance in range(1, peers):
        copy(distance).start()

    def finish(sum_ref):
        sum_ref[...] = own_ref[...]
        for distance in range(1, peers):
            copy(distance).wait()
            sum_ref[...] += held[distance]

    return finish


def attend_forward(col, heads, peers, packed, tables, segments, own):
    length = packed.shape[0]
    whole = lambda i: (0, 0)
    return pl.pallas_call(
        functools.partial(attend_forward_kernel, col, heads, peers),
        grid=(1,),
        in_specs=[
            pl.BlockSpec((length, col.attention), whole),
            pl.BlockSpec((length, ATT_DIM), whole),
            pl.BlockSpec((length, ATT_DIM), whole),
            pl.BlockSpec((length, 1), whole),
            pl.BlockSpec((1, length), whole),
            pl.BlockSpec(own.shape, whole),
        ],
        out_specs=[
            pl.BlockSpec((length, heads * ATT_DIM), whole),
            pl.BlockSpec((length, heads * ATT_DIM), whole),
            pl.BlockSpec(own.shape, whole),
        ],
        out_shape=[
            jax.ShapeDtypeStruct((length, heads * ATT_DIM), HALF),
            jax.ShapeDtypeStruct((length, heads * ATT_DIM), FULL),
            jax.ShapeDtypeStruct(own.shape, FULL),
        ],
        scratch_shapes=exchange_scratch(peers, own.shape),
        name="attend_forward",
        cost_estimate=pl.CostEstimate(flops=6_000_000_000, bytes_accessed=5_000_000, transcendentals=2_000_000),
        compiler_params=pltpu.CompilerParams(
            vmem_limit_bytes=48 * 2**20, collective_id=4, has_side_effects=True
        ),
    )(packed, tables[0], tables[1], segments[:, None], segments[None, :], own)


def attend_backward_kernel(
    col, heads, peers, p_ref, out_ref, lse_ref, go_ref, cos_ref, sin_ref, segc_ref, segr_ref, own_ref, g_ref, sum_ref,
    key_grad, value_grad, held, sends, receives,
):
    length = p_ref.shape[0]
    finish = spread(peers, own_ref, held, sends, receives)
    scale = 1.0 / math.sqrt(ATT_DIM)
    keys = turned(p_ref[:, col.key[0] : col.key[1]], cos_ref[...], sin_ref[...]).astype(HALF)
    values = p_ref[:, col.value[0] : col.value[1]].astype(HALF)
    key_grad[...] = jnp.zeros_like(key_grad)
    value_grad[...] = jnp.zeros_like(value_grad)
    for block in range(length // ATT_BLOCK):
        rows = slice(block * ATT_BLOCK, (block + 1) * ATT_BLOCK)
        end = (block + 1) * ATT_BLOCK
        place = iota((ATT_BLOCK, end), 0) + block * ATT_BLOCK
        allowed = (place >= iota((ATT_BLOCK, end), 1)) & (segc_ref[rows, :] == segr_ref[:, :end])
        blocked = jnp.where(allowed, 0.0, MASKED)
        cosine, sine = cos_ref[rows, :], sin_ref[rows, :]
        for head in range(heads):
            lanes = slice(head * ATT_DIM, (head + 1) * ATT_DIM)
            query = (turned(p_ref[rows, lanes], cosine, sine) * scale).astype(HALF)
            weights = jnp.exp(mm_nt(query, keys[:end]) + blocked - lse_ref[rows, lanes][:, 0:1])
            grad_low = go_ref[rows, lanes].astype(HALF)
            delta = jnp.sum(grad_low.astype(FULL) * out_ref[rows, lanes].astype(FULL), 1, keepdims=True)
            grad_scores = (weights * (mm_nt(grad_low, values[:end]) - delta)).astype(HALF)
            value_grad[:end, :] += mm_tn(weights.astype(HALF), grad_low)
            key_grad[:end, :] += mm_tn(grad_scores, query)
            grad_query = mm(grad_scores, keys[:end]) * scale
            g_ref[rows, lanes] = turned(grad_query, cosine, -sine).astype(HALF)
    g_ref[:, col.key[0] : col.key[1]] = turned(key_grad[...], cos_ref[...], -sin_ref[...]).astype(HALF)
    g_ref[:, col.value[0] : col.value[1]] = value_grad[...].astype(HALF)
    finish(sum_ref)


def attend_backward(col, heads, peers, packed, attended, lse, grad_branches, tables, segments, own):
    length = packed.shape[0]
    width = heads * ATT_DIM
    whole = lambda i: (0, 0)
    return pl.pallas_call(
        functools.partial(attend_backward_kernel, col, heads, peers),
        grid=(1,),
        in_specs=[
            pl.BlockSpec((length, col.attention), whole),
            pl.BlockSpec((length, width), whole),
            pl.BlockSpec((length, width), whole),
            pl.BlockSpec((length, width), lambda i: (0, grad_branches.shape[1] // width - 1)),
            pl.BlockSpec((length, ATT_DIM), whole),
            pl.BlockSpec((length, ATT_DIM), whole),
            pl.BlockSpec((length, 1), whole),
            pl.BlockSpec((1, length), whole),
            pl.BlockSpec(own.shape, whole),
        ],
        out_specs=[pl.BlockSpec((length, col.attention), whole), pl.BlockSpec(own.shape, whole)],
        out_shape=[
            jax.ShapeDtypeStruct((length, col.attention), HALF),
            jax.ShapeDtypeStruct(own.shape, FULL),
        ],
        scratch_shapes=[pltpu.VMEM((length, ATT_DIM), FULL), pltpu.VMEM((length, ATT_DIM), FULL)]
        + exchange_scratch(peers, own.shape),
        name="attend_backward",
        cost_estimate=pl.CostEstimate(flops=8_000_000_000, bytes_accessed=10_000_000, transcendentals=2_000_000),
        compiler_params=pltpu.CompilerParams(
            vmem_limit_bytes=48 * 2**20, collective_id=5, has_side_effects=True
        ),
    )(
        packed, attended, lse, grad_branches, tables[0], tables[1], segments[:, None], segments[None, :], own
    )


def rope_tables(positions):
    half = ATT_DIM // 2
    frequency = ROPE_BASE ** (-jnp.arange(half, dtype=FULL) / half)
    angles = positions[:, None] * frequency[None, :]
    cosine, sine = jnp.cos(angles), jnp.sin(angles)
    return jnp.concatenate([cosine, cosine], 1), jnp.concatenate([-sine, sine], 1)


class Plane:
    def __init__(self, peers, source, whole, sends, receives):
        self.peers, self.source, self.whole = peers, source, whole
        self.sends, self.receives = sends, receives
        self.me = lax.axis_index("dp")
        self.rows = source.shape[0]
        self.width = source.shape[1]
        self.half = self.width // (2 * LANES) * LANES
        outer = [1 << bit for bit in range(1, peers.bit_length() - 1)]
        self.orders = [outer, outer[::-1]]
        self.steps = len(outer)

    def greet(self, barrier):
        for bit in [1] + self.orders[0]:
            pl.semaphore_signal(
                barrier, inc=1, device_id={"dp": self.me ^ bit}, device_id_type=MESH
            )
        return 1 + self.steps

    def held(self, side, step):
        order = self.orders[side]
        if step == 0:
            return [0]
        bit, before = order[step - 1], [0]
        for earlier in order[: step - 1]:
            before = before + [offset ^ earlier for offset in before]
        return [offset ^ bit for offset in before]

    def lanes(self, side):
        return pl.ds(0, self.half) if side == 0 else pl.ds(self.half, self.width - self.half)

    def block(self, side, offset):
        at = pl.ds(pl.multiple_of((self.me ^ offset) * self.rows, 16), self.rows)
        return self.whole.at[at, self.lanes(side)]

    def copy(self, side, bit, offset):
        source = self.source.at[:, self.lanes(side)] if offset == 0 else self.block(side, offset)
        at = (side, bit.bit_length() - 1, offset)
        return pltpu.make_async_remote_copy(
            src_ref=source,
            dst_ref=self.block(side, offset),
            send_sem=self.sends.at[at],
            recv_sem=self.receives.at[at],
            device_id={"dp": self.me ^ bit},
            device_id_type=MESH,
        )

    def arrival(self, side, bit, offset):
        at = (side, bit.bit_length() - 1, offset)
        return pltpu.make_async_remote_copy(
            src_ref=self.block(side, offset ^ bit),
            dst_ref=self.block(side, offset ^ bit),
            send_sem=self.sends.at[at],
            recv_sem=self.receives.at[at],
            device_id={"dp": self.me ^ bit},
            device_id_type=MESH,
        )

    def sent(self, side, step):
        blocks = []
        for earlier in range(step):
            blocks += self.held(side, earlier)
        return blocks

    def start(self):
        for side in (0, 1):
            if self.steps:
                self.copy(side, self.orders[side][0], 0).start()
        for side in (0, 1):
            self.copy(side, 1, 0).start()

    def advance(self, step):
        for side in (0, 1):
            bit = self.orders[side][step - 1]
            for offset in self.held(side, step):
                self.arrival(side, bit, offset ^ bit).wait_recv()
        for side in (0, 1):
            if step < self.steps:
                following = self.orders[side][step]
                for offset in self.sent(side, step + 1):
                    self.copy(side, following, offset).start()
        for side in (0, 1):
            for offset in self.held(side, step):
                self.copy(side, 1, offset).start()

    def finish(self):
        for side in (0, 1):
            for offset in self.sent(side, self.steps + 1):
                self.arrival(side, 1, offset).wait_recv()

    def drain(self):
        for side in (0, 1):
            for offset in self.sent(side, self.steps + 1):
                self.copy(side, 1, offset).wait_send()
            for step in range(1, self.steps + 1):
                for offset in self.sent(side, step):
                    self.copy(side, self.orders[side][step - 1], offset).wait_send()


class Swarm:
    def __init__(self, peers, count):
        self.peers, self.count = peers, count
        self.at_dp, self.at_tensor = lax.axis_index("dp"), lax.axis_index("tensor")

    def greet(self):
        barrier = pltpu.get_barrier_semaphore()
        for offset in range(1, self.peers):
            pl.semaphore_signal(barrier, inc=1, device_id={"dp": self.at_dp ^ offset}, device_id_type=MESH)
        for distance in range(1, self.count):
            pl.semaphore_signal(
                barrier, inc=1, device_id={"tensor": lax.rem(self.at_tensor + distance, self.count)}, device_id_type=MESH
            )
        pl.semaphore_wait(barrier, self.peers + self.count - 2)

    def along_dp(self, source_of, held, sends, receives):
        return [
            pltpu.make_async_remote_copy(
                src_ref=source_of(self.at_dp ^ offset),
                dst_ref=held.at[offset],
                send_sem=sends.at[offset],
                recv_sem=receives.at[offset],
                device_id={"dp": self.at_dp ^ offset},
                device_id_type=MESH,
            )
            for offset in range(1, self.peers)
        ]

    def along_tensor(self, source, held, sends, receives):
        return [
            pltpu.make_async_remote_copy(
                src_ref=source,
                dst_ref=held.at[distance],
                send_sem=sends.at[distance],
                recv_sem=receives.at[distance],
                device_id={"tensor": lax.rem(self.at_tensor + distance, self.count)},
                device_id_type=MESH,
            )
            for distance in range(1, self.count)
        ]


def plane_semaphores(peers):
    return [pltpu.SemaphoreType.DMA((2, max(peers.bit_length() - 1, 1), peers))] * 2


MESH = pl.DeviceIdType.MESH
TILE = 256
WIDE = 1024


class Line:
    def __init__(self, count):
        self.count = count
        self.me = lax.axis_index("tensor")
        self.has_left = self.me > 0
        self.has_right = self.me < count - 1

    def greet(self, plane=None):
        barrier = pltpu.get_barrier_semaphore()
        extra = 0 if plane is None else plane.greet(barrier)
        for present, shift in ((self.has_left, -1), (self.has_right, 1)):

            @pl.when(present)
            def _():
                pl.semaphore_signal(
                    barrier, inc=1, device_id={"tensor": self.me + shift}, device_id_type=MESH
                )

        inside = self.has_left & self.has_right

        @pl.when(inside)
        def _():
            pl.semaphore_wait(barrier, 2 + extra)

        @pl.when(jnp.logical_not(inside))
        def _():
            pl.semaphore_wait(barrier, 1 + extra)

    def copy(self, source, target, sends, receives, at, side):
        return pltpu.make_async_remote_copy(
            src_ref=source,
            dst_ref=target,
            send_sem=sends.at[at],
            recv_sem=receives.at[at],
            device_id={"tensor": self.me + (1 if side == 0 else -1)},
            device_id_type=MESH,
        )

    def place(self, side):
        return self.me if side == 0 else self.count - 1 - self.me

    def ahead(self, side, distance):
        return self.me + distance if side == 0 else self.me - distance

    def next_there(self, side):
        return self.has_right if side == 0 else self.has_left

    def last_there(self, side):
        return self.has_left if side == 0 else self.has_right


class Scatter:
    def __init__(self, line, parts, rows, span, slots, sends, receives):
        self.line, self.parts, self.rows, self.span = line, parts, rows, span
        self.slots, self.sends, self.receives = slots, sends, receives

    def own(self, owner, chunk):
        return self.parts.at[pl.ds(pl.multiple_of(owner * self.rows + chunk * self.span, 16), self.span), :]

    def transfer(self, side, chunk, hop, source=None):
        target = self.slots.at[side, chunk, hop - 1]
        return self.line.copy(
            target if source is None else source, target, self.sends, self.receives, (side, chunk, hop - 1), side
        )

    def hop(self, chunk, hop):
        line = self.line
        for side in (0, 1):
            place = line.place(side)
            owner = line.ahead(side, line.count - hop)

            @pl.when(place == 0)
            def _():
                self.transfer(side, chunk, hop, self.own(owner, chunk)).start()

            if hop > 1:

                @pl.when((place > 0) & (place <= hop - 1))
                def _():
                    slot = self.slots.at[side, chunk, hop - 2]
                    self.transfer(side, chunk, hop - 1).wait_recv()
                    slot[...] = (slot[...].astype(FULL) + self.own(owner, chunk)[...].astype(FULL)).astype(slot.dtype)
                    self.transfer(side, chunk, hop, slot).start()

    def finish(self, chunk, total):
        line = self.line
        total[...] = self.own(line.me, chunk)[...].astype(FULL)
        last = line.count - 1
        for side in (0, 1):

            @pl.when(line.last_there(side))
            def _():
                self.transfer(side, chunk, last).wait_recv()
                total[...] += self.slots[side, chunk, last - 1].astype(FULL)

    def drain(self, chunk):
        for hop in range(1, self.line.count):
            for side in (0, 1):

                @pl.when(self.line.place(side) <= hop - 1)
                def _():
                    self.transfer(side, chunk, hop).wait_send()


class Gather:
    def __init__(self, line, whole, rows, span, sends, receives):
        self.line, self.whole, self.rows, self.span = line, whole, rows, span
        self.sends, self.receives = sends, receives

    def at(self, owner, chunk):
        return self.whole.at[pl.ds(pl.multiple_of(owner * self.rows + chunk * self.span, 16), self.span), :]

    def transfer(self, side, chunk, hop):
        piece = self.at(self.line.ahead(1 - side, hop - 1), chunk)
        return self.line.copy(piece, piece, self.sends, self.receives, (side, chunk, hop - 1), side)

    def arrival(self, side, chunk, hop):
        piece = self.at(self.line.ahead(1 - side, hop), chunk)
        return self.line.copy(piece, piece, self.sends, self.receives, (side, chunk, hop - 1), side)

    def send(self, chunk, hop):
        line = self.line
        for side in (0, 1):

            @pl.when(line.next_there(side) & (line.place(side) >= hop - 1))
            def _():
                self.transfer(side, chunk, hop).start()

    def receive(self, chunk, hop):
        line = self.line
        for side in (0, 1):

            @pl.when(line.place(side) >= hop)
            def _():
                self.arrival(side, chunk, hop).wait_recv()

    def step(self, chunk, hop):
        line = self.line
        for side in (0, 1):

            @pl.when(line.place(side) >= hop)
            def _():
                self.arrival(side, chunk, hop).wait_recv()

            if hop < line.count - 1:

                @pl.when(line.next_there(side) & (line.place(side) >= hop))
                def _():
                    self.transfer(side, chunk, hop + 1).start()

    def drain(self, chunk):
        line = self.line
        for hop in range(1, line.count):
            for side in (0, 1):

                @pl.when(line.next_there(side) & (line.place(side) >= hop - 1))
                def _():
                    self.transfer(side, chunk, hop).wait_send()


def project(line, left, right, parts, rows, forward):
    upper = line.me < line.count // 2
    far = jnp.where(upper, line.count - 1, 0) * rows
    rest = jnp.where(upper, 0, 1) * rows

    def block(start, size):
        at = pl.ds(pl.multiple_of(start, 16), size)

        def tile(index, carry):
            lanes = pl.ds(pl.multiple_of(index * TILE, TILE), TILE)
            if forward:
                parts[at, lanes] = mm(left[at, :], right[:, lanes]).astype(parts.dtype)
            else:
                parts[at, lanes] = mm_nt(left[at, :], right[lanes, : left.shape[1]]).astype(parts.dtype)
            return carry

        lax.fori_loop(0, parts.shape[1] // TILE, tile, 0)

    return (lambda: block(far, rows)), (lambda: block(rest, (line.count - 1) * rows))


def relay(line, scatter, gather, chunks, lag, rows_done, first=None, second=None, events=None, received=None):
    last = line.count - 1
    if first is not None:
        first()
    turns = lag * (chunks - 1) + last + 1 + (0 if gather is None else last)
    for turn in range(turns):
        arrived = []
        for chunk in range(chunks):
            hop = turn - lag * chunk + 1
            if 1 <= hop <= last:
                scatter.hop(chunk, hop)
            elif hop == last + 1:
                rows_done(chunk)
                if gather is not None:
                    gather.send(chunk, 1)
            elif gather is not None and last + 1 < hop <= 2 * last + 1:
                gather.step(chunk, hop - last - 1)
                if hop == 2 * last + 1:
                    arrived.append(chunk)
        if turn == 0 and second is not None:
            second()
        if events is not None and turn in events:
            events[turn]()
        if received is not None:
            for chunk in arrived:
                scatter.drain(chunk)
                received(chunk)
    for chunk in range(chunks):
        if received is None:
            scatter.drain(chunk)
        if gather is not None:
            gather.drain(chunk)


def norm_below(value, above, gain):
    inverse = lax.rsqrt(jnp.mean(value * value, -1, keepdims=True) + EPSILON)
    plain = value * inverse
    scaled = above * gain
    below = inverse * (scaled - plain * jnp.mean(scaled * plain, -1, keepdims=True))
    return below, jnp.sum(above * plain, 0, keepdims=True)


def ffn_kernel(
    count, peers, chunks, lag, rows, units,
    left, right, hidden, gain, cot_rows, local_weight,
    out, activated, grad_gate, parts, out_parts, middle,
    weight, slots, total, part_rows, part_cot, part_gate, part_act, own_sem, s0, s1, s2, s3, p0, p1,
):
    line = Line(count)
    span = rows // chunks
    features = hidden.shape[1]
    plane = Plane(peers, local_weight, weight, p0, p1)
    keep_weight = pltpu.make_async_copy(
        local_weight, weight.at[pl.ds(pl.multiple_of(plane.me * plane.rows, 16), plane.rows), :], own_sem
    )
    keep_weight.start()
    line.greet(plane)
    plane.start()
    scatter = Scatter(line, parts, rows, span, slots, s0, s1)
    gather = Gather(line, out, rows, span, s2, s3)

    def rows_done(chunk):
        at = pl.ds(chunk * span, span)
        scatter.finish(chunk, total)
        value = total[...] + hidden[at, :].astype(FULL)
        middle[at, :] = value
        inverse = lax.rsqrt(jnp.mean(value * value, -1, keepdims=True) + EPSILON)
        gather.at(line.me, chunk)[...] = (value * inverse * gain[...]).astype(HALF)

    wide = min(WIDE, units)

    def received(chunk):
        if chunk == 0:
            plane.finish()
            keep_weight.wait()
        here = [pl.ds(owner * rows + chunk * span, span) for owner in range(count)]
        there = [slice(owner * span, (owner + 1) * span) for owner in range(count)]
        for source, target in zip(here, there):
            part_rows[target, :] = out[source, :]
            part_cot[target, :] = cot_rows[source, :]

        def gates(index, carry):
            lanes = pl.ds(pl.multiple_of(index * wide, wide), wide)
            upper = pl.ds(pl.multiple_of(units + index * wide, wide), wide)
            lower = pl.ds(pl.multiple_of(2 * units + index * wide, wide), wide)
            gate = mm(part_rows[...], weight[:, lanes])
            up = mm(part_rows[...], weight[:, upper])
            grad_act = mm(part_cot[...], weight[:, lower])
            sig = sigmoid(gate)
            silu = gate * sig
            act = (silu * up).astype(HALF)
            grad_one = (grad_act * up * (sig * (1.0 + gate * (1.0 - sig)))).astype(HALF)
            grad_two = (grad_act * silu).astype(HALF)
            part_gate[:, lanes] = grad_one
            part_gate[:, upper] = grad_two
            part_act[:, lanes] = act
            for source, target in zip(there, here):
                activated[target, lanes] = act[source, :]
                grad_gate[target, lanes] = grad_one[source, :]
                grad_gate[target, upper] = grad_two[source, :]
            return carry

        lax.fori_loop(0, units // wide, gates, 0)

        def back(index, carry):
            lanes = pl.ds(pl.multiple_of(index * wide, wide), wide)
            result = mm_nt(part_gate[...], weight[lanes, : 2 * units]).astype(parts.dtype)
            for source, target in zip(there, here):
                parts[target, lanes] = result[source, :]
            result = mm_nt(part_act[...], weight[lanes, 2 * units :]).astype(out_parts.dtype)
            for source, target in zip(there, here):
                out_parts[target, lanes] = result[source, :]
            return carry

        lax.fori_loop(0, features // wide, back, 0)

    last = count - 1
    events = {}
    for step in range(1, plane.steps + 1):
        events[min(2 + 3 * (step - 1), 2 * last - 1 - (plane.steps - step))] = functools.partial(plane.advance, step)
    first, second = project(line, left, right, parts, rows, True)
    relay(line, scatter, gather, chunks, lag, rows_done, first, second, events, received)
    plane.drain()


def ffn_rows_call(count, peers, chunks, lag, branches, weight_out, hidden, gain, cot_rows, local_weight):
    rows, features = hidden.shape
    length = count * rows
    units = local_weight.shape[1] // 3
    span = rows // chunks
    vmem = pl.BlockSpec(memory_space=pltpu.VMEM)
    return pl.pallas_call(
        functools.partial(ffn_kernel, count, peers, chunks, lag, rows, units),
        in_specs=[vmem] * 5 + [pl.BlockSpec(memory_space=pl.ANY)],
        out_specs=[vmem] * 6,
        out_shape=[
            jax.ShapeDtypeStruct((length, features), HALF),
            jax.ShapeDtypeStruct((length, units), HALF),
            jax.ShapeDtypeStruct((length, 2 * units), HALF),
            jax.ShapeDtypeStruct((length, features), HALF),
            jax.ShapeDtypeStruct((length, features), HALF),
            jax.ShapeDtypeStruct((rows, features), FULL),
        ],
        scratch_shapes=[
            pltpu.VMEM((peers * local_weight.shape[0], 3 * units), HALF),
            pltpu.VMEM((2, chunks, count - 1, span, features), HALF),
            pltpu.VMEM((span, features), FULL),
            pltpu.VMEM((count * span, features), HALF),
            pltpu.VMEM((count * span, features), HALF),
            pltpu.VMEM((count * span, 2 * units), HALF),
            pltpu.VMEM((count * span, units), HALF),
            pltpu.SemaphoreType.DMA(()),
        ]
        + [pltpu.SemaphoreType.DMA((2, chunks, count - 1))] * 4
        + plane_semaphores(peers),
        name="ffn_rows",
        cost_estimate=pl.CostEstimate(flops=150_000_000_000, bytes_accessed=40_000_000, transcendentals=0),
        compiler_params=pltpu.CompilerParams(
            collective_id=1, has_side_effects=True, vmem_limit_bytes=61 * 2**20
        ),
    )(branches, weight_out, hidden, gain, cot_rows, local_weight)


def entry_kernel(
    count, peers, rows, own, gains, query, keyval, mamba, state, step, kv_lanes,
    out, weight, all_gains, raw, local, held, own_sems, s0, s1, p0, p1, g0, g1,
):
    line = Line(count)
    swarm = Swarm(peers, count)
    plane = Plane(peers, local, weight, p0, p1)
    block = gains.shape[1]
    keep = pltpu.make_async_copy(own, raw.at[pl.ds(pl.multiple_of(line.me * rows, 16), rows), :], own_sems.at[0])
    keep.start()
    swarm.greet()
    keep.wait()
    gather = Gather(line, raw, rows, rows, s0, s1)
    gather.send(0, 1)
    sent = swarm.along_dp(lambda device: gains, held, g0, g1)
    for copy in sent:
        copy.start()
    start = 0
    shared = pl.ds(pl.multiple_of(kv_lanes(line.me), ATT_DIM), ATT_DIM)
    for part in (query[...], keyval[:, 0, shared], keyval[:, 1, shared], mamba[:, 0, :], mamba[:, 1, :],
                 state[:, 0, :], state[:, 1, :], step[...]):
        local[:, start : start + part.shape[1]] = part
        start += part.shape[1]
    keep_weight = pltpu.make_async_copy(
        local, weight.at[pl.ds(pl.multiple_of(plane.me * plane.rows, 16), plane.rows), :], own_sems.at[1]
    )
    keep_weight.start()
    plane.start()
    held[0] = gains[...]
    for copy in sent:
        copy.wait()
    for offset in range(peers):
        lanes = pl.ds(pl.multiple_of((swarm.at_dp ^ offset) * block, block), block)
        all_gains[:, lanes] = held[offset]

    def normed(owner):
        at = pl.ds(pl.multiple_of(owner * rows, 16), rows)
        value = raw[at, :].astype(FULL)
        inverse = lax.rsqrt(jnp.mean(value * value, -1, keepdims=True) + EPSILON)
        out[at, :] = (value * inverse * all_gains[0:1, :]).astype(HALF)

    normed(line.me)
    for hop in range(1, count):
        gather.step(0, hop)
        if hop <= plane.steps:
            plane.advance(hop)
        for side in (0, 1):

            @pl.when(line.place(side) >= hop)
            def _():
                normed(line.ahead(1 - side, hop))

    for extra in range(count, plane.steps + 1):
        plane.advance(extra)
    plane.finish()
    gather.drain(0)
    plane.drain()
    keep_weight.wait()


def entry(count, peers, own, gains, query, keyval, mamba, state, step, kv_lanes):
    rows, features = own.shape
    block = query.shape[0]
    total = query.shape[1] + 2 * ATT_DIM + 2 * mamba.shape[2] + 2 * state.shape[2] + step.shape[1]
    vmem, anywhere = pl.BlockSpec(memory_space=pltpu.VMEM), pl.BlockSpec(memory_space=pl.ANY)
    return pl.pallas_call(
        lambda *refs: entry_kernel(count, peers, rows, *refs[:7], kv_lanes, *refs[7:]),
        in_specs=[vmem] * 7,
        out_specs=[vmem, anywhere, vmem],
        out_shape=[
            jax.ShapeDtypeStruct((count * rows, features), own.dtype),
            jax.ShapeDtypeStruct((peers * block, total), HALF),
            jax.ShapeDtypeStruct((gains.shape[0], peers * block), FULL),
        ],
        scratch_shapes=[
            pltpu.VMEM((count * rows, features), HALF),
            pltpu.VMEM((block, total), HALF),
            pltpu.VMEM((peers,) + gains.shape, FULL),
            pltpu.SemaphoreType.DMA((2,)),
        ]
        + [pltpu.SemaphoreType.DMA((2, 1, count - 1))] * 2
        + plane_semaphores(peers)
        + [pltpu.SemaphoreType.DMA((peers,))] * 2,
        name="entry",
        cost_estimate=pl.CostEstimate(flops=80_000_000_000, bytes_accessed=20_000_000, transcendentals=0),
        compiler_params=pltpu.CompilerParams(
            collective_id=0, has_side_effects=True, vmem_limit_bytes=48 * 2**20
        ),
    )(own, gains, query, keyval, mamba, state, step)


class Fold:
    def __init__(self, peers, chunks, product, parts, held, store, sends, receives, early=()):
        self.me, self.early = lax.axis_index("dp"), list(early)
        self.peers, self.chunks = peers, chunks
        self.product, self.parts, self.held, self.store = product, parts, held, store
        self.sends, self.receives = sends, receives
        outer = [1 << bit for bit in range(1, peers.bit_length() - 1)]
        self.orders = [[1] + outer, [1] + outer[::-1]]
        self.stages = len(outer) + 2
        self.turns = chunks + 2 * (self.stages - 1)

    def greet(self, barrier):
        for bit in self.orders[0]:
            pl.semaphore_signal(
                barrier, inc=1, device_id={"dp": self.me ^ bit}, device_id_type=MESH
            )
        return len(self.orders[0])

    def column(self, chunk):
        return (self.early + [at for at in range(self.chunks) if at not in self.early])[chunk]

    def place(self, parity, owner):
        offset = self.me ^ owner
        return sum(
            lax.rem(offset // bit, 2) * (self.peers >> (step + 1)) for step, bit in enumerate(self.orders[parity])
        )

    def level(self, chunk, step, upper):
        size = self.peers >> (step + 1)
        at = pl.ds(size if upper else 0, size)
        if step == 0:
            return self.parts.at[chunk % 3, at]
        return self.held[step - 1].at[chunk, at]

    def copy(self, parity, chunk, step):
        return pltpu.make_async_remote_copy(
            src_ref=self.level(chunk, step, True),
            dst_ref=self.held[step].at[chunk],
            send_sem=self.sends[step].at[chunk],
            recv_sem=self.receives[step].at[chunk],
            device_id={"dp": self.me ^ self.orders[parity][step]},
            device_id_type=MESH,
        )

    def stage(self, number, parity, chunk):
        if number == 0:
            self.product(
                self.column(chunk), self.parts.at[chunk % 3], functools.partial(self.place, parity)
            )
        else:
            step = number - 1
            copy = self.copy(parity, chunk, step)
            copy.wait_recv()
            value = self.level(chunk, step, False)[...].astype(FULL) + self.held[step][chunk].astype(FULL)
            if number == self.stages - 1:
                self.store(self.column(chunk), value[0])
            else:
                self.held[step][chunk] = value.astype(HALF)
            if step == 0:
                copy.wait_send()
        if number < self.stages - 1:
            self.copy(parity, chunk, number).start()

    def run(self, first, last):
        for turn in range(first, min(last, self.turns)):
            for number in reversed(range(self.stages)):
                chunk = turn - 2 * number
                if 0 <= chunk < self.chunks:
                    self.stage(number, chunk % 2, chunk)

    def drain(self):
        for chunk in range(self.chunks):
            for step in range(1, self.stages - 1):
                self.copy(chunk % 2, chunk, step).wait_send()


def fold_scratch(peers, chunks, rows, width):
    steps = peers.bit_length() - 1
    sizes = [peers >> (step + 1) for step in range(steps)]
    return (
        [pltpu.VMEM((3, peers, rows, width), HALF)]
        + [pltpu.VMEM((chunks, size, rows, width), HALF) for size in sizes]
        + [pltpu.SemaphoreType.DMA((chunks,)) for _ in sizes] * 2
    )


def final_kernel(
    count, peers, chunks, rows, kv_owner, col, heads, width,
    left, weight_in, hidden, grad_middle, gain, ffn_gain_grad, head_rows, sequence, grad_mixed, branches,
    out, gain_out, head_out, query_out, inner_out, step_out, state_out, keyval_out, mamba_out, attn_out,
    parts, total, slots, gain_rows, held_heads, held_dp, held_tensor, gain_sum, tiles, gathered, fold_parts, *rest,
):
    steps = peers.bit_length() - 1
    held, fold_sends, fold_receives = rest[:steps], rest[steps : 2 * steps], rest[2 * steps : 3 * steps]
    s0, s1, h0, h1, d0, d1, t0, t1, tile_sems, a0, a1 = rest[3 * steps :]
    line = Line(count)
    swarm = Swarm(peers, count)
    span = rows // chunks
    block = gain_out.shape[1]
    first_chunks = left.shape[1] // width
    fold_chunks = first_chunks + branches.shape[1] // width
    swarm.greet()
    heads_sent = swarm.along_dp(lambda device: head_rows, held_heads, h0, h1)
    for copy in heads_sent:
        copy.start()
    scatter = Scatter(line, parts, rows, span, slots, s0, s1)
    gain_rows[...] = jnp.zeros_like(gain_rows)
    gain_rows[1:2, :] = ffn_gain_grad[...]

    def rows_done(chunk):
        at = pl.ds(chunk * span, span)
        scatter.finish(chunk, total)
        value = hidden[at, :].astype(FULL)
        below, part = norm_below(value, total[...], gain[...])
        gain_rows[0:1, :] += part
        out[at, :] = grad_middle[at, :] + below

    upper = line.me < line.count // 2
    pieces = parts.shape[1] // TILE

    def fetch(index):
        slot = index % 2
        return pltpu.make_async_copy(
            weight_in.at[index * TILE : (index + 1) * TILE, :], tiles.at[slot], tile_sems.at[slot]
        )

    def project_tile(start, size, index, following):
        at = pl.ds(pl.multiple_of(start, 16), size)
        if following is not None:
            fetch(following).start()
        fetch(index).wait()
        parts[at, index * TILE : (index + 1) * TILE] = mm_nt(left[at, :], tiles[index % 2]).astype(parts.dtype)

    def product(column, target, place):
        def fill(grad_left, grad_right, index):
            lanes = slice(index * width, (index + 1) * width)
            result = mm_tn(grad_left[...], grad_right[:, lanes]).astype(HALF)
            size = target.shape[1]
            for owner in range(target.shape[0]):
                target[place(owner)] = result[owner * size : (owner + 1) * size, :]

        if column < first_chunks:
            fill(sequence, left, column)
        else:
            fill(grad_mixed, branches, column - first_chunks)

    shared = (col.key, col.value, col.inmap, col.outmap)
    own_rows = pl.ds(pl.multiple_of(line.me * block, block), block)

    def store(at, value):
        for piece in range(0, width, LANES):
            begin = at * width + piece
            part = value[:, piece : piece + LANES]
            place = 0
            for start, end in shared:
                if start <= begin < end:
                    gathered[own_rows, place + begin - start : place + begin - start + LANES] = part.astype(HALF)
                place += end - start
            if begin < col.query[1]:
                query_out[:, begin : begin + LANES] = part
            for index, (start, end) in enumerate((col.gate, col.drive)):
                if start <= begin < end:
                    inner_out[:, index, begin - start : begin - start + LANES] = part
            if begin == col.step[0]:
                step_out[...] = part[:, :heads]
            if begin >= col.total:
                turned_part = part.T
                begin -= col.total
                if begin < mamba_out.shape[0]:
                    mamba_out[begin : begin + LANES, :] = turned_part
                else:
                    begin -= mamba_out.shape[0]
                    attn_out[begin : begin + LANES, :] = turned_part

    early = sorted({at for begin, end in shared for at in range(begin // width, (end - 1) // width + 1)})
    fold = Fold(peers, fold_chunks, product, fold_parts, held, store, fold_sends, fold_receives, early)
    gather = Gather(line, gathered, block, block, a0, a1)
    gains = []

    def send_gains():
        gains.extend(
            swarm.along_dp(
                lambda device: gain_rows.at[:, pl.ds(pl.multiple_of(device * block, block), block)], held_dp, d0, d1
            )
        )
        for copy in gains:
            copy.start()

    far, others = jnp.where(upper, count - 1, 0) * rows, jnp.where(upper, 0, 1) * rows
    fetch(0).start()
    for index in range(pieces):
        project_tile(far, rows, index, (index + 1) % pieces)
    for chunk in range(chunks):
        scatter.hop(chunk, 1)

    def project_others(first, last):
        for index in range(first, last):
            project_tile(others, (count - 1) * rows, index, index + 1 if index + 1 < pieces else None)

    early_done = len(early) + 2 * (fold.stages - 1)
    half = pieces // 2
    line_steps = [functools.partial(project_others, 0, half), functools.partial(project_others, half, pieces)]
    line_steps += [functools.partial(scatter.hop, chunk, hop) for hop in range(2, count) for chunk in range(chunks)]
    line_steps += [functools.partial(rows_done, chunk) for chunk in range(chunks)] + [send_gains]
    early_steps = [lambda: gather.send(0, 1)] + [functools.partial(gather.step, 0, hop) for hop in range(1, count)]
    for done in range(1, fold.turns + 1):
        fold.run(done - 1, done)
        if line_steps and done % 2 == 0:
            line_steps.pop(0)()
        if done >= early_done and early_steps and (done - early_done) % 4 == 0:
            early_steps.pop(0)()
    for step in line_steps + early_steps:
        step()
    head_out[...] = head_rows[...]
    for offset, copy in enumerate(heads_sent):
        copy.wait()
        head_out[...] += held_heads[offset + 1]
    gain_sum[...] = gain_rows[:, pl.ds(pl.multiple_of(swarm.at_dp * block, block), block)]
    for offset, copy in enumerate(gains):
        copy.wait()
        gain_sum[...] += held_dp[offset + 1]
    last_sent = swarm.along_tensor(gain_sum, held_tensor, t0, t1)
    for copy in last_sent:
        copy.start()
    pair = 2 * ATT_DIM
    state = (gathered.shape[1] - pair) // 2
    for part in range(2):
        lanes = slice(pair + part * state, pair + (part + 1) * state)
        whole = gathered[0:block, lanes].astype(FULL)
        for owner in range(1, count):
            whole = whole + gathered[owner * block : (owner + 1) * block, lanes].astype(FULL)
        state_out[:, part, :] = whole
    for head in range(KV_HEADS):
        for part in range(2):
            lanes = slice(part * ATT_DIM, (part + 1) * ATT_DIM)
            value = jnp.zeros((block, ATT_DIM), FULL)
            for owner in range(count):
                if kv_owner(owner) == head:
                    value = value + gathered[owner * block : (owner + 1) * block, lanes].astype(FULL)
            keyval_out[:, part, head * ATT_DIM : (head + 1) * ATT_DIM] = value
    gain_out[...] = gain_sum[...]
    for distance, copy in enumerate(last_sent):
        copy.wait()
        gain_out[...] += held_tensor[distance + 1]
    for chunk in range(chunks):
        scatter.drain(chunk)
    gather.drain(0)
    fold.drain()


def final_rows(
    count, peers, chunks, kv_owner, col, heads, width, grads, weight_in, hidden, grad_middle, gain, ffn_gain_grad,
    head_rows, sequence, grad_mixed, branches,
):
    rows, features = hidden.shape
    span = rows // chunks
    block = features // peers
    one, two = grads.shape[1], branches.shape[1]
    tile = 256 if one % 256 == 0 and two % 256 == 0 else 128
    fold_chunks = (one + two) // tile
    vmem = pl.BlockSpec(memory_space=pltpu.VMEM)
    state = col.inmap[1] - col.inmap[0]
    operands = (
        grads, weight_in, hidden, grad_middle, gain, ffn_gain_grad, head_rows, sequence, grad_mixed, branches
    )
    outputs = [
        (rows, features),
        (8, block),
        head_rows.shape,
        (block, col.query[1]),
        (block, 2, width),
        (block, heads),
        (block, 2, state),
        (block, 2, KV_HEADS * ATT_DIM),
        (width, block),
        (two - width, block),
    ]
    return pl.pallas_call(
        functools.partial(final_kernel, count, peers, chunks, rows, kv_owner, col, heads, tile),
        in_specs=[vmem, pl.BlockSpec(memory_space=pl.ANY)] + [vmem] * (len(operands) - 2),
        out_specs=[vmem] * len(outputs),
        out_shape=[jax.ShapeDtypeStruct(shape, FULL) for shape in outputs],
        scratch_shapes=[
            pltpu.VMEM((count * rows, features), HALF),
            pltpu.VMEM((span, features), FULL),
            pltpu.VMEM((2, chunks, count - 1, span, features), HALF),
            pltpu.VMEM((8, features), FULL),
            pltpu.VMEM((peers,) + head_rows.shape, FULL),
            pltpu.VMEM((peers, 8, block), FULL),
            pltpu.VMEM((count, 8, block), FULL),
            pltpu.VMEM((8, block), FULL),
            pltpu.VMEM((2, TILE, one), HALF),
            pltpu.VMEM((count * block, 2 * (ATT_DIM + state)), HALF),
        ]
        + fold_scratch(peers, fold_chunks, block, tile)
        + [pltpu.SemaphoreType.DMA((2, chunks, count - 1))] * 2
        + [pltpu.SemaphoreType.DMA((peers,))] * 4
        + [pltpu.SemaphoreType.DMA((count,))] * 2
        + [pltpu.SemaphoreType.DMA((2,))]
        + [pltpu.SemaphoreType.DMA((2, 1, count - 1))] * 2,
        name="final_rows",
        cost_estimate=pl.CostEstimate(flops=80_000_000_000, bytes_accessed=20_000_000, transcendentals=0),
        compiler_params=pltpu.CompilerParams(
            collective_id=3, has_side_effects=True, vmem_limit_bytes=62 * 2**20
        ),
    )(*operands)


def ffn_grad_kernel(
    count, peers, chunks, lag, rows, width,
    parts, middle, cotangent, gain, ffn_rows, grad_gate, cot_rows, activated,
    out, grad_middle, gain_grad, up_out, down_out,
    total, slots, fold_parts, *rest,
):
    steps = peers.bit_length() - 1
    held, fold_sends, fold_receives = rest[:steps], rest[steps : 2 * steps], rest[2 * steps : 3 * steps]
    s0, s1, s2, s3 = rest[3 * steps :]
    line = Line(count)
    span = rows // chunks
    units = activated.shape[1]
    first_chunks = 2 * units // width

    def product(column, target, place):
        def fill(grad_left, grad_right, index):
            lanes = slice(index * width, (index + 1) * width)
            result = mm_tn(grad_left[...], grad_right[:, lanes]).astype(HALF)
            size = target.shape[1]
            for owner in range(target.shape[0]):
                target[place(owner)] = result[owner * size : (owner + 1) * size, :]

        if column < first_chunks:
            fill(ffn_rows, grad_gate, column)
        else:
            fill(cot_rows, activated, column - first_chunks)

    def store(at, value):
        begin = at * width
        if begin < 2 * units:
            up_out[:, begin // units, begin % units : begin % units + width] = value
        else:
            down_out[begin - 2 * units : begin - 2 * units + width, :] = value.T

    fold = Fold(peers, 3 * units // width, product, fold_parts, held, store, fold_sends, fold_receives)
    line.greet(fold)
    scatter = Scatter(line, parts, rows, span, slots, s0, s1)
    gather = Gather(line, out, rows, span, s2, s3)
    gain_grad[...] = jnp.zeros_like(gain_grad)

    def rows_done(chunk):
        at = pl.ds(chunk * span, span)
        scatter.finish(chunk, total)
        below, part = norm_below(middle[at, :], total[...], gain[...])
        gain_grad[...] += part
        result = cotangent[at, :].astype(FULL) + below
        grad_middle[at, :] = result
        gather.at(line.me, chunk)[...] = result.astype(HALF)

    turns = lag * (chunks - 1) + 2 * (count - 1) + 1
    ends = [min(fold.turns, -(-fold.turns * (turn + 1) // (turns - 2))) for turn in range(turns)]
    events = {
        turn: functools.partial(fold.run, ends[turn - 1] if turn else 0, ends[turn]) for turn in range(turns)
    }
    relay(line, scatter, gather, chunks, lag, rows_done, events=events)
    fold.drain()


def ffn_grad_rows(count, peers, chunks, lag, parts, middle, cotangent, gain, ffn_rows, grad_gate, cot_rows, activated):
    rows, features = middle.shape
    span = rows // chunks
    block = features // peers
    units = activated.shape[1]
    width = 256
    vmem = pl.BlockSpec(memory_space=pltpu.VMEM)
    operands = (parts, middle, cotangent, gain, ffn_rows, grad_gate, cot_rows, activated)
    return pl.pallas_call(
        functools.partial(ffn_grad_kernel, count, peers, chunks, lag, rows, width),
        in_specs=[vmem] * len(operands),
        out_specs=[vmem] * 5,
        out_shape=[
            jax.ShapeDtypeStruct((count * rows, features), HALF),
            jax.ShapeDtypeStruct((rows, features), FULL),
            jax.ShapeDtypeStruct((1, features), FULL),
            jax.ShapeDtypeStruct((block, 2, units), FULL),
            jax.ShapeDtypeStruct((units, block), FULL),
        ],
        scratch_shapes=[
            pltpu.VMEM((span, features), FULL),
            pltpu.VMEM((2, chunks, count - 1, span, features), HALF),
        ]
        + fold_scratch(peers, 3 * units // width, block, width)
        + [pltpu.SemaphoreType.DMA((2, chunks, count - 1))] * 4,
        name="ffn_grad_rows",
        cost_estimate=pl.CostEstimate(flops=100_000_000_000, bytes_accessed=20_000_000, transcendentals=0),
        compiler_params=pltpu.CompilerParams(
            collective_id=2, has_side_effects=True, vmem_limit_bytes=62 * 2**20
        ),
    )(*operands)


CHUNKS = 4
LAG = 2


def sum_rows(pieces):
    return lax.psum_scatter(pieces, "tensor", scatter_dimension=0, tiled=True).astype(FULL)


def dot_nt(a, b):
    return jnp.einsum("sb,ab->sa", a, b, preferred_element_type=FULL)


def body(
    hidden_in,
    segments,
    norm_gain,
    mamba_in,
    step_weight,
    state_weight,
    decay_log,
    step_bias,
    skip_gain,
    gated_gain,
    query_weight,
    keyval_weight,
    mamba_out,
    attn_out,
    ffn_gain,
    gate_up,
    down_weight,
    cotangent,
):
    tensor_index = lax.axis_index("tensor")
    count, peers = lax.axis_size("tensor"), lax.axis_size("dp")
    heads = decay_log.shape[0]
    width = mamba_in.shape[2]
    state_size = state_weight.shape[2]
    query_width = query_weight.shape[1]
    qheads = query_width // ATT_DIM
    units = gate_up.shape[2]
    rows_local = hidden_in.shape[0]
    block = norm_gain.shape[0]
    group_size = ATT_HEADS // KV_HEADS
    kv_head = tensor_index * qheads // group_size
    col = Columns(query_width, width, state_size)

    gains = jnp.pad(jnp.stack([norm_gain, ffn_gain]).astype(FULL), ((0, 6), (0, 0)))
    step_padded = jnp.pad(step_weight, ((0, 0), (0, 2 * LANES - heads)))
    sequence, weight_in, gains = entry(
        count,
        peers,
        hidden_in,
        gains,
        query_weight,
        keyval_weight,
        mamba_in,
        state_weight,
        step_padded,
        lambda place: (place * qheads // group_size) * ATT_DIM,
    )
    gain_one, gain_two = gains[0:1], gains[1:2]
    weight_out = lax.all_gather(jnp.concatenate([mamba_out, attn_out], 0), "dp", axis=1, tiled=True)
    sequence, cotangent_late, weight_out, gate_late, down_late, positions = lax.optimization_barrier(
        (sequence, cotangent, weight_out, gate_up, down_weight, jnp.arange(sequence.shape[0], dtype=FULL))
    )
    cot_rows = lax.all_gather(cotangent_late, "tensor", axis=0, tiled=True)
    local_ffn = jnp.concatenate([gate_late.reshape(block, 2 * units), down_late.T], 1)
    length = sequence.shape[0]
    packed = jnp.dot(sequence, weight_in, preferred_element_type=FULL)
    head_params = jnp.pad(
        jnp.stack([decay_log, step_bias, skip_gain]), ((0, 5), (0, LANES - heads))
    )
    tables = rope_tables(positions)

    scan_y, states, gated_vals, squares = scan_forward(
        col, heads, state_size, packed, segments, head_params
    )
    attended, lse, squares = attend_forward(col, qheads, count, packed, tables, segments, squares)
    gated_inverse = lax.rsqrt(squares / (MAMBA_HEADS * HEAD_DIM) + EPSILON).reshape(length, 1)
    gated_scale = gated_gain.astype(FULL)
    gated_plain = gated_vals * gated_inverse
    branches = jnp.concatenate([(gated_plain * gated_scale).astype(HALF), attended], 1)
    ffn_rows, activated, grad_gate, ffn_parts, out_parts, middle = ffn_rows_call(
        count, peers, CHUNKS, LAG, branches, weight_out, hidden_in, gain_two, cot_rows, local_ffn
    )
    grad_mixed, grad_middle, ffn_gain_part, gate_up_grad, down_weight_grad = ffn_grad_rows(
        count, peers, CHUNKS, LAG, ffn_parts, middle, cotangent, gain_two, ffn_rows, grad_gate, cot_rows, activated
    )
    grad_mixed, out_parts = lax.optimization_barrier((grad_mixed, out_parts))
    ffn_out = sum_rows(out_parts)
    grad_branches = dot_nt(grad_mixed, weight_out)
    product_sum = jnp.sum(grad_branches[:, :width] * gated_scale * gated_plain, -1).reshape(-1, LANES)
    attention_grads, product_sum = attend_backward(
        col, qheads, count, packed, attended, lse, grad_branches, tables, segments, product_sum
    )
    grads, gain_part, skip_part, head_part = scan_backward(
        col,
        heads,
        state_size,
        packed,
        scan_y,
        states,
        grad_branches,
        squares,
        product_sum,
        gated_scale[None, :],
        segments,
        head_params,
        attention_grads,
    )
    head_sums = jnp.concatenate(
        [
            gain_part[0],
            head_part[0, :heads],
            head_part[1, :heads],
            skip_part.reshape(heads, HEAD_DIM).sum(1),
        ]
    )
    head_rows = jnp.pad(head_sums, (0, 8 * LANES - head_sums.shape[0])).reshape(8, LANES)
    (
        hidden_grad,
        gain_grads,
        head_rows,
        query_grad,
        inner_grad,
        step_grad,
        state_grad,
        keyval_grad,
        mamba_out_grad,
        attn_out_grad,
    ) = final_rows(
        count,
        peers,
        2,
        lambda place: place * qheads // group_size,
        col,
        heads,
        width,
        grads,
        weight_in,
        hidden_in,
        grad_middle,
        gain_one,
        ffn_gain_part,
        head_rows,
        sequence,
        grad_mixed,
        branches,
    )
    head_sums = head_rows.reshape(-1)
    hidden_out = (middle + ffn_out).astype(HALF)
    return (
        hidden_out,
        hidden_grad,
        gain_grads[0],
        inner_grad,
        step_grad,
        state_grad,
        head_sums[width : width + heads],
        head_sums[width + heads : width + 2 * heads],
        head_sums[width + 2 * heads : width + 3 * heads],
        head_sums[:width],
        query_grad,
        keyval_grad,
        mamba_out_grad,
        attn_out_grad,
        gain_grads[1],
        gate_up_grad,
        down_weight_grad,
    )


def solution(mesh):
    rows = P(("dp", "tensor"), None)
    weights_in = P("dp", None, "tensor")
    return jax.shard_map(
        body,
        mesh=mesh,
        in_specs=(
            rows,
            P("dp"),
            P("dp"),
            weights_in,
            P("dp", "tensor"),
            P("dp", None, None),
            P("tensor"),
            P("tensor"),
            P("tensor"),
            P("tensor"),
            P("dp", "tensor"),
            P("dp", None, None),
            P("tensor", "dp"),
            P("tensor", "dp"),
            P("dp"),
            weights_in,
            P("tensor", "dp"),
            rows,
        ),
        out_specs=(
            rows,
            rows,
            P("dp"),
            weights_in,
            P("dp", "tensor"),
            P("dp", None, None),
            P("tensor"),
            P("tensor"),
            P("tensor"),
            P("tensor"),
            P("dp", "tensor"),
            P("dp", None, None),
            P("tensor", "dp"),
            P("tensor", "dp"),
            P("dp"),
            weights_in,
            P("tensor", "dp"),
        ),
        check_vma=False,
    )
```
